32 devices in a mesh: batch: 4 (over x, core), blk: 8 (over z, y).
Axes of the slice: x: 2, y: 2, z: 4, core: 2. Of those that a mesh axis runs over, the one named last changes fastest.
Arguments:
- tokens_in: bfloat16 [4, 1024, 1024], P('batch', 'blk'), may hold values from -6 to 6
- clip_lengths: int32 [4, 8], P('batch'), may hold values from 1 to 1017, as said below
- attn_gain: bfloat16 [1024], replicated, may hold values from 0.099609375 to 1.8984375
- attn_shift: bfloat16 [1024], replicated, may hold values from -3 to 3
- qkv_weight: bfloat16 [1024, 3072], replicated, may hold values from -0.25 to 0.25
- qkv_bias: bfloat16 [3072], replicated, may hold values from -3 to 3
- proj_weight: bfloat16 [1024, 1024], replicated, may hold values from -1.5 to 1.5
- proj_bias: bfloat16 [1024], replicated, may hold values from -3 to 3
- mlp_gain: bfloat16 [1024], replicated, may hold values from 0.099609375 to 1.8984375
- mlp_shift: bfloat16 [1024], replicated, may hold values from -3 to 3
- up_weight: bfloat16 [1024, 4096], replicated, may hold values from -0.1875 to 0.1875
- up_bias: bfloat16 [4096], replicated, may hold values from -3 to 3
- down_weight: bfloat16 [4096, 1024], replicated, may hold values from -0.09375 to 0.09375
- down_bias: bfloat16 [1024], replicated, may hold values from -3 to 3
- out_cotangent: bfloat16 [4, 1024, 1024], P('batch', 'blk'), may hold values from -6 to 6
Outputs:
- layer_out: bfloat16 [4, 1024, 1024], P('batch', 'blk')
- tokens_grad: float32 [4, 1024, 1024], P('batch', 'blk')
- attn_gain_grad: float32 [1024], P(('batch', 'blk'))
- attn_shift_grad: float32 [1024], P(('batch', 'blk'))
- qkv_weight_grad: float32 [1024, 3072], P(('batch', 'blk'))
- qkv_bias_grad: float32 [3072], P(('batch', 'blk'))
- proj_weight_grad: float32 [1024, 1024], P(('batch', 'blk'))
- proj_bias_grad: float32 [1024], P(('batch', 'blk'))
- mlp_gain_grad: float32 [1024], P(('batch', 'blk'))
- mlp_shift_grad: float32 [1024], P(('batch', 'blk'))
- up_weight_grad: float32 [1024, 4096], P(('batch', 'blk'))
- up_bias_grad: float32 [4096], P(('batch', 'blk'))
- down_weight_grad: float32 [4096, 1024], P(('batch', 'blk'))
- down_bias_grad: float32 [1024], P(('batch', 'blk'))
The draws below stay inside these ranges and needn't reach their ends.
Inputs may be any that keep to these rules, and one draw needn't show every extreme that they name: `clip_lengths`: the 8 lengths of each row sum to 1024; in every row one clip starts among the first 128 tokens and ends among the last 128, and the other clips together hold fewer than 128 tokens.
All inputs are finite; a program needn't handle non-finite values.
Results may differ from the reference program's by a relative error of at most 0.025.
Values may be sent and summed in bfloat16 or wider, within the bound.
No kernel may reach another device: no remote copies, remote signals or barrier semaphores. Data moves between devices by JAX's collectives and lax.ppermute only.
A program may use at most 320 MiB of HBM per device.

```python
import math
import jax
import jax.numpy as jnp
from jax import lax

D = 1024
H = 16
HD = 64
FF = 4096
TOK_DEV = 128
CLIPS = 8
SEQ = 1024
BATCH = 4


def draw_clip_lengths(key, part):
    key = jax.random.fold_in(key, 7)
    key_short, key_long = jax.random.split(key)
    short_len = jax.random.randint(key_short, (BATCH, CLIPS), 1, TOK_DEV // CLIPS + 1)
    long_slot = jax.random.randint(key_long, (BATCH, 1), 0, CLIPS)
    column = jnp.arange(CLIPS)[None, :]
    short_len = jnp.where(column == long_slot, 0, short_len)
    long_len = SEQ - jnp.sum(short_len, axis=1, keepdims=True)
    return jnp.where(column == long_slot, long_len, short_len).astype(jnp.int32)


def with_spikes(values, key, source, target, shards_of, factor):
    def block_of(dim):
        return (jnp.arange(values.shape[dim]) // (values.shape[dim] // shards_of)).reshape((-1,) + (1,) * (values.ndim - 1 - dim))

    near = jax.random.permutation(key, shards_of)[block_of(target)]
    far = (block_of(target) + shards_of // 2) % shards_of
    return jnp.where((block_of(source) == near) | (block_of(source) == far), factor * values, values)


def shard_levels(key, dims, shards, least, largest):
    level = 1.0
    for dim, parts in shards:
        draws = jax.random.uniform(jax.random.fold_in(jax.random.fold_in(key, 6), dim), (parts,), jnp.float32, least / len(shards), largest / len(shards))
        level = level * jnp.repeat(jnp.exp(draws), dims[dim] // parts).reshape((-1,) + (1,) * (len(dims) - 1 - dim))
    return level


def bell_draw(rng, dims, deviation, reach, cuts=(), kind=jnp.bfloat16):
    drawn = deviation * jax.random.normal(rng, dims, jnp.float32)
    if cuts:
        drawn = drawn * shard_levels(rng, dims, cuts, -0.22, 0.18)
    return jnp.clip(drawn, -reach, reach).astype(kind)


def bell_draw_with(own_key, shape, spread, limit, cuts, heavy, held_as=jnp.bfloat16):
    values = spread * jax.random.normal(own_key, shape, jnp.float32)
    if cuts:
        values = values * shard_levels(own_key, shape, cuts, -0.22, 0.18)
    return jnp.clip(with_spikes(values, jax.random.fold_in(own_key, 3), *heavy), -limit, limit).astype(held_as)


def setup_inputs(seed: int = 0) -> dict:
    key_list = jax.random.split(jax.random.key(seed), 16)
    return {
        "tokens_in": bell_draw(key_list[0], (BATCH, SEQ, D), 1.0, 6.0, ((0, 4), (1, 8))),
        "clip_lengths": draw_clip_lengths(jax.random.fold_in(key_list[15], 71), 0),
        "attn_gain": jnp.clip(1.0 + 0.18 * jax.random.normal(key_list[2], (D,), jnp.float32), 0.099609375, 1.8984375).astype(jnp.bfloat16),
        "attn_shift": bell_draw(key_list[3], (D,), 0.5, 3.0),
        "qkv_weight": bell_draw(key_list[4], (D, 3 * D), (D // 2) ** -0.5, 0.25),
        "qkv_bias": bell_draw(key_list[5], (3 * D,), 0.5, 3.0),
        "proj_weight": bell_draw(key_list[6], (D, D), (HD // 4) ** -0.5, 1.5),
        "proj_bias": bell_draw(key_list[7], (D,), 0.5, 3.0),
        "mlp_gain": jnp.clip(1.0 + 0.18 * jax.random.normal(key_list[8], (D,), jnp.float32), 0.099609375, 1.8984375).astype(jnp.bfloat16),
        "mlp_shift": bell_draw(key_list[9], (D,), 0.5, 3.0),
        "up_weight": bell_draw(key_list[10], (D, FF), D ** -0.5, 0.1875),
        "up_bias": bell_draw(key_list[11], (FF,), 0.5, 3.0),
        "down_weight": bell_draw(key_list[12], (FF, D), FF ** -0.5, 0.09375),
        "down_bias": bell_draw(key_list[13], (D,), 0.5, 3.0),
        "out_cotangent": bell_draw_with(key_list[14], (BATCH, SEQ, D), 1.0, 6.0, ((0, 4), (1, 8)), (1, 2, 8, 2.0)),
    }


@jax.custom_vjp
def low(v):
    return lax.optimization_barrier(v.astype(jnp.bfloat16)).astype(jnp.float32)

@jax.custom_vjp
def low_back(v):
    return v

def low_keep(v):
    return (low(v), None)

def low_pass(kept, grad):
    return (grad,)

def back_keep(v):
    return (v, None)

def back_low(kept, grad):
    return (low(grad),)
low.defvjp(low_keep, low_pass)
low_back.defvjp(back_keep, back_low)

def pair_table():
    part_map = [0] * 10 + [1] * 11 + [2] * 11
    freq_list = [10000.0 ** (-rank / 10.0) for rank in range(10)] + [10000.0 ** (-rank / 11.0) for rank in range(11)] * 2
    table_rows = [[freq_list[column] if part_map[column] == axis_id else 0.0 for column in range(32)] for axis_id in range(3)]
    return jnp.array(table_rows, dtype=jnp.float32)

def clip_layout(lengths_row, positions):
    clip_end = jnp.cumsum(lengths_row).astype(jnp.int32)
    starts = clip_end - lengths_row
    clip_ids = lax.optimization_barrier(jnp.sum((positions[:, None] >= clip_end[None, :]).astype(jnp.int32), axis=1))
    member = clip_ids[:, None] == jnp.arange(lengths_row.shape[0], dtype=jnp.int32)[None, :]
    within = positions - lax.optimization_barrier(jnp.sum(jnp.where(member, starts[None, :], 0), axis=1))
    coords = jnp.stack([within // 196, within // 14 % 14, within % 14], axis=1).astype(jnp.float32)
    angles = jnp.dot(coords, pair_table().astype(coords.dtype), precision=lax.Precision.HIGHEST)
    return (clip_ids, jnp.cos(angles), jnp.sin(angles))

def rotate(values, cos_tab, sin_tab):
    half_dim = values.shape[-1] // 2
    first_half = values[..., :half_dim]
    second_half = values[..., half_dim:]
    cos_b = cos_tab[:, None, :]
    sin_b = sin_tab[:, None, :]
    return jnp.concatenate([first_half * cos_b - second_half * sin_b, first_half * sin_b + second_half * cos_b], axis=-1)

def layer_norm(values, gain_vec, shift_vec):
    row_mean = lax.optimization_barrier(jnp.mean(values, -1, keepdims=True))
    centered = values - row_mean
    row_var = lax.optimization_barrier(jnp.mean(centered * centered, -1, keepdims=True))
    return centered * lax.rsqrt(row_var + 1e-06) * gain_vec + shift_vec

def attend_row(queries, keys, values, clip_ids):
    seq_len = queries.shape[0]
    block_rows = math.gcd(seq_len, 512)
    block_count = seq_len // block_rows
    query_blocks = queries.reshape(block_count, block_rows, H, HD)
    clip_blocks = clip_ids.reshape(block_count, block_rows)

    def one_block(pair_in):
        query_part, clip_part = pair_in
        raw_scores = jnp.einsum('qhd,khd->hqk', query_part, keys, precision=lax.Precision.HIGHEST)
        scores = low_back(0.125 * raw_scores)
        allowed = (clip_part[:, None] == clip_ids[None, :])[None]
        scores = jnp.where(allowed, scores, -1e+30)
        row_max = lax.optimization_barrier(jnp.max(scores, -1, keepdims=True))
        weights = jnp.where(allowed, jnp.exp(scores - row_max), 0.0)
        probs = weights / lax.optimization_barrier(jnp.sum(weights, -1, keepdims=True))
        return jnp.einsum('hqk,khd->qhd', low(probs), values, precision=lax.Precision.HIGHEST)
    outputs = lax.map(jax.checkpoint(one_block), (query_blocks, clip_blocks))
    return outputs.reshape(seq_len, H * HD)

def layer_row(tokens, lengths_row, params):
    gain_one, shift_one, w_qkv, b_qkv, w_proj, b_proj, gain_two, shift_two, w_up, b_up, w_down, b_down = params
    seq_len = tokens.shape[0]
    width = tokens.shape[1]
    clip_ids, cos_tab, sin_tab = clip_layout(lengths_row, jnp.arange(seq_len, dtype=jnp.int32))
    normed = low(layer_norm(tokens, gain_one, shift_one))
    qkv_mixed = low_back(jnp.dot(normed, w_qkv, precision=lax.Precision.HIGHEST) + b_qkv)
    queries = low(rotate(qkv_mixed[:, :width].reshape(seq_len, H, HD), cos_tab, sin_tab))
    keys = low(rotate(qkv_mixed[:, width:2 * width].reshape(seq_len, H, HD), cos_tab, sin_tab))
    values = low(qkv_mixed[:, 2 * width:].reshape(seq_len, H, HD))
    attended = low(low_back(attend_row(queries, keys, values, clip_ids)))
    branch = low_back(jnp.dot(attended, w_proj, precision=lax.Precision.HIGHEST) + b_proj)
    middle = tokens + branch
    normed_two = low(layer_norm(middle, gain_two, shift_two))
    hidden = low_back(jnp.dot(normed_two, w_up, precision=lax.Precision.HIGHEST) + b_up)
    active = low(jax.nn.gelu(hidden))
    return middle + jnp.dot(active, w_down, precision=lax.Precision.HIGHEST) + b_down

def reference(tokens_in, clip_lengths, attn_gain, attn_shift, qkv_weight, qkv_bias, proj_weight, proj_bias, mlp_gain, mlp_shift, up_weight, up_bias, down_weight, down_bias, out_cotangent):
    params = (attn_gain.astype(jnp.float32), attn_shift.astype(jnp.float32), qkv_weight.astype(jnp.float32), qkv_bias.astype(jnp.float32), proj_weight.astype(jnp.float32), proj_bias.astype(jnp.float32), mlp_gain.astype(jnp.float32), mlp_shift.astype(jnp.float32), up_weight.astype(jnp.float32), up_bias.astype(jnp.float32), down_weight.astype(jnp.float32), down_bias.astype(jnp.float32))

    def forward(tokens, weights):
        return lax.map(lambda item: layer_row(item[0], item[1], weights), (tokens, clip_lengths))
    result, pull = jax.vjp(forward, tokens_in.astype(jnp.float32), params)
    tokens_grad, grads = pull(out_cotangent.astype(jnp.float32))
    return (result.astype(jnp.bfloat16), tokens_grad, grads[0], grads[1], grads[2], grads[3], grads[4], grads[5], grads[6], grads[7], grads[8], grads[9], grads[10], grads[11])
```

```python
import math

import jax
import jax.numpy as jnp
from jax import lax
from jax.experimental import pallas as pl
from jax.experimental.pallas import tpu as pltpu
from jax.sharding import Mesh
from jax.sharding import PartitionSpec as P

H = 16
HD = 64


NEG_FILL = -1e30


def pair_table():
    part_map = [0] * 10 + [1] * 11 + [2] * 11
    freq_list = [10000.0 ** (-rank / 10.0) for rank in range(10)] + [
        10000.0 ** (-rank / 11.0) for rank in range(11)
    ] * 2
    table_rows = [
        [freq_list[column] if part_map[column] == axis_id else 0.0 for column in range(32)]
        for axis_id in range(3)
    ]
    return jnp.array(table_rows, dtype=jnp.float32)


def clip_of(lengths_row, positions):
    clip_end = jnp.cumsum(lengths_row)
    return jnp.sum((positions[:, None] >= clip_end[None, :]).astype(jnp.int32), axis=1)


def clip_layout(lengths_row, positions):
    clip_end = jnp.cumsum(lengths_row)
    starts = clip_end - lengths_row
    clip_ids = jnp.sum((positions[:, None] >= clip_end[None, :]).astype(jnp.int32), axis=1)
    member = clip_ids[:, None] == jnp.arange(lengths_row.shape[0], dtype=jnp.int32)[None, :]
    within = positions - jnp.sum(jnp.where(member, starts[None, :], 0), axis=1)
    coords = jnp.stack([within // 196, within // 14 % 14, within % 14], axis=1).astype(jnp.float32)
    angles = jnp.dot(coords, pair_table(), precision=lax.Precision.HIGHEST)
    return (clip_ids, jnp.cos(angles), jnp.sin(angles))


def rotate(values, cos_tab, sin_tab):
    half_dim = values.shape[-1] // 2
    first_half = values[..., :half_dim]
    second_half = values[..., half_dim:]
    cos_b = cos_tab[:, None, :]
    sin_b = sin_tab[:, None, :]
    return jnp.concatenate(
        [first_half * cos_b - second_half * sin_b, first_half * sin_b + second_half * cos_b],
        axis=-1,
    )


def norm_fwd(values, gain_vec, shift_vec):
    row_mean = jnp.mean(values, -1, keepdims=True)
    centered = values - row_mean
    inv_std = lax.rsqrt(jnp.mean(centered * centered, -1, keepdims=True) + 1e-06)
    normalized = centered * inv_std
    return (normalized * gain_vec + shift_vec, normalized, inv_std)


def norm_back(upstream, normalized, inv_std, gain_vec):
    scaled = upstream * gain_vec
    inner = (
        scaled
        - jnp.mean(scaled, -1, keepdims=True)
        - normalized * jnp.mean(scaled * normalized, -1, keepdims=True)
    )
    return (inv_std * inner, jnp.sum(upstream * normalized, 0), jnp.sum(upstream, 0))


def outer_sum(left, right):
    return lax.dot_general(
        left, right, (((0,), (0,)), ((), ())), preferred_element_type=jnp.float32
    )


def times_transposed(left, right):
    return lax.dot_general(
        left, right, (((1,), (1,)), ((), ())), preferred_element_type=jnp.float32
    )


def add_rows(buffer, block, first_key):
    current = lax.dynamic_slice_in_dim(buffer, first_key, block.shape[0], 0)
    return lax.dynamic_update_slice_in_dim(buffer, current + block, first_key, 0)


def in_blocks(block_step, running, pieces):
    row_count = pieces[0].shape[0]
    block_rows = math.gcd(row_count, 2048)

    def advance(block_idx, state):
        first_row = block_idx * block_rows
        sliced = tuple(
            (lax.dynamic_slice_in_dim(piece, first_row, block_rows, 0) for piece in pieces)
        )
        return block_step(state, sliced, first_row)

    return lax.fori_loop(0, row_count // block_rows, advance, running)


def shards(
    tokens_in,
    clip_lengths,
    attn_gain,
    attn_shift,
    qkv_weight,
    qkv_bias,
    proj_weight,
    proj_bias,
    mlp_gain,
    mlp_shift,
    up_weight,
    up_bias,
    down_weight,
    down_bias,
    out_cotangent,
):
    tok_rows = tokens_in.shape[1]
    model_width = tokens_in.shape[2]
    seq_len = tok_rows * lax.axis_size("blk")
    lens_row = clip_lengths[0]
    own_pos = lax.axis_index("blk") * tok_rows + jnp.arange(tok_rows, dtype=jnp.int32)
    clip_q, cos_tab, sin_tab = clip_layout(lens_row, own_pos)
    residual = tokens_in[0].astype(jnp.float32)
    attn_gain_f = attn_gain.astype(jnp.float32)
    mlp_gain_f = mlp_gain.astype(jnp.float32)
    normed, hat_one, inv_one = norm_fwd(residual, attn_gain_f, attn_shift.astype(jnp.float32))
    normed_low = normed.astype(jnp.bfloat16)
    qkv_mixed = jnp.dot(
        normed_low, qkv_weight, preferred_element_type=jnp.float32
    ) + qkv_bias.astype(jnp.float32)
    query_h = rotate(qkv_mixed[:, :model_width].reshape(tok_rows, H, HD), cos_tab, sin_tab).astype(
        jnp.bfloat16
    )
    key_low = (
        rotate(
            qkv_mixed[:, model_width : 2 * model_width].reshape(tok_rows, H, HD), cos_tab, sin_tab
        )
        .astype(jnp.bfloat16)
        .reshape(tok_rows, model_width)
    )
    value_low = qkv_mixed[:, 2 * model_width :].astype(jnp.bfloat16)

    def block_scores(keys_blk, first_key):
        key_count = keys_blk.shape[0]
        clip_k = clip_of(lens_row, first_key + jnp.arange(key_count, dtype=jnp.int32))
        raw_scores = jnp.einsum(
            "qhd,khd->hqk",
            query_h,
            keys_blk.reshape(key_count, H, HD),
            preferred_element_type=jnp.float32,
        )
        allowed = (clip_q[:, None] == clip_k[None, :])[None]
        return (jnp.where(allowed, 0.125 * raw_scores, NEG_FILL), allowed)

    def stats_step(state, sliced, first_key):
        row_max, row_sum = state
        scores, allowed = block_scores(sliced[0], first_key)
        new_max = jnp.maximum(row_max, jnp.max(scores, -1))
        weights = jnp.where(allowed, jnp.exp(scores - new_max[:, :, None]), 0.0)
        return (new_max, row_sum * jnp.exp(row_max - new_max) + jnp.sum(weights, -1))

    stats_init = (
        jnp.full((H, tok_rows), NEG_FILL, jnp.float32),
        jnp.zeros((H, tok_rows), jnp.float32),
    )
    row_max, row_sum = in_blocks(
        stats_step, stats_init, (lax.all_gather(key_low, "blk", axis=0, tiled=True),)
    )
    log_sum = row_max + jnp.log(row_sum)

    def output_step(acc_state, sliced, first_key):
        keys_blk, values_blk = sliced
        key_count = keys_blk.shape[0]
        scores, allowed = block_scores(keys_blk, first_key)
        weights = jnp.where(allowed, jnp.exp(scores - log_sum[:, :, None]), 0.0)
        return acc_state + jnp.einsum(
            "hqk,khd->qhd",
            weights.astype(jnp.bfloat16),
            values_blk.reshape(key_count, H, HD),
            preferred_element_type=jnp.float32,
        )

    acc_init = jnp.zeros((tok_rows, H, HD), jnp.float32)
    attended_f = in_blocks(
        output_step,
        acc_init,
        (
            lax.all_gather(key_low, "blk", axis=0, tiled=True),
            lax.all_gather(value_low, "blk", axis=0, tiled=True),
        ),
    )
    attended_low = attended_f.reshape(tok_rows, model_width).astype(jnp.bfloat16)
    middle = (
        residual
        + jnp.dot(attended_low, proj_weight, preferred_element_type=jnp.float32)
        + proj_bias.astype(jnp.float32)
    )
    normed_two, hat_two, inv_two = norm_fwd(middle, mlp_gain_f, mlp_shift.astype(jnp.float32))
    normed_two_low = normed_two.astype(jnp.bfloat16)
    hidden = jnp.dot(
        normed_two_low, up_weight, preferred_element_type=jnp.float32
    ) + up_bias.astype(jnp.float32)
    active_low = jax.nn.gelu(hidden).astype(jnp.bfloat16)
    result = (
        middle
        + jnp.dot(active_low, down_weight, preferred_element_type=jnp.float32)
        + down_bias.astype(jnp.float32)
    )
    layer_out = result.astype(jnp.bfloat16)[None]
    cot_low = out_cotangent[0]
    cot_f = cot_low.astype(jnp.float32)
    grad_down_w = outer_sum(active_low, cot_low)
    grad_down_b = jnp.sum(cot_f, 0)
    d_active = times_transposed(cot_low, down_weight)
    hidden_unused, gelu_back = jax.vjp(jax.nn.gelu, hidden)
    d_hidden = gelu_back(d_active)[0].astype(jnp.bfloat16)
    grad_up_w = outer_sum(normed_two_low, d_hidden)
    grad_up_b = jnp.sum(d_hidden.astype(jnp.float32), 0)
    d_normed_two = times_transposed(d_hidden, up_weight)
    d_mid_norm, grad_mlp_gain, grad_mlp_shift = norm_back(
        d_normed_two, hat_two, inv_two, mlp_gain_f
    )
    d_middle = cot_f + d_mid_norm
    d_branch = d_middle.astype(jnp.bfloat16)
    grad_proj_w = outer_sum(attended_low, d_branch)
    grad_proj_b = jnp.sum(d_branch.astype(jnp.float32), 0)
    d_attended = (
        times_transposed(d_branch, proj_weight).astype(jnp.bfloat16).reshape(tok_rows, H, HD)
    )
    delta = jnp.einsum("qhd,qhd->hq", d_attended.astype(jnp.float32), attended_f)

    def back_step(state, sliced, first_key):
        dq_acc, buffers = state
        keys_blk, values_blk = sliced
        key_count = keys_blk.shape[0]
        scores, allowed = block_scores(keys_blk, first_key)
        weights = jnp.where(allowed, jnp.exp(scores - log_sum[:, :, None]), 0.0)
        d_weights = jnp.einsum(
            "qhd,khd->hqk",
            d_attended,
            values_blk.reshape(key_count, H, HD),
            preferred_element_type=jnp.float32,
        )
        d_scores = (weights * (d_weights - delta[:, :, None])).astype(jnp.bfloat16)
        dq_acc = dq_acc + 0.125 * jnp.einsum(
            "hqk,khd->qhd",
            d_scores,
            keys_blk.reshape(key_count, H, HD),
            preferred_element_type=jnp.float32,
        )
        d_keys = 0.125 * jnp.einsum(
            "hqk,qhd->khd", d_scores, query_h, preferred_element_type=jnp.float32
        )
        d_values = jnp.einsum(
            "hqk,qhd->khd",
            weights.astype(jnp.bfloat16),
            d_attended,
            preferred_element_type=jnp.float32,
        )
        key_buffer = add_rows(buffers[0], d_keys.reshape(key_count, model_width), first_key)
        value_buffer = add_rows(buffers[1], d_values.reshape(key_count, model_width), first_key)
        buffers = (key_buffer, value_buffer)
        return (dq_acc, buffers)

    buffer_init = (
        jnp.zeros((seq_len, model_width), jnp.float32),
        jnp.zeros((seq_len, model_width), jnp.float32),
    )
    back_init = (jnp.zeros((tok_rows, H, HD), jnp.float32), buffer_init)
    d_queries, key_grads = in_blocks(
        back_step,
        back_init,
        (
            lax.all_gather(key_low, "blk", axis=0, tiled=True),
            lax.all_gather(value_low, "blk", axis=0, tiled=True),
        ),
    )
    d_keys_own, d_values_own = (
        lax.psum_scatter(key_grads[0], "blk", scatter_dimension=0, tiled=True),
        lax.psum_scatter(key_grads[1], "blk", scatter_dimension=0, tiled=True),
    )
    d_queries_pre = rotate(d_queries, cos_tab, -sin_tab).reshape(tok_rows, model_width)
    d_keys_pre = rotate(d_keys_own.reshape(tok_rows, H, HD), cos_tab, -sin_tab).reshape(
        tok_rows, model_width
    )
    d_mixed = jnp.concatenate([d_queries_pre, d_keys_pre, d_values_own], axis=1).astype(
        jnp.bfloat16
    )
    grad_qkv_w = outer_sum(normed_low, d_mixed)
    grad_qkv_b = jnp.sum(d_mixed.astype(jnp.float32), 0)
    d_normed = times_transposed(d_mixed, qkv_weight)
    d_res_norm, grad_attn_gain, grad_attn_shift = norm_back(d_normed, hat_one, inv_one, attn_gain_f)
    tokens_grad = (d_middle + d_res_norm)[None]
    summed = (
        lax.psum_scatter(grad_qkv_w, ("batch", "blk"), scatter_dimension=0, tiled=True),
        lax.psum_scatter(grad_proj_w, ("batch", "blk"), scatter_dimension=0, tiled=True),
        lax.psum_scatter(grad_up_w, ("batch", "blk"), scatter_dimension=0, tiled=True),
        lax.psum_scatter(grad_down_w, ("batch", "blk"), scatter_dimension=0, tiled=True),
        lax.psum_scatter(grad_attn_gain, ("batch", "blk"), scatter_dimension=0, tiled=True),
        lax.psum_scatter(grad_attn_shift, ("batch", "blk"), scatter_dimension=0, tiled=True),
        lax.psum_scatter(grad_qkv_b, ("batch", "blk"), scatter_dimension=0, tiled=True),
        lax.psum_scatter(grad_proj_b, ("batch", "blk"), scatter_dimension=0, tiled=True),
        lax.psum_scatter(grad_mlp_gain, ("batch", "blk"), scatter_dimension=0, tiled=True),
        lax.psum_scatter(grad_mlp_shift, ("batch", "blk"), scatter_dimension=0, tiled=True),
        lax.psum_scatter(grad_up_b, ("batch", "blk"), scatter_dimension=0, tiled=True),
        lax.psum_scatter(grad_down_b, ("batch", "blk"), scatter_dimension=0, tiled=True),
    )
    return (
        layer_out,
        tokens_grad,
        summed[4],
        summed[5],
        summed[0],
        summed[6],
        summed[1],
        summed[7],
        summed[8],
        summed[9],
        summed[2],
        summed[10],
        summed[3],
        summed[11],
    )


BF = jnp.bfloat16
F32 = jnp.float32
AXES = ("x", "core", "zh", "zl", "y")
ROW = ("zh", "zl", "y")
CLUSTER = ("core", "zl", "y")
GELU_A = 0.7978845608028654
GELU_B = 0.044715


def mm(left, right):
    return jnp.dot(left, right, preferred_element_type=F32)


def swap_over(value, *names):
    mask = sum(16 >> AXES.index(name) for name in names)
    return lax.ppermute(value, AXES, [(i, i ^ mask) for i in range(32)])


def whole(shape):
    zeros = (0,) * len(shape)
    return pl.BlockSpec(shape, lambda *_: zeros)


def call(body, grid, in_specs, out_specs, out_shape, scratch, flops, nbytes, args, scalars=None):
    params = pltpu.CompilerParams(vmem_limit_bytes=48 << 20)
    cost = pl.CostEstimate(flops=flops, bytes_accessed=nbytes, transcendentals=0)
    if scalars is None:
        return pl.pallas_call(
            body,
            grid=grid,
            in_specs=in_specs,
            out_specs=out_specs,
            out_shape=out_shape,
            scratch_shapes=scratch,
            compiler_params=params,
            cost_estimate=cost,
        )(*args)
    return pl.pallas_call(
        body,
        grid_spec=pltpu.PrefetchScalarGridSpec(
            num_scalar_prefetch=1,
            grid=grid,
            in_specs=in_specs,
            out_specs=out_specs,
            scratch_shapes=scratch,
        ),
        out_shape=out_shape,
        compiler_params=params,
        cost_estimate=cost,
    )(scalars, *args)


def arr(shape, dtype):
    return jax.ShapeDtypeStruct(shape, dtype)


def standardize(x):
    mean = jnp.mean(x, -1, keepdims=True)
    centered = x - mean
    inv = lax.rsqrt(jnp.mean(centered * centered, -1, keepdims=True) + 1e-06)
    return centered * inv, inv


def swap_halves(x):
    lane = lax.broadcasted_iota(jnp.int32, x.shape, 1)
    return jnp.where(lane % 64 < 32, pltpu.roll(x, 96, 1), pltpu.roll(x, 32, 1))


def gelu_both(h):
    t = jnp.tanh(GELU_A * (h + GELU_B * h * h * h))
    act = 0.5 * h * (1.0 + t)
    slope = 0.5 * (1.0 + t) + 0.5 * h * (1.0 - t * t) * (GELU_A * (1.0 + 3.0 * GELU_B * h * h))
    return act, slope


def down_back_body(cot, down, d_act, bias_part):
    @pl.when(pl.program_id(0) == 0)
    def _():
        bias_part[...] = jnp.sum(cot[...].astype(F32), 0, keepdims=True)

    d_act[...] = times_transposed(cot[...], down[...])


def qkv_body(
    b0, b1, b2, b3a, b3b, gain, shift, w3, bias3, cos, sin, q_out, k_out, v_out, hat_out, normed
):
    g = gain[...].astype(F32)
    s = shift[...].astype(F32)
    first = 0
    for block in (b0, b1, b2, b3a, b3b):
        rows = block.shape[0]
        hat, _ = standardize(block[...].astype(F32))
        hat_out[first : first + rows, :] = hat.astype(BF)
        normed[first : first + rows, :] = (hat * g + s).astype(BF)
        first += rows
    mixed = mm(normed[...], w3[...]) + bias3[...].astype(F32)
    c = cos[...]
    sn = sin[...]
    q = mixed[:, :128]
    k = mixed[:, 128:256]
    q_out[...] = ((q * c + swap_halves(q) * sn) * 0.125).astype(BF)
    k_out[...] = (k * c + swap_halves(k) * sn).astype(BF)
    v_out[...] = mixed[:, 256:].astype(BF)


def head_mask(shape, head):
    return lax.broadcasted_iota(jnp.int32, shape, 1) // 64 == head


def attend_body(place, q, k0, k1, v0, v1, id_col, id_row, att_f, att_low, probs):
    keys = jnp.concatenate([k0[...], k1[...]], 0)
    values = jnp.concatenate([v0[...], v1[...]], 0)
    queries = q[...]
    allowed = id_col[...] == id_row[...]
    halves = []
    for head in range(2):
        mine = jnp.where(head_mask(queries.shape, head), queries, jnp.zeros_like(queries))
        scores = jnp.where(allowed, times_transposed(keys, mine), NEG_FILL)
        weights = jnp.exp(scores - jnp.max(scores, 0, keepdims=True))
        low = (weights / jnp.sum(weights, 0, keepdims=True)).astype(BF)
        probs[head] = low
        halves.append(outer_sum(values, low)[64 * head : 64 * head + 64])
    out = jnp.concatenate(halves, 0).T
    att_f[...] = out
    step = pl.program_id(0)
    att_low[place[0] ^ (2 * step)] = out[:128].astype(BF)
    att_low[place[0] ^ (2 * step + 1)] = out[128:].astype(BF)


def proj_body(att, tok, proj_w, proj_b, gain, shift, middle, normed, att_rows):
    rows = jnp.concatenate([att[k] for k in range(8)], 1)
    att_rows[...] = rows
    mid = tok[...].astype(F32) + mm(rows, proj_w[...]) + proj_b[...].astype(F32)
    middle[...] = mid
    hat, _ = standardize(mid)
    normed[...] = (hat * gain[...].astype(F32) + shift[...].astype(F32)).astype(BF)


def mlp_body(
    normed, d_act, up_w, up_b, middle, cot, gain, proj_w,
    active, up_bias, d_mid, d_branch, d_att, vectors, acc,
):
    step = pl.program_id(0)
    hidden = mm(normed[...], up_w[...]) + up_b[...].astype(F32)
    act, slope = gelu_both(hidden)
    active[...] = act.astype(BF)
    d_hidden = (d_act[...] * slope).astype(BF)
    up_bias[...] = jnp.sum(d_hidden.astype(F32), 0, keepdims=True)
    part = times_transposed(d_hidden, up_w[...])

    @pl.when(step == 0)
    def _():
        acc[...] = part

    @pl.when(step > 0)
    def _():
        acc[...] += part

    @pl.when(step == pl.num_programs(0) - 1)
    def _():
        up = acc[...]
        hat, inv = standardize(middle[...])
        e = up * gain[...].astype(F32)
        inner = e - jnp.mean(e, -1, keepdims=True) - hat * jnp.mean(e * hat, -1, keepdims=True)
        d_m = cot[...].astype(F32) + inv * inner
        d_mid[...] = d_m
        d_b = d_m.astype(BF)
        d_branch[...] = d_b
        vectors[0:1] = jnp.sum(up * hat, 0, keepdims=True)
        vectors[1:2] = jnp.sum(up, 0, keepdims=True)
        vectors[2:3] = jnp.sum(d_b.astype(F32), 0, keepdims=True)
        d_a = times_transposed(d_b, proj_w[...]).astype(BF)
        for k in range(8):
            d_att[k] = d_a[:, 128 * k : 128 * k + 128]


def proj_grad_body(place, att, d_branch, out):
    grad = outer_sum(att[...], d_branch[...])
    for i in range(32):
        rel = place[1] ^ i
        x, core, zh, zl, y = ((rel >> s) & 1 for s in (4, 3, 2, 1, 0))
        out[core * 16 + y * 8 + zl * 4 + x * 2 + zh] = grad[32 * i : 32 * i + 32]


def mlp_grad_body(place, *refs):
    n_refs, c_refs = refs[0:8], refs[8:16]
    up_w, up_b, down_w = refs[16:19]
    down_keep, down_send, up_keep, up_send, n_all, c_all, grad = refs[19:]
    for j in range(8):
        n_all[128 * j : 128 * j + 128, :] = n_refs[j][...]
        c_all[128 * j : 128 * j + 128, :] = c_refs[j][...]
    n = n_all[...]
    c = c_all[...]
    act, slope = gelu_both(mm(n, up_w[...]) + up_b[...].astype(F32))
    grad_down = outer_sum(act.astype(BF), c)
    for g in range(4):
        rows = grad_down[128 * g : 128 * g + 128]
        if g < 2:
            down_keep[g] = rows
        else:
            down_send[g - 2] = rows.astype(BF)
    d_hidden = (times_transposed(c, down_w[...]) * slope).astype(BF)
    for g in range(4):
        lanes = pl.ds(pl.multiple_of((place[2] ^ g) * 128, 128), 128)
        grad[:, lanes] = outer_sum(n, d_hidden[:, 128 * g : 128 * g + 128])
    for rz in range(2):
        for core in range(2):
            first = core * 256 + (place[4] ^ rz) * 128
            keep = pl.multiple_of(place[3] * 512 + first, 128)
            send = pl.multiple_of((1 - place[3]) * 512 + first, 128)
            up_keep[rz, core] = grad[pl.ds(keep, 128), :]
            up_send[rz, core] = grad[pl.ds(send, 128), :].astype(BF)


def attend_back_body(
    place, probs, d_att, att_f, q, k_all, v_all, cos, sin, d_all, bias_part, *rest
):
    pieces, (dq, dk, dv) = rest[:8], rest[8:]
    step = pl.program_id(0)
    keys = k_all[...]
    values = v_all[...]
    queries = q[...]
    d_out = jnp.concatenate([d_att[place[0] ^ (2 * step)], d_att[place[0] ^ (2 * step + 1)]], 0)
    products = (d_out.astype(F32) * att_f[...]).T
    key_parts, value_parts, query_parts = [], [], []
    for head in range(2):
        weights = probs[head]
        mine = jnp.where(head_mask(d_out.shape, head), d_out, jnp.zeros_like(d_out))
        delta = jnp.sum(products[64 * head : 64 * head + 64], 0, keepdims=True)
        d_weights = times_transposed(values, mine)
        d_scores = (weights.astype(F32) * (d_weights - delta)).astype(BF)
        key_parts.append(mm(d_scores, queries))
        value_parts.append(mm(weights, d_out))
        query_parts.append(outer_sum(keys, d_scores)[64 * head : 64 * head + 64])
    first = head_mask((1024, 128), 0)
    dk_new = jnp.where(first, key_parts[0], key_parts[1])
    dv_new = jnp.where(first, value_parts[0], value_parts[1])
    dq[pl.ds(pl.multiple_of(step * 256, 256), 256), :] = jnp.concatenate(query_parts, 0).T

    @pl.when(step == 0)
    def _():
        dk[...] = dk_new
        dv[...] = dv_new

    @pl.when(step > 0)
    def _():
        dk[...] += dk_new
        dv[...] += dv_new

    @pl.when(step == pl.num_programs(0) - 1)
    def _():
        total = jnp.zeros((1, 384), F32)
        for j in range(8):
            rows = slice(128 * j, 128 * j + 128)
            c = cos[rows, :]
            sn = sin[rows, :]
            back_q = 0.125 * dq[rows, :]
            back_k = dk[rows, :]
            piece = jnp.concatenate(
                [
                    back_q * c - swap_halves(back_q) * sn,
                    back_k * c - swap_halves(back_k) * sn,
                    dv[rows, :],
                ],
                1,
            ).astype(BF)
            pieces[j][...] = piece
            d_all[rows, :] = piece
            total = total + jnp.sum(piece.astype(F32), 0, keepdims=True)
        bias_part[...] = total


def rel_block(step, place):
    rel = jnp.where(step < 2, 2, 0) + step % 2
    return ((rel & 1) ^ place[3]) * 2 + ((rel >> 1) ^ place[5])


def qkv_grad_body(place, h0, h1, d_all, bias_part, gain, shift, w3, send, keep, gain_part, shift_part):
    step = pl.program_id(0)
    d = d_all[...]
    inner = outer_sum(h0[...], d[:512]) + outer_sum(h1[...], d[512:])
    total = bias_part[...]
    w = w3[...].astype(F32)
    gain_part[...] = jnp.sum(w * inner, 1, keepdims=True)
    shift_part[...] = jnp.sum(w * total, 1, keepdims=True)
    grad = gain[...].astype(F32) * inner + shift[...].astype(F32) * total

    @pl.when(step < 2)
    def _():
        send[0] = grad.astype(BF)

    @pl.when(step >= 2)
    def _():
        keep[0] = grad


def last_body(place, *refs):
    pieces = refs[:8]
    w, tok, d_mid, gain, out, d_mixed, acc = refs[8:]
    step = pl.program_id(0)

    @pl.when(step == 0)
    def _():
        for j in range(8):
            lanes = pl.ds(pl.multiple_of((place[0] ^ j) * 128, 128), 128)
            for p in range(3):
                d_mixed[p, :, lanes] = pieces[j][:, 128 * p : 128 * p + 128]

    part = times_transposed(d_mixed[step], w[...])

    @pl.when(step == 0)
    def _():
        acc[...] = part

    @pl.when(step > 0)
    def _():
        acc[...] += part

    @pl.when(step == pl.num_programs(0) - 1)
    def _():
        hat, inv = standardize(tok[...].astype(F32))
        e = acc[...] * gain[...].astype(F32)
        inner = e - jnp.mean(e, -1, keepdims=True) - hat * jnp.mean(e * hat, -1, keepdims=True)
        out[...] = d_mid[...] + inv * inner


def row_tables(lens_row, k):
    blocks = jnp.arange(8, dtype=jnp.int32) ^ k
    pos = (blocks[:, None] * 128 + jnp.arange(128, dtype=jnp.int32)[None, :]).reshape(1024)
    clip_end = jnp.cumsum(lens_row)
    starts = clip_end - lens_row
    ids = jnp.sum((pos[:, None] >= clip_end[None, :]).astype(jnp.int32), axis=1)
    member = ids[:, None] == jnp.arange(lens_row.shape[0], dtype=jnp.int32)[None, :]
    within = pos - jnp.sum(jnp.where(member, starts[None, :], 0), axis=1)
    coords = jnp.stack([within // 196, within // 14 % 14, within % 14], axis=1).astype(F32)
    pair = jnp.arange(128) % 32
    table = pair_table()[:, pair]
    angles = jnp.sum(coords[:, :, None] * table[None], axis=1)
    sign = jnp.where(jnp.arange(128) % 64 < 32, -1.0, 1.0).astype(F32)
    return ids, jnp.cos(angles), jnp.sin(angles) * sign[None, :]


def row_gather(a):
    half = a.shape[0] // 2

    def local(v):
        y1 = swap_over(v, "y")
        z1 = swap_over(v, "zl")
        return y1, z1, swap_over(z1[:half], "y"), swap_over(y1[half:], "zl")

    far = swap_over(a, "zh")
    return (a, *local(a)), (far, *local(far))


def cluster_gather(a):
    y1 = swap_over(a, "y")
    z1 = swap_over(a, "zl")
    d1 = swap_over(a, "y", "zl")
    return [a, y1, z1, d1] + [swap_over(v, "core") for v in (a, y1, z1, d1)]


def fast_shards(
    tokens_in, clip_lengths, attn_gain, attn_shift, qkv_weight, qkv_bias, proj_weight, proj_bias,
    mlp_gain, mlp_shift, up_weight, up_bias, down_weight, down_bias, out_cotangent,
):
    x, core, zh, zl, y = (lax.axis_index(name) for name in AXES)
    k = zh * 4 + zl * 2 + y
    me = x * 16 + core * 8 + k
    place = jnp.stack([k, me, x * 2 + zh, x, zh, core]).astype(jnp.int32)
    tok = tokens_in[0]
    cot = out_cotangent[0]
    row = lambda v: v.reshape(1, -1)

    near, far = row_gather(tok)
    cots = cluster_gather(lax.optimization_barrier((cot, far))[0])

    ids, cos_tab, sin_tab = row_tables(clip_lengths[0], k)
    w3 = jnp.concatenate(
        [lax.dynamic_slice(qkv_weight, (0, p * 1024 + k * 128), (1024, 128)) for p in range(3)], 1
    )
    bias3 = jnp.concatenate(
        [lax.dynamic_slice(qkv_bias, (p * 1024 + k * 128,), (128,)) for p in range(3)]
    )
    firsts = [
        ((x ^ (g >> 1)) * 16 + core * 8 + (zh ^ (g & 1)) * 4 + zl * 2 + y) * 128 for g in range(4)
    ]
    up_part = jnp.concatenate([lax.dynamic_slice(up_weight, (0, f), (1024, 128)) for f in firsts], 1)
    up_b_part = jnp.concatenate([lax.dynamic_slice(up_bias, (f,), (128,)) for f in firsts])
    down_part = jnp.concatenate(
        [lax.dynamic_slice(down_weight, (f, 0), (128, 1024)) for f in firsts], 0
    )

    d_act, down_bias_part = call(
        down_back_body,
        (4,),
        [whole((128, 1024)), pl.BlockSpec((1024, 1024), lambda i: (i, 0))],
        [pl.BlockSpec((128, 1024), lambda i: (0, i)), whole((1, 1024))],
        [arr((128, 4096), F32), arr((1, 1024), F32)],
        [],
        1 << 30,
        10 << 20,
        (cot, down_weight),
    )

    def qkv_half(blocks, part):
        rows = slice(512 * part, 512 * part + 512)
        ins = (
            *blocks, row(attn_gain), row(attn_shift), w3, row(bias3), cos_tab[rows], sin_tab[rows]
        )
        outs = [arr((512, 128), BF)] * 3 + [arr((512, 1024), BF)]
        return call(
            qkv_body,
            (1,),
            [whole(v.shape) for v in ins],
            [whole(o.shape) for o in outs],
            outs,
            [pltpu.VMEM((512, 1024), BF)],
            400 << 20,
            4 << 20,
            ins,
        )

    q0, k0, v0, hat0 = qkv_half(near, 0)
    q1, k1, v1, hat1 = qkv_half(far, 1)
    q_all = jnp.concatenate([q0, q1], 0)
    k_all = jnp.concatenate([k0, k1], 0)
    v_all = jnp.concatenate([v0, v1], 0)
    half = whole((512, 128))
    att_f, att_low, probs = call(
        attend_body,
        (4,),
        [
            pl.BlockSpec((256, 128), lambda i, s: (i, 0)), half, half, half, half,
            whole((1024, 1)), pl.BlockSpec((1, 256), lambda i, s: (0, i)),
        ],
        [
            pl.BlockSpec((256, 128), lambda i, s: (i, 0)),
            whole((8, 128, 128)),
            pl.BlockSpec((2, 1024, 256), lambda i, s: (0, 0, i)),
        ],
        [arr((1024, 128), F32), arr((8, 128, 128), BF), arr((2, 1024, 1024), BF)],
        [],
        1 << 30,
        8 << 20,
        (q_all, k0, k1, v0, v1, ids.reshape(1024, 1), ids.reshape(1, 1024)),
        place,
    )
    att_in = lax.all_to_all(att_low, ROW, 0, 0, tiled=True)
    ins = (
        att_in, tok, proj_weight, row(proj_bias), row(mlp_gain), row(mlp_shift)
    )
    outs = [arr((128, 1024), F32), arr((128, 1024), BF), arr((128, 1024), BF)]
    middle, normed2, att_rows = call(
        proj_body,
        (1,),
        [whole(v.shape) for v in ins],
        [whole(o.shape) for o in outs],
        outs,
        [],
        256 << 20,
        4 << 20,
        ins,
    )
    normeds = cluster_gather(normed2)
    wide = pl.BlockSpec((128, 1024), lambda i: (0, i))
    fixed = whole((128, 1024))
    active, up_bias_part, d_mid, d_branch, d_att, vectors = call(
        mlp_body,
        (4,),
        [
            fixed, wide, pl.BlockSpec((1024, 1024), lambda i: (0, i)),
            pl.BlockSpec((1, 1024), lambda i: (0, i)), fixed, fixed, whole((1, 1024)),
            whole((1024, 1024)),
        ],
        [
            wide, pl.BlockSpec((1, 1024), lambda i: (0, i)), fixed, fixed, whole((8, 128, 128)),
            whole((8, 1024)),
        ],
        [
            arr((128, 4096), BF), arr((1, 4096), F32), arr((128, 1024), F32), arr((128, 1024), BF),
            arr((8, 128, 128), BF), arr((8, 1024), F32),
        ],
        [pltpu.VMEM((128, 1024), F32)],
        2 << 30,
        16 << 20,
        (normed2, d_act, up_weight, row(up_bias), middle, cot, row(mlp_gain), proj_weight),
    )
    d_att_in = lax.all_to_all(d_att, ROW, 0, 0, tiled=True)

    result = middle + mm(active, down_weight) + down_bias.astype(F32)
    layer_out = result.astype(BF)[None]

    proj_parts = call(
        proj_grad_body,
        (1,),
        [whole((128, 1024))] * 2,
        whole((32, 32, 1024)),
        arr((32, 32, 1024), F32),
        [],
        256 << 20,
        5 << 20,
        (att_rows, d_branch),
        place,
    )
    total = proj_parts
    for name in ("core", "y", "zl", "x", "zh"):
        count = total.shape[0] // 2
        total = total[:count] + swap_over(total[count:].astype(BF), name).astype(F32)
    grad_proj = total[0]

    ins = (*normeds, *cots, up_part, row(up_b_part), down_part)
    outs = [
        arr((2, 128, 1024), F32), arr((2, 128, 1024), BF), arr((2, 2, 128, 512), F32),
        arr((2, 2, 128, 512), BF),
    ]
    down_keep, down_send, up_keep, up_send = call(
        mlp_grad_body,
        (1,),
        [whole(v.shape) for v in ins],
        [whole(o.shape) for o in outs],
        outs,
        [
            pltpu.VMEM((1024, 1024), BF), pltpu.VMEM((1024, 1024), BF),
            pltpu.VMEM((1024, 512), F32),
        ],
        4 << 30,
        12 << 20,
        ins,
        place,
    )

    def two_sums(keep, send):
        keep = keep + swap_over(send, "x").astype(F32)
        return keep[0] + swap_over(keep[1].astype(BF), "zh").astype(F32)

    grad_down = two_sums(down_keep, down_send)
    grad_up = two_sums(up_keep, up_send).astype(BF)
    grad_up = lax.all_to_all(grad_up.reshape(8, 32, 512), CLUSTER, 0, 0, tiled=True)
    grad_up = grad_up.reshape(2, 4, 32, 2, 2, 128).transpose(2, 3, 0, 4, 1, 5)
    grad_up = grad_up.reshape(32, 4096).astype(F32)

    mids = jnp.concatenate(
        [v.reshape(32, -1) for v in (vectors[0], vectors[1], vectors[2], down_bias_part, up_bias_part)],
        1,
    )
    mids = jnp.sum(lax.all_to_all(mids, AXES, 0, 0, tiled=True), 0)

    step_rows = pl.BlockSpec((256, 128), lambda i, s: (i, 0))
    full = whole((1024, 128))
    back = call(
        attend_back_body,
        (4,),
        [
            pl.BlockSpec((2, 1024, 256), lambda i, s: (0, 0, i)), whole((8, 128, 128)), step_rows,
            step_rows, full, full, full, full,
        ],
        [whole((1024, 384)), whole((1, 384))] + [whole((128, 384))] * 8,
        [arr((1024, 384), BF), arr((1, 384), F32)] + [arr((128, 384), BF)] * 8,
        [pltpu.VMEM((1024, 128), F32)] * 3,
        2 << 30,
        8 << 20,
        (probs, d_att_in, att_f, q_all, k_all, v_all, cos_tab, sin_tab),
        place,
    )
    d_all, qkv_bias_part = back[:2]
    pieces = back[2:]
    moved = [pieces[0]] + [
        swap_over(pieces[j], *[n for n, bit in zip(ROW, (4, 2, 1)) if j & bit]) for j in range(1, 8)
    ]

    block_of = lambda i, s: (rel_block(i, s), 0)
    lanes_of = lambda i, s: (0, rel_block(i, s))
    send, keep, gain_part, shift_part = call(
        qkv_grad_body,
        (4,),
        [
            pl.BlockSpec((512, 256), lanes_of), pl.BlockSpec((512, 256), lanes_of),
            whole((1024, 384)), whole((1, 384)), pl.BlockSpec((256, 1), block_of),
            pl.BlockSpec((256, 1), block_of), pl.BlockSpec((256, 384), block_of),
        ],
        [
            pl.BlockSpec((1, 256, 384), lambda i, s: (jnp.minimum(i, 1), 0, 0)),
            pl.BlockSpec((1, 256, 384), lambda i, s: (jnp.maximum(i - 2, 0), 0, 0)),
            pl.BlockSpec((256, 1), block_of), pl.BlockSpec((256, 1), block_of),
        ],
        [
            arr((2, 256, 384), BF), arr((2, 256, 384), F32), arr((1024, 1), F32),
            arr((1024, 1), F32),
        ],
        [],
        800 << 20,
        4 << 20,
        (
            hat0, hat1, d_all, qkv_bias_part, attn_gain.reshape(1024, 1),
            attn_shift.reshape(1024, 1), w3,
        ),
        place,
    )
    keep = keep + swap_over(send, "core").astype(F32)
    grad_qkv = (keep[0] + swap_over(keep[1].astype(BF), "x").astype(F32)).astype(BF)
    grad_qkv = lax.all_to_all(grad_qkv.reshape(8, 32, 384), ROW, 0, 0, tiled=True)
    grad_qkv = grad_qkv.reshape(8, 32, 3, 128).transpose(1, 2, 0, 3).reshape(32, 3072).astype(F32)

    spread = lax.dynamic_update_slice(
        jnp.zeros((3, 1024), F32), qkv_bias_part.reshape(3, 128), (0, k * 128)
    )
    lates = jnp.concatenate(
        [v.reshape(32, -1) for v in (gain_part, shift_part, spread)], 1
    )
    lates = jnp.sum(lax.all_to_all(lates, AXES, 0, 0, tiled=True), 0)

    tokens_grad = call(
        last_body,
        (3,),
        [whole((128, 384))] * 8
        + [pl.BlockSpec((1024, 1024), lambda i, s: (0, i)), whole((128, 1024)), whole((128, 1024)),
           whole((1, 1024))],
        whole((128, 1024)),
        arr((128, 1024), F32),
        [pltpu.VMEM((3, 128, 1024), BF), pltpu.VMEM((128, 1024), F32)],
        800 << 20,
        8 << 20,
        (*moved, qkv_weight, tok, d_mid, row(attn_gain)),
        place,
    )[None]

    return (
        layer_out, tokens_grad, lates[:32], lates[32:64], grad_qkv, lates[64:160], grad_proj,
        mids[64:96], mids[:32], mids[32:64], grad_up, mids[128:256], grad_down, mids[96:128],
    )


def fast_solution(mesh):
    wide_mesh = Mesh(mesh.devices.reshape(2, 2, 2, 2, 2), AXES)
    batch, blk = AXES[:2], AXES[2:]
    spread = P(batch, blk, None)
    return jax.shard_map(
        fast_shards,
        mesh=wide_mesh,
        in_specs=(spread, P(batch, None)) + (P(),) * 12 + (spread,),
        out_specs=(spread, spread)
        + tuple(P(AXES, None) if i in (2, 4, 8, 10) else P(AXES) for i in range(12)),
        check_vma=False,
    )


def solution(mesh):
    if tuple(mesh.devices.shape) == (4, 8):
        return fast_solution(mesh)
    placed = (
        P("batch", "blk", None),
        P("batch", None),
        P(),
        P(),
        P(),
        P(),
        P(),
        P(),
        P(),
        P(),
        P(),
        P(),
        P(),
        P(),
        P("batch", "blk", None),
    )
    return jax.shard_map(
        shards,
        mesh=mesh,
        in_specs=placed,
        out_specs=(
            P("batch", "blk", None),
            P("batch", "blk", None),
            P(("batch", "blk")),
            P(("batch", "blk")),
            P(("batch", "blk"), None),
            P(("batch", "blk")),
            P(("batch", "blk"), None),
            P(("batch", "blk")),
            P(("batch", "blk")),
            P(("batch", "blk")),
            P(("batch", "blk"), None),
            P(("batch", "blk")),
            P(("batch", "blk"), None),
            P(("batch", "blk")),
        ),
        check_vma=False,
    )
```

```python
import math

import jax
import jax.numpy as jnp
import numpy as np
from jax import lax
from jax.experimental import pallas as pl
from jax.experimental.pallas import tpu as pltpu
from jax.sharding import Mesh
from jax.sharding import PartitionSpec as P

H = 16
HD = 64


NEG_FILL = -1e30


def pair_table():
    part_map = [0] * 10 + [1] * 11 + [2] * 11
    freq_list = [10000.0 ** (-rank / 10.0) for rank in range(10)] + [
        10000.0 ** (-rank / 11.0) for rank in range(11)
    ] * 2
    table_rows = [
        [freq_list[column] if part_map[column] == axis_id else 0.0 for column in range(32)]
        for axis_id in range(3)
    ]
    return jnp.array(table_rows, dtype=jnp.float32)


def clip_of(lengths_row, positions):
    clip_end = jnp.cumsum(lengths_row)
    return jnp.sum((positions[:, None] >= clip_end[None, :]).astype(jnp.int32), axis=1)


def clip_layout(lengths_row, positions):
    clip_end = jnp.cumsum(lengths_row)
    starts = clip_end - lengths_row
    clip_ids = jnp.sum((positions[:, None] >= clip_end[None, :]).astype(jnp.int32), axis=1)
    member = clip_ids[:, None] == jnp.arange(lengths_row.shape[0], dtype=jnp.int32)[None, :]
    within = positions - jnp.sum(jnp.where(member, starts[None, :], 0), axis=1)
    coords = jnp.stack([within // 196, within // 14 % 14, within % 14], axis=1).astype(jnp.float32)
    angles = jnp.dot(coords, pair_table(), precision=lax.Precision.HIGHEST)
    return (clip_ids, jnp.cos(angles), jnp.sin(angles))


def rotate(values, cos_tab, sin_tab):
    half_dim = values.shape[-1] // 2
    first_half = values[..., :half_dim]
    second_half = values[..., half_dim:]
    cos_b = cos_tab[:, None, :]
    sin_b = sin_tab[:, None, :]
    return jnp.concatenate(
        [first_half * cos_b - second_half * sin_b, first_half * sin_b + second_half * cos_b],
        axis=-1,
    )


def norm_fwd(values, gain_vec, shift_vec):
    row_mean = jnp.mean(values, -1, keepdims=True)
    centered = values - row_mean
    inv_std = lax.rsqrt(jnp.mean(centered * centered, -1, keepdims=True) + 1e-06)
    normalized = centered * inv_std
    return (normalized * gain_vec + shift_vec, normalized, inv_std)


def norm_back(upstream, normalized, inv_std, gain_vec):
    scaled = upstream * gain_vec
    inner = (
        scaled
        - jnp.mean(scaled, -1, keepdims=True)
        - normalized * jnp.mean(scaled * normalized, -1, keepdims=True)
    )
    return (inv_std * inner, jnp.sum(upstream * normalized, 0), jnp.sum(upstream, 0))


def outer_sum(left, right):
    return lax.dot_general(
        left, right, (((0,), (0,)), ((), ())), preferred_element_type=jnp.float32
    )


def times_transposed(left, right):
    return lax.dot_general(
        left, right, (((1,), (1,)), ((), ())), preferred_element_type=jnp.float32
    )


def add_rows(buffer, block, first_key):
    current = lax.dynamic_slice_in_dim(buffer, first_key, block.shape[0], 0)
    return lax.dynamic_update_slice_in_dim(buffer, current + block, first_key, 0)


def in_blocks(block_step, running, pieces):
    row_count = pieces[0].shape[0]
    block_rows = math.gcd(row_count, 2048)

    def advance(block_idx, state):
        first_row = block_idx * block_rows
        sliced = tuple(
            (lax.dynamic_slice_in_dim(piece, first_row, block_rows, 0) for piece in pieces)
        )
        return block_step(state, sliced, first_row)

    return lax.fori_loop(0, row_count // block_rows, advance, running)


def shards(
    tokens_in,
    clip_lengths,
    attn_gain,
    attn_shift,
    qkv_weight,
    qkv_bias,
    proj_weight,
    proj_bias,
    mlp_gain,
    mlp_shift,
    up_weight,
    up_bias,
    down_weight,
    down_bias,
    out_cotangent,
):
    tok_rows = tokens_in.shape[1]
    model_width = tokens_in.shape[2]
    seq_len = tok_rows * lax.axis_size("blk")
    lens_row = clip_lengths[0]
    own_pos = lax.axis_index("blk") * tok_rows + jnp.arange(tok_rows, dtype=jnp.int32)
    clip_q, cos_tab, sin_tab = clip_layout(lens_row, own_pos)
    residual = tokens_in[0].astype(jnp.float32)
    attn_gain_f = attn_gain.astype(jnp.float32)
    mlp_gain_f = mlp_gain.astype(jnp.float32)
    normed, hat_one, inv_one = norm_fwd(residual, attn_gain_f, attn_shift.astype(jnp.float32))
    normed_low = normed.astype(jnp.bfloat16)
    qkv_mixed = jnp.dot(
        normed_low, qkv_weight, preferred_element_type=jnp.float32
    ) + qkv_bias.astype(jnp.float32)
    query_h = rotate(qkv_mixed[:, :model_width].reshape(tok_rows, H, HD), cos_tab, sin_tab).astype(
        jnp.bfloat16
    )
    key_low = (
        rotate(
            qkv_mixed[:, model_width : 2 * model_width].reshape(tok_rows, H, HD), cos_tab, sin_tab
        )
        .astype(jnp.bfloat16)
        .reshape(tok_rows, model_width)
    )
    value_low = qkv_mixed[:, 2 * model_width :].astype(jnp.bfloat16)

    def block_scores(keys_blk, first_key):
        key_count = keys_blk.shape[0]
        clip_k = clip_of(lens_row, first_key + jnp.arange(key_count, dtype=jnp.int32))
        raw_scores = jnp.einsum(
            "qhd,khd->hqk",
            query_h,
            keys_blk.reshape(key_count, H, HD),
            preferred_element_type=jnp.float32,
        )
        allowed = (clip_q[:, None] == clip_k[None, :])[None]
        return (jnp.where(allowed, 0.125 * raw_scores, NEG_FILL), allowed)

    def stats_step(state, sliced, first_key):
        row_max, row_sum = state
        scores, allowed = block_scores(sliced[0], first_key)
        new_max = jnp.maximum(row_max, jnp.max(scores, -1))
        weights = jnp.where(allowed, jnp.exp(scores - new_max[:, :, None]), 0.0)
        return (new_max, row_sum * jnp.exp(row_max - new_max) + jnp.sum(weights, -1))

    stats_init = (
        jnp.full((H, tok_rows), NEG_FILL, jnp.float32),
        jnp.zeros((H, tok_rows), jnp.float32),
    )
    row_max, row_sum = in_blocks(
        stats_step, stats_init, (lax.all_gather(key_low, "blk", axis=0, tiled=True),)
    )
    log_sum = row_max + jnp.log(row_sum)

    def output_step(acc_state, sliced, first_key):
        keys_blk, values_blk = sliced
        key_count = keys_blk.shape[0]
        scores, allowed = block_scores(keys_blk, first_key)
        weights = jnp.where(allowed, jnp.exp(scores - log_sum[:, :, None]), 0.0)
        return acc_state + jnp.einsum(
            "hqk,khd->qhd",
            weights.astype(jnp.bfloat16),
            values_blk.reshape(key_count, H, HD),
            preferred_element_type=jnp.float32,
        )

    acc_init = jnp.zeros((tok_rows, H, HD), jnp.float32)
    attended_f = in_blocks(
        output_step,
        acc_init,
        (
            lax.all_gather(key_low, "blk", axis=0, tiled=True),
            lax.all_gather(value_low, "blk", axis=0, tiled=True),
        ),
    )
    attended_low = attended_f.reshape(tok_rows, model_width).astype(jnp.bfloat16)
    middle = (
        residual
        + jnp.dot(attended_low, proj_weight, preferred_element_type=jnp.float32)
        + proj_bias.astype(jnp.float32)
    )
    normed_two, hat_two, inv_two = norm_fwd(middle, mlp_gain_f, mlp_shift.astype(jnp.float32))
    normed_two_low = normed_two.astype(jnp.bfloat16)
    hidden = jnp.dot(
        normed_two_low, up_weight, preferred_element_type=jnp.float32
    ) + up_bias.astype(jnp.float32)
    active_low = jax.nn.gelu(hidden).astype(jnp.bfloat16)
    result = (
        middle
        + jnp.dot(active_low, down_weight, preferred_element_type=jnp.float32)
        + down_bias.astype(jnp.float32)
    )
    layer_out = result.astype(jnp.bfloat16)[None]
    cot_low = out_cotangent[0]
    cot_f = cot_low.astype(jnp.float32)
    grad_down_w = outer_sum(active_low, cot_low)
    grad_down_b = jnp.sum(cot_f, 0)
    d_active = times_transposed(cot_low, down_weight)
    hidden_unused, gelu_back = jax.vjp(jax.nn.gelu, hidden)
    d_hidden = gelu_back(d_active)[0].astype(jnp.bfloat16)
    grad_up_w = outer_sum(normed_two_low, d_hidden)
    grad_up_b = jnp.sum(d_hidden.astype(jnp.float32), 0)
    d_normed_two = times_transposed(d_hidden, up_weight)
    d_mid_norm, grad_mlp_gain, grad_mlp_shift = norm_back(
        d_normed_two, hat_two, inv_two, mlp_gain_f
    )
    d_middle = cot_f + d_mid_norm
    d_branch = d_middle.astype(jnp.bfloat16)
    grad_proj_w = outer_sum(attended_low, d_branch)
    grad_proj_b = jnp.sum(d_branch.astype(jnp.float32), 0)
    d_attended = (
        times_transposed(d_branch, proj_weight).astype(jnp.bfloat16).reshape(tok_rows, H, HD)
    )
    delta = jnp.einsum("qhd,qhd->hq", d_attended.astype(jnp.float32), attended_f)

    def back_step(state, sliced, first_key):
        dq_acc, buffers = state
        keys_blk, values_blk = sliced
        key_count = keys_blk.shape[0]
        scores, allowed = block_scores(keys_blk, first_key)
        weights = jnp.where(allowed, jnp.exp(scores - log_sum[:, :, None]), 0.0)
        d_weights = jnp.einsum(
            "qhd,khd->hqk",
            d_attended,
            values_blk.reshape(key_count, H, HD),
            preferred_element_type=jnp.float32,
        )
        d_scores = (weights * (d_weights - delta[:, :, None])).astype(jnp.bfloat16)
        dq_acc = dq_acc + 0.125 * jnp.einsum(
            "hqk,khd->qhd",
            d_scores,
            keys_blk.reshape(key_count, H, HD),
            preferred_element_type=jnp.float32,
        )
        d_keys = 0.125 * jnp.einsum(
            "hqk,qhd->khd", d_scores, query_h, preferred_element_type=jnp.float32
        )
        d_values = jnp.einsum(
            "hqk,qhd->khd",
            weights.astype(jnp.bfloat16),
            d_attended,
            preferred_element_type=jnp.float32,
        )
        key_buffer = add_rows(buffers[0], d_keys.reshape(key_count, model_width), first_key)
        value_buffer = add_rows(buffers[1], d_values.reshape(key_count, model_width), first_key)
        buffers = (key_buffer, value_buffer)
        return (dq_acc, buffers)

    buffer_init = (
        jnp.zeros((seq_len, model_width), jnp.float32),
        jnp.zeros((seq_len, model_width), jnp.float32),
    )
    back_init = (jnp.zeros((tok_rows, H, HD), jnp.float32), buffer_init)
    d_queries, key_grads = in_blocks(
        back_step,
        back_init,
        (
            lax.all_gather(key_low, "blk", axis=0, tiled=True),
            lax.all_gather(value_low, "blk", axis=0, tiled=True),
        ),
    )
    d_keys_own, d_values_own = (
        lax.psum_scatter(key_grads[0], "blk", scatter_dimension=0, tiled=True),
        lax.psum_scatter(key_grads[1], "blk", scatter_dimension=0, tiled=True),
    )
    d_queries_pre = rotate(d_queries, cos_tab, -sin_tab).reshape(tok_rows, model_width)
    d_keys_pre = rotate(d_keys_own.reshape(tok_rows, H, HD), cos_tab, -sin_tab).reshape(
        tok_rows, model_width
    )
    d_mixed = jnp.concatenate([d_queries_pre, d_keys_pre, d_values_own], axis=1).astype(
        jnp.bfloat16
    )
    grad_qkv_w = outer_sum(normed_low, d_mixed)
    grad_qkv_b = jnp.sum(d_mixed.astype(jnp.float32), 0)
    d_normed = times_transposed(d_mixed, qkv_weight)
    d_res_norm, grad_attn_gain, grad_attn_shift = norm_back(d_normed, hat_one, inv_one, attn_gain_f)
    tokens_grad = (d_middle + d_res_norm)[None]
    summed = (
        lax.psum_scatter(grad_qkv_w, ("batch", "blk"), scatter_dimension=0, tiled=True),
        lax.psum_scatter(grad_proj_w, ("batch", "blk"), scatter_dimension=0, tiled=True),
        lax.psum_scatter(grad_up_w, ("batch", "blk"), scatter_dimension=0, tiled=True),
        lax.psum_scatter(grad_down_w, ("batch", "blk"), scatter_dimension=0, tiled=True),
        lax.psum_scatter(grad_attn_gain, ("batch", "blk"), scatter_dimension=0, tiled=True),
        lax.psum_scatter(grad_attn_shift, ("batch", "blk"), scatter_dimension=0, tiled=True),
        lax.psum_scatter(grad_qkv_b, ("batch", "blk"), scatter_dimension=0, tiled=True),
        lax.psum_scatter(grad_proj_b, ("batch", "blk"), scatter_dimension=0, tiled=True),
        lax.psum_scatter(grad_mlp_gain, ("batch", "blk"), scatter_dimension=0, tiled=True),
        lax.psum_scatter(grad_mlp_shift, ("batch", "blk"), scatter_dimension=0, tiled=True),
        lax.psum_scatter(grad_up_b, ("batch", "blk"), scatter_dimension=0, tiled=True),
        lax.psum_scatter(grad_down_b, ("batch", "blk"), scatter_dimension=0, tiled=True),
    )
    return (
        layer_out,
        tokens_grad,
        summed[4],
        summed[5],
        summed[0],
        summed[6],
        summed[1],
        summed[7],
        summed[8],
        summed[9],
        summed[2],
        summed[10],
        summed[3],
        summed[11],
    )


BF = jnp.bfloat16
F32 = jnp.float32
AXES = ("x", "core", "zh", "zl", "y")
ROW = ("zh", "zl", "y")
GELU_A = 0.7978845608028654
GELU_B = 0.044715
VMEM_MIB = 56
COST = 1e3


def mm(left, right):
    return jnp.dot(left, right, preferred_element_type=F32)


def swap_over(value, *names):
    mask = sum(16 >> AXES.index(name) for name in names)
    return lax.ppermute(value, AXES, [(i, i ^ mask) for i in range(32)])


def whole(shape):
    zeros = (0,) * len(shape)
    return pl.BlockSpec(shape, lambda *_: zeros)


def arr(shape, dtype):
    return jax.ShapeDtypeStruct(shape, dtype)


def call(body, grid, in_specs, out_specs, out_shape, scratch, micros, scalars, args):
    nbytes = int(micros * COST)
    return pl.pallas_call(
        body,
        grid_spec=pltpu.PrefetchScalarGridSpec(
            num_scalar_prefetch=1,
            grid=grid,
            in_specs=in_specs,
            out_specs=out_specs,
            scratch_shapes=scratch,
        ),
        out_shape=out_shape,
        compiler_params=pltpu.CompilerParams(vmem_limit_bytes=VMEM_MIB << 20),
        cost_estimate=pl.CostEstimate(flops=0, bytes_accessed=nbytes, transcendentals=0),
    )(scalars, *args)


def one_step(body, outs, scratch, micros, scalars, args):
    return call(
        body, (1,), [whole(v.shape) for v in args], [whole(o.shape) for o in outs], outs, scratch,
        micros, scalars, args,
    )


def standardize(x):
    mean = jnp.mean(x, -1, keepdims=True)
    centered = x - mean
    inv = lax.rsqrt(jnp.mean(centered * centered, -1, keepdims=True) + 1e-06)
    return centered * inv, inv


def swap_halves(x):
    lane = lax.broadcasted_iota(jnp.int32, x.shape, 1)
    return jnp.where(lane % 64 < 32, pltpu.roll(x, 96, 1), pltpu.roll(x, 32, 1))


def gelu_both(h):
    t = jnp.tanh(h * (GELU_A + (GELU_A * GELU_B) * (h * h)))
    half = 0.5 * h
    act = half + half * t
    slope = (0.5 + 0.5 * t) + half * (1.0 - t * t) * (GELU_A + (3.0 * GELU_A * GELU_B) * (h * h))
    return act, slope


def down_back_body(place, cot, down, d_act, bias_part):
    @pl.when(pl.program_id(0) == 0)
    def _():
        bias_part[...] = jnp.sum(cot[...].astype(F32), 0, keepdims=True)

    d_act[...] = times_transposed(cot[...], down[...])


def qkv_half(place, blocks, vecs, ws, cos, sin, hat_out, normed):
    g = vecs[0:1, :]
    s = vecs[1:2, :]
    for j in range(4):
        rows = slice(128 * j, 128 * j + 128)
        hat, _ = standardize(blocks[j][...].astype(F32))
        hat_out[rows, :] = hat.astype(BF)
        normed[rows, :] = (hat * g + s).astype(BF)
    lanes = pl.ds(pl.multiple_of(place[0] * 128, 128), 128)
    bias3 = jnp.concatenate([vecs[12 + p : 13 + p, lanes] for p in range(3)], 1)
    mixed = mm(normed[...], jnp.concatenate([w[...] for w in ws], 1)) + bias3
    c = cos[...]
    sn = sin[...]
    q = mixed[:, :128]
    k = mixed[:, 128:256]
    return (
        ((q * c + swap_halves(q) * sn) * 0.125).astype(BF),
        (k * c + swap_halves(k) * sn).astype(BF),
        mixed[:, 256:].astype(BF),
    )


def near_body(place, *refs):
    blocks = refs[:4]
    vecs, wq, wk, wv, cos, sin, hat_out, q_out, k_out, v_out, normed = refs[4:]
    q, k, v = qkv_half(place, blocks, vecs, (wq, wk, wv), cos, sin, hat_out, normed)
    q_out[...] = q
    k_out[...] = k
    v_out[...] = v


def far_body(place, *refs):
    blocks = refs[:4]
    vecs, wq, wk, wv, cos, sin, q0, k0, v0, hat_out, q_out, k_out, v_out, normed = refs[4:]
    q, k, v = qkv_half(place, blocks, vecs, (wq, wk, wv), cos, sin, hat_out, normed)
    for out, near, far in ((q_out, q0, q), (k_out, k0, k), (v_out, v0, v)):
        out[:512, :] = near[...]
        out[512:, :] = far


def head_mask(shape, head):
    return lax.broadcasted_iota(jnp.int32, shape, 1) // 64 == head


def attend_body(place, q, k_all, v_all, id_col, id_row, att_f, att_low, probs):
    keys = k_all[...]
    values = v_all[...]
    queries = q[...]
    own = id_col[...]
    allowed = jnp.concatenate([own, own], 1) == id_row[0:1, :]
    halves = []
    for head in range(2):
        mine = jnp.where(head_mask(queries.shape, head), queries, jnp.zeros_like(queries))
        scores = jnp.where(allowed, times_transposed(keys, mine), NEG_FILL)
        weights = jnp.exp(scores - jnp.max(scores, 0, keepdims=True))
        low = (weights * (1.0 / jnp.sum(weights, 0, keepdims=True))).astype(BF)
        probs[head] = low
        halves.append(outer_sum(values, low)[64 * head : 64 * head + 64])
    out = jnp.concatenate(halves, 0).T
    att_f[...] = out
    step = pl.program_id(0)
    att_low[place[0] ^ (2 * step)] = out[:128].astype(BF)
    att_low[place[0] ^ (2 * step + 1)] = out[128:].astype(BF)


def proj_body(place, att, tok, proj_w, vecs, middle, normed, att_rows):
    rows = jnp.concatenate([att[k] for k in range(8)], 1)
    att_rows[...] = rows
    mid = tok[...].astype(F32) + mm(rows, proj_w[...]) + vecs[2:3, :]
    middle[...] = mid
    hat, _ = standardize(mid)
    low = (hat * vecs[3:4, :] + vecs[4:5, :]).astype(BF)
    normed[...] = low


def proj_grad(place, att, d_b, vectors, send, keep):
    grad = outer_sum(att, d_b)
    row = lax.broadcasted_iota(jnp.int32, (32, 128), 0)
    rel_y = place[0] & 1
    rel_zl = (place[0] >> 1) & 1
    rel_zh = place[0] >> 2
    for owner in range(32):
        x, core, k = owner // 16, (owner // 8) % 2, owner % 8
        rows = grad[32 * owner : 32 * owner + 32]
        extra = jnp.zeros((32, 128), F32)
        first = 128 * (owner // 4)
        for m in range(4):
            extra = jnp.where(row == m, vectors[m : m + 1, first : first + 128], extra)
        group = 2 * x + core
        last = vectors[4 + group : 5 + group, 128 * k : 128 * k + 128]
        extra = jnp.where(row == 4, last, extra)
        slot = ((rel_y ^ (k & 1)) * 8 + (rel_zl ^ ((k >> 1) & 1)) * 4) + (
            (place[1] ^ x) * 2 + (rel_zh ^ (k >> 2))
        )

        @pl.when(core == place[2])
        def _():
            keep[slot, :, :1024] = rows
            keep[slot, :, 1024:] = extra

        @pl.when(core != place[2])
        def _():
            send[slot, :, :1024] = rows.astype(BF)
            send[slot, :, 1024:] = extra.astype(BF)


def mlp_body(
    place, normed, d_act, up_w, vecs, middle, cot, proj_w, down_bias, att,
    active, d_mid, d_att, proj_send, proj_keep, acc, vectors,
):
    step = pl.program_id(0)
    hidden = mm(normed[...], up_w[...]) + vecs[pl.ds(8 + step, 1), :]
    act, slope = gelu_both(hidden)
    active[...] = act.astype(BF)
    d_hidden = (d_act[...] * slope).astype(BF)
    vectors[pl.ds(4 + step, 1), :] = jnp.sum(d_hidden.astype(F32), 0, keepdims=True)
    part = times_transposed(d_hidden, up_w[...])

    @pl.when(step == 0)
    def _():
        acc[...] = part

    @pl.when(step > 0)
    def _():
        acc[...] += part

    @pl.when(step == pl.num_programs(0) - 1)
    def _():
        up = acc[...]
        hat, inv = standardize(middle[...])
        e = up * vecs[3:4, :]
        inner = e - jnp.mean(e, -1, keepdims=True) - hat * jnp.mean(e * hat, -1, keepdims=True)
        d_m = cot[...].astype(F32) + inv * inner
        d_mid[...] = d_m
        d_b = d_m.astype(BF)
        vectors[0:1, :] = jnp.sum(up * hat, 0, keepdims=True)
        vectors[1:2, :] = jnp.sum(up, 0, keepdims=True)
        vectors[2:3, :] = jnp.sum(d_b.astype(F32), 0, keepdims=True)
        vectors[3:4, :] = down_bias[...]
        d_a = times_transposed(d_b, proj_w[...]).astype(BF)
        for k in range(8):
            d_att[k] = d_a[:, 128 * k : 128 * k + 128]
        proj_grad(place, att[...], d_b, vectors, proj_send, proj_keep)


def mlp_grad_body(place, *refs):
    blocks, cots, ups, downs = refs[:8], refs[8:16], refs[16:20], refs[20:24]
    vecs, down_keep, down_send, up_keep, up_send, n_all, c_all, u_all, d_all, grad = refs[24:]
    for j in range(8):
        n_all[128 * j : 128 * j + 128, :] = blocks[j][...]
        c_all[128 * j : 128 * j + 128, :] = cots[j][...]
    lanes = pl.ds(pl.multiple_of(place[0] * 128, 128), 128)
    up_b = []
    rows = vecs[8:12, lanes]
    biases = lax.broadcasted_iota(jnp.int32, (4, 128), 0)
    for g in range(4):
        u_all[:, 128 * g : 128 * g + 128] = ups[g][...]
        d_all[128 * g : 128 * g + 128, :] = downs[g][...]
        group = (place[1] ^ (g & 1)) * 2 + (place[2] ^ (g >> 1))
        up_b.append(jnp.sum(jnp.where(biases == group, rows, 0.0), 0, keepdims=True))
    n = n_all[...]
    c = c_all[...]
    act, slope = gelu_both(mm(n, u_all[...]) + jnp.concatenate(up_b, 1))
    grad_down = outer_sum(act.astype(BF), c)
    for g in range(4):
        rows = grad_down[128 * g : 128 * g + 128]
        if g < 2:
            down_keep[g] = rows
        else:
            down_send[g - 2] = rows.astype(BF)
    d_hidden = (times_transposed(c, d_all[...]) * slope).astype(BF)
    both = outer_sum(n, d_hidden)
    for g in range(4):
        group = ((place[1] ^ (g & 1)) * 2) + (place[2] ^ (g >> 1))
        lanes = pl.ds(pl.multiple_of(group * 128, 128), 128)
        grad[:, lanes] = both[:, 128 * g : 128 * g + 128]
    for rx in range(2):
        first = (place[1] ^ rx) * 512
        keep = pl.multiple_of(first + place[2] * 256, 256)
        send = pl.multiple_of(first + (1 - place[2]) * 256, 256)
        up_keep[rx] = grad[pl.ds(keep, 256), :]
        up_send[rx] = grad[pl.ds(send, 256), :].astype(BF)


def attend_back_body(
    place, probs, d_att, att_f, q, k_all, v_all, cos, sin, d_all, bias_part, dq, dk, dv
):
    step = pl.program_id(0)
    keys = k_all[...]
    values = v_all[...]
    queries = q[...]
    d_out = jnp.concatenate([d_att[place[0] ^ (2 * step)], d_att[place[0] ^ (2 * step + 1)]], 0)
    products = (d_out.astype(F32) * att_f[...]).T
    key_parts, value_parts, query_parts = [], [], []
    for head in range(2):
        weights = probs[head]
        mine = jnp.where(head_mask(d_out.shape, head), d_out, jnp.zeros_like(d_out))
        delta = jnp.sum(products[64 * head : 64 * head + 64], 0, keepdims=True)
        d_weights = times_transposed(values, mine)
        d_scores = (weights.astype(F32) * (d_weights - delta)).astype(BF)
        key_parts.append(mm(d_scores, queries))
        value_parts.append(mm(weights, d_out))
        query_parts.append(outer_sum(keys, d_scores)[64 * head : 64 * head + 64])
    first = head_mask((1024, 128), 0)
    dk_new = jnp.where(first, key_parts[0], key_parts[1])
    dv_new = jnp.where(first, value_parts[0], value_parts[1])
    dq[pl.ds(pl.multiple_of(step * 256, 256), 256), :] = jnp.concatenate(query_parts, 0).T

    @pl.when(step == 0)
    def _():
        dk[...] = dk_new
        dv[...] = dv_new

    @pl.when(step > 0)
    def _():
        dk[...] += dk_new
        dv[...] += dv_new

    @pl.when(step == pl.num_programs(0) - 1)
    def _():
        total = jnp.zeros((1, 384), F32)
        for j in range(8):
            rows = slice(128 * j, 128 * j + 128)
            c = cos[rows, :]
            sn = sin[rows, :]
            back_q = 0.125 * dq[rows, :]
            back_k = dk[rows, :]
            piece = jnp.concatenate(
                [
                    back_q * c - swap_halves(back_q) * sn,
                    back_k * c - swap_halves(back_k) * sn,
                    dv[rows, :],
                ],
                1,
            ).astype(BF)
            d_all[place[0] ^ j] = piece
            total = total + jnp.sum(piece.astype(F32), 0, keepdims=True)
        bias_part[...] = total


def rel_block(step, place):
    rel = jnp.where(step < 2, 2, 0) + step % 2
    return ((rel & 1) ^ place[1]) * 2 + ((rel >> 1) ^ place[2])


def qkv_grad_body(place, h0, h1, d_all, bias_part, columns, wq, wk, wv, send, keep):
    step = pl.program_id(0)
    d_near = jnp.concatenate([d_all[place[0] ^ j] for j in range(4)], 0)
    d_far = jnp.concatenate([d_all[place[0] ^ j] for j in range(4, 8)], 0)
    inner = outer_sum(h0[...], d_near) + outer_sum(h1[...], d_far)
    total = bias_part[...]
    w = jnp.concatenate([wq[...], wk[...], wv[...]], 1).astype(F32)
    gain = columns[:, 0:1]
    shift = columns[:, 1:2]
    grad = gain * inner + shift * total
    row = lax.broadcasted_iota(jnp.int32, (256, 128), 0) % 32
    lane = lax.broadcasted_iota(jnp.int32, (256, 128), 1)
    extra = jnp.where(
        lane == 0,
        jnp.sum(w * inner, 1, keepdims=True),
        jnp.where(lane == 1, jnp.sum(w * total, 1, keepdims=True), 0.0),
    )
    for m in range(6):
        part = total[:, 128 * (m // 2) : 128 * (m // 2) + 128]
        part = part if m % 2 else pltpu.roll(part, 64, 1)
        extra = jnp.where((row == m) & (lane >= 64), part, extra)

    @pl.when(step < 2)
    def _():
        send[0, :, :384] = grad.astype(BF)
        send[0, :, 384:] = extra.astype(BF)

    @pl.when(step >= 2)
    def _():
        keep[0, :, :384] = grad
        keep[0, :, 384:] = extra


def finish_body(place, came, grad_up, grad_qkv, sums, bias):
    total = jnp.zeros((32, 128), F32)
    for k in range(8):
        for g in range(4):
            lanes = slice(1024 * g + 128 * k, 1024 * g + 128 * k + 128)
            grad_up[:, lanes] = came[k, :32, 128 * g : 128 * g + 128].astype(F32)
            if g < 3:
                grad_qkv[:, lanes] = came[k, 32:, 128 * g : 128 * g + 128].astype(F32)
        extra = came[k, 32:, 384:].astype(F32)
        total = total + extra
        bias[6 * k : 6 * k + 6, :] = extra[:6]
    sums[...] = total


def last_body(place, came, w, tok, d_mid, vecs, out, acc):
    step = pl.program_id(0)
    for p in range(3):

        @pl.when(step == p)
        def _():
            d_mixed = jnp.concatenate([came[k, :, 128 * p : 128 * p + 128] for k in range(8)], 1)
            part = times_transposed(d_mixed, w[...])
            if p == 0:
                acc[...] = part
            elif p == 1:
                acc[...] += part
            else:
                up = acc[...] + part
                hat, inv = standardize(tok[...].astype(F32))
                e = up * vecs[0:1, :]
                mean = jnp.mean(e, -1, keepdims=True)
                inner = e - mean - hat * jnp.mean(e * hat, -1, keepdims=True)
                out[...] = d_mid[...] + inv * inner


def frequency_rows():
    rows = np.zeros((8, 128), np.float32)
    for lane in range(128):
        pair = lane % 32
        part, rank, count = (0, pair, 10) if pair < 10 else ((1, pair - 10, 11) if pair < 21 else (2, pair - 21, 11))
        rows[part, lane] = 10000.0 ** (-rank / count)
        rows[3, lane] = -1.0 if lane % 64 < 32 else 1.0
    return rows


def clip_starts(place, pos):
    ids = jnp.zeros_like(pos)
    start = jnp.zeros_like(pos)
    end = jnp.int32(0)
    for c in range(8):
        length = place[8 + c]
        end = end + length
        past = pos >= end.astype(F32)
        ids = jnp.where(past, ids + 1.0, ids)
        start = jnp.where(past, end.astype(F32), start)
    return ids, start


def prep_body(place, freq, vecs, cos, sin, id_col, id_row, columns):
    for j in range(8):
        first = ((place[0] ^ j) * 128).astype(F32)
        rows = slice(128 * j, 128 * j + 128)
        pos = first + lax.broadcasted_iota(jnp.int32, (128, 128), 0).astype(F32)
        ids, start = clip_starts(place, pos)
        id_col[rows, :] = ids
        within = pos - start
        row14 = jnp.floor((within + 0.5) * (1.0 / 14.0))
        t = jnp.floor((within + 0.5) * (1.0 / 196.0))
        angle = t * freq[0:1, :] + (row14 - 14.0 * t) * freq[1:2, :] + (within - 14.0 * row14) * freq[2:3, :]
        cos[rows, :] = jnp.cos(angle)
        sin[rows, :] = jnp.sin(angle) * freq[3:4, :]
        flat = first + lax.broadcasted_iota(jnp.int32, (8, 128), 1).astype(F32)
        id_row[:, 128 * j : 128 * j + 128] = clip_starts(place, flat)[0]
    columns[...] = vecs[0:8, :].T


def after(value, *others):
    return lax.optimization_barrier((value, *others))[0]


def spread_four(a):
    return [a, swap_over(a, "y"), swap_over(a, "zl"), swap_over(a, "zl", "y")]


def fast_shards(
    tokens_in, clip_lengths, attn_gain, attn_shift, qkv_weight, qkv_bias, proj_weight, proj_bias,
    mlp_gain, mlp_shift, up_weight, up_bias, down_weight, down_bias, out_cotangent,
):
    x, core, zh, zl, y = (lax.axis_index(name) for name in AXES)
    k = zh * 4 + zl * 2 + y
    me = x * 16 + core * 8 + k
    place = jnp.concatenate(
        [jnp.stack([k, x, core, k, k, k, k, k]).astype(jnp.int32), clip_lengths[0]]
    )
    tok = tokens_in[0]
    cot = out_cotangent[0]

    far_tok = swap_over(tok, "zh")
    near = spread_four(tok)
    rows = [attn_gain, attn_shift, proj_bias, mlp_gain, mlp_shift, down_bias, down_bias, down_bias]
    vecs = jnp.concatenate([v.astype(F32).reshape(-1, 1024) for v in (*rows, up_bias, qkv_bias)], 0)
    cos_tab, sin_tab, id_col, id_row, columns = one_step(
        prep_body,
        [arr((1024, 128), F32), arr((1024, 128), F32), arr((1024, 128), F32), arr((8, 1024), F32),
         arr((1024, 8), F32)],
        [],
        3,
        place,
        (jnp.asarray(frequency_rows()), vecs),
    )
    far_tok, cos_tab, *near = lax.optimization_barrier((far_tok, cos_tab, *near))
    far = spread_four(far_tok)
    cot_here, *_ = lax.optimization_barrier((cot, far_tok))
    far_cot = swap_over(cot_here, "zh")
    cots = spread_four(cot_here)

    def table_half(part):
        return pl.BlockSpec((512, 128), lambda i, s: (part, 0))

    half = arr((512, 128), BF)
    full = arr((1024, 128), BF)
    common = (vecs, qkv_weight, qkv_weight, qkv_weight, cos_tab, sin_tab)
    columns_of = [pl.BlockSpec((1024, 128), lambda i, s, p=p: (0, 8 * p + s[0])) for p in range(3)]

    def qkv(body, part, blocks, more, outs):
        specs = [whole(v.shape) for v in (*blocks, vecs)] + columns_of
        specs += [table_half(part), table_half(part)] + [whole(v.shape) for v in more]
        return call(
            body, (1,), specs, [whole(o.shape) for o in outs], outs,
            [pltpu.VMEM((512, 1024), BF)], 2, place, (*blocks, *common, *more),
        )

    hat0, q0, k0, v0 = qkv(near_body, 0, near, (), [arr((512, 1024), BF), half, half, half])
    far = lax.optimization_barrier((q0, *far))[1:]
    hat1, q_all, k_all, v_all = qkv(
        far_body, 1, far, (q0, k0, v0), [arr((512, 1024), BF), full, full, full]
    )
    step_rows = pl.BlockSpec((256, 128), lambda i, s: (i, 0))
    flat = whole((1024, 128))
    att_f, att_low, probs = call(
        attend_body,
        (4,),
        [
            step_rows, flat, flat, flat, pl.BlockSpec((8, 256), lambda i, s: (0, i)),
        ],
        [step_rows, whole((8, 128, 128)), pl.BlockSpec((2, 1024, 256), lambda i, s: (0, 0, i))],
        [arr((1024, 128), F32), arr((8, 128, 128), BF), arr((2, 1024, 1024), BF)],
        [],
        6,
        place,
        (q_all, k_all, v_all, id_col, id_row),
    )
    att_low, far_cot, *cots = lax.optimization_barrier((att_low, far_cot, *cots))
    att_in = lax.all_to_all(att_low, ROW, 0, 0, tiled=True)
    cots = cots + spread_four(far_cot)
    d_act, down_bias_part = call(
        down_back_body,
        (4,),
        [whole((128, 1024)), pl.BlockSpec((1024, 1024), lambda i, s: (i, 0))],
        [pl.BlockSpec((128, 1024), lambda i, s: (0, i)), whole((1, 1024))],
        [arr((128, 4096), F32), arr((1, 1024), F32)],
        [],
        4,
        place,
        (after(cot, att_low), down_weight),
    )


    middle, normed2, att_rows = one_step(
        proj_body,
        [arr((128, 1024), F32), arr((128, 1024), BF), arr((128, 1024), BF)],
        [],
        2,
        place,
        (after(att_in, d_act), tok, proj_weight, vecs),
    )
    normed2, *cots = lax.optimization_barrier((normed2, *cots))
    far_n = swap_over(normed2, "zh")
    near_n = spread_four(normed2)
    wide = pl.BlockSpec((128, 1024), lambda i, s: (0, i))
    fixed = whole((128, 1024))
    active, d_mid, d_att, proj_send, proj_keep = call(
        mlp_body,
        (4,),
        [
            fixed, wide, wide_columns(), whole((15, 1024)), fixed, fixed, whole((1024, 1024)),
            whole((1, 1024)), fixed,
        ],
        [wide, fixed, whole((8, 128, 128)), whole((16, 32, 1152)), whole((16, 32, 1152))],
        [
            arr((128, 4096), BF), arr((128, 1024), F32), arr((8, 128, 128), BF),
            arr((16, 32, 1152), BF), arr((16, 32, 1152), F32),
        ],
        [pltpu.VMEM((128, 1024), F32), pltpu.VMEM((8, 1024), F32)],
        8,
        place,
        (normed2, d_act, up_weight, vecs, middle, cot, proj_weight, down_bias_part, att_rows),
    )
    d_att, far_n, active, proj_send, *near_n = lax.optimization_barrier(
        (d_att, far_n, active, proj_send, *near_n)
    )
    d_att_in = lax.all_to_all(d_att, ROW, 0, 0, tiled=True)

    result = middle + mm(active, down_weight) + down_bias.astype(F32)
    layer_out = result.astype(BF)[None]
    far_n = spread_four(after(far_n, layer_out))

    def core_sum(keep, send):
        return keep + swap_over(send, "core").astype(F32)

    def x_sum(keep):
        return keep[0] + swap_over(keep[1].astype(BF), "x").astype(F32)

    def half_sum(value, name):
        count = value.shape[0] // 2
        return value[:count] + swap_over(value[count:].astype(BF), name).astype(F32)

    d_all, qkv_bias_part = call(
        attend_back_body,
        (4,),
        [
            pl.BlockSpec((2, 1024, 256), lambda i, s: (0, 0, i)), whole((8, 128, 128)), step_rows,
            step_rows, flat, flat, flat, flat,
        ],
        [whole((8, 128, 384)), whole((1, 384))],
        [arr((8, 128, 384), BF), arr((1, 384), F32)],
        [pltpu.VMEM((1024, 128), F32)] * 3,
        6,
        place,
        (probs, after(d_att_in, layer_out), att_f, q_all, k_all, v_all, cos_tab, sin_tab),
    )
    d_all, *far_n = lax.optimization_barrier((d_all, *far_n))
    moved = lax.all_to_all(d_all, ROW, 0, 0, tiled=True)

    def group_of(s, g):
        return (s[1] ^ (g & 1)) * 16 + (s[2] ^ (g >> 1)) * 8 + s[0]

    outs = [
        arr((2, 128, 1024), F32), arr((2, 128, 1024), BF), arr((2, 256, 512), F32),
        arr((2, 256, 512), BF),
    ]
    down_keep, down_send, up_keep, up_send = call(
        mlp_grad_body,
        (1,),
        [fixed] * 16
        + [pl.BlockSpec((1024, 128), lambda i, s, g=g: (0, group_of(s, g))) for g in range(4)]
        + [pl.BlockSpec((128, 1024), lambda i, s, g=g: (group_of(s, g), 0)) for g in range(4)]
        + [whole((15, 1024))],
        [whole(o.shape) for o in outs],
        outs,
        [
            pltpu.VMEM((1024, 1024), BF), pltpu.VMEM((1024, 1024), BF),
            pltpu.VMEM((1024, 512), BF), pltpu.VMEM((512, 1024), BF), pltpu.VMEM((1024, 512), F32),
        ],
        8,
        place,
        (after(near_n[0], d_all), *near_n[1:], *far_n, *cots, *([up_weight] * 4), *([down_weight] * 4), vecs),
    )


    block_of = lambda i, s: (rel_block(i, s), 0)
    lanes_of = lambda i, s: (0, rel_block(i, s))
    send, keep = call(
        qkv_grad_body,
        (4,),
        [
            pl.BlockSpec((512, 256), lanes_of), pl.BlockSpec((512, 256), lanes_of),
            whole((8, 128, 384)), whole((1, 384)), pl.BlockSpec((256, 8), block_of),
        ]
        + [pl.BlockSpec((256, 128), lambda i, s, p=p: (rel_block(i, s), 8 * p + s[0])) for p in range(3)],
        [
            pl.BlockSpec((1, 256, 512), lambda i, s: (jnp.minimum(i, 1), 0, 0)),
            pl.BlockSpec((1, 256, 512), lambda i, s: (jnp.maximum(i - 2, 0), 0, 0)),
        ],
        [arr((2, 256, 512), BF), arr((2, 256, 512), F32)],
        [],
        4,
        place,
        (after(hat0, up_send), hat1, d_all, qkv_bias_part, columns, qkv_weight, qkv_weight, qkv_weight),
    )
    up_keep = core_sum(after(up_keep, moved), up_send)
    up_sum = x_sum(up_keep)
    keep = core_sum(after(keep, moved), send)
    qkv_sum = x_sum(keep)
    down_keep = core_sum(down_keep, down_send)
    grad_down = x_sum(after(down_keep, keep))
    proj_half = core_sum(after(proj_keep, up_send), proj_send)
    proj_half = half_sum(proj_half, "y")
    proj_half = half_sum(proj_half, "zl")
    proj_half = half_sum(proj_half, "x")

    def turn(value, *others):
        return lax.all_to_all(after(value, *others), ROW, 0, 0, tiled=True)

    lows = jnp.concatenate([v.astype(BF).reshape(8, 32, 512) for v in (up_sum, qkv_sum)], 1)
    came = turn(lows, moved)
    proj_total = half_sum(proj_half, "zh")[0]
    grad_proj = proj_total[:, :1024]
    own = lax.dynamic_slice(proj_total[:4, 1024:], (0, (me % 4) * 32), (4, 32))
    grad_up_b = proj_total[4, 1024:]

    grad_up, grad_qkv, sums, bias = one_step(
        finish_body,
        [arr((32, 4096), F32), arr((32, 3072), F32), arr((32, 128), F32), arr((48, 128), F32)],
        [],
        2,
        place,
        (came,),
    )
    bias = bias[:, 64:].reshape(8, 3, 128).transpose(1, 0, 2).reshape(3072)
    grad_qkv_b = lax.dynamic_slice(bias, (me * 96,), (96,))

    (tokens_grad,) = call(
        last_body,
        (3,),
        [
            whole((8, 128, 384)), pl.BlockSpec((1024, 1024), lambda i, s: (0, i)), fixed, fixed,
            whole((15, 1024)),
        ],
        [fixed],
        [arr((128, 1024), F32)],
        [pltpu.VMEM((128, 1024), F32)],
        5,
        place,
        (moved, qkv_weight, tok, d_mid, vecs),
    )

    return (
        layer_out, tokens_grad[None], sums[:, 0], sums[:, 1], grad_qkv, grad_qkv_b, grad_proj,
        own[2], own[0], own[1], grad_up, grad_up_b, grad_down, own[3],
    )


def wide_columns():
    return pl.BlockSpec((1024, 1024), lambda i, s: (0, i))


def fast_solution(mesh):
    wide_mesh = Mesh(mesh.devices.reshape(2, 2, 2, 2, 2), AXES)
    batch, blk = AXES[:2], AXES[2:]
    spread = P(batch, blk, None)
    return jax.shard_map(
        fast_shards,
        mesh=wide_mesh,
        in_specs=(spread, P(batch, None)) + (P(),) * 12 + (spread,),
        out_specs=(spread, spread)
        + tuple(P(AXES, None) if i in (2, 4, 8, 10) else P(AXES) for i in range(12)),
        check_vma=False,
    )


def solution(mesh):
    if tuple(mesh.devices.shape) == (4, 8):
        return fast_solution(mesh)
    placed = (
        P("batch", "blk", None),
        P("batch", None),
        P(),
        P(),
        P(),
        P(),
        P(),
        P(),
        P(),
        P(),
        P(),
        P(),
        P(),
        P(),
        P("batch", "blk", None),
    )
    return jax.shard_map(
        shards,
        mesh=mesh,
        in_specs=placed,
        out_specs=(
            P("batch", "blk", None),
            P("batch", "blk", None),
            P(("batch", "blk")),
            P(("batch", "blk")),
            P(("batch", "blk"), None),
            P(("batch", "blk")),
            P(("batch", "blk"), None),
            P(("batch", "blk")),
            P(("batch", "blk")),
            P(("batch", "blk")),
            P(("batch", "blk"), None),
            P(("batch", "blk")),
            P(("batch", "blk"), None),
            P(("batch", "blk")),
        ),
        check_vma=False,
    )
```

```python
import math

import jax
import jax.numpy as jnp
import numpy as np
from jax import lax
from jax.experimental import pallas as pl
from jax.experimental.pallas import tpu as pltpu
from jax.sharding import Mesh
from jax.sharding import PartitionSpec as P

H = 16
HD = 64


NEG_FILL = -1e30


def pair_table():
    part_map = [0] * 10 + [1] * 11 + [2] * 11
    freq_list = [10000.0 ** (-rank / 10.0) for rank in range(10)] + [
        10000.0 ** (-rank / 11.0) for rank in range(11)
    ] * 2
    table_rows = [
        [freq_list[column] if part_map[column] == axis_id else 0.0 for column in range(32)]
        for axis_id in range(3)
    ]
    return jnp.array(table_rows, dtype=jnp.float32)


def clip_of(lengths_row, positions):
    clip_end = jnp.cumsum(lengths_row)
    return jnp.sum((positions[:, None] >= clip_end[None, :]).astype(jnp.int32), axis=1)


def clip_layout(lengths_row, positions):
    clip_end = jnp.cumsum(lengths_row)
    starts = clip_end - lengths_row
    clip_ids = jnp.sum((positions[:, None] >= clip_end[None, :]).astype(jnp.int32), axis=1)
    member = clip_ids[:, None] == jnp.arange(lengths_row.shape[0], dtype=jnp.int32)[None, :]
    within = positions - jnp.sum(jnp.where(member, starts[None, :], 0), axis=1)
    coords = jnp.stack([within // 196, within // 14 % 14, within % 14], axis=1).astype(jnp.float32)
    angles = jnp.dot(coords, pair_table(), precision=lax.Precision.HIGHEST)
    return (clip_ids, jnp.cos(angles), jnp.sin(angles))


def rotate(values, cos_tab, sin_tab):
    half_dim = values.shape[-1] // 2
    first_half = values[..., :half_dim]
    second_half = values[..., half_dim:]
    cos_b = cos_tab[:, None, :]
    sin_b = sin_tab[:, None, :]
    return jnp.concatenate(
        [first_half * cos_b - second_half * sin_b, first_half * sin_b + second_half * cos_b],
        axis=-1,
    )


def norm_fwd(values, gain_vec, shift_vec):
    row_mean = jnp.mean(values, -1, keepdims=True)
    centered = values - row_mean
    inv_std = lax.rsqrt(jnp.mean(centered * centered, -1, keepdims=True) + 1e-06)
    normalized = centered * inv_std
    return (normalized * gain_vec + shift_vec, normalized, inv_std)


def norm_back(upstream, normalized, inv_std, gain_vec):
    scaled = upstream * gain_vec
    inner = (
        scaled
        - jnp.mean(scaled, -1, keepdims=True)
        - normalized * jnp.mean(scaled * normalized, -1, keepdims=True)
    )
    return (inv_std * inner, jnp.sum(upstream * normalized, 0), jnp.sum(upstream, 0))


def outer_sum(left, right):
    return lax.dot_general(
        left, right, (((0,), (0,)), ((), ())), preferred_element_type=jnp.float32
    )


def times_transposed(left, right):
    return lax.dot_general(
        left, right, (((1,), (1,)), ((), ())), preferred_element_type=jnp.float32
    )


def add_rows(buffer, block, first_key):
    current = lax.dynamic_slice_in_dim(buffer, first_key, block.shape[0], 0)
    return lax.dynamic_update_slice_in_dim(buffer, current + block, first_key, 0)


def in_blocks(block_step, running, pieces):
    row_count = pieces[0].shape[0]
    block_rows = math.gcd(row_count, 2048)

    def advance(block_idx, state):
        first_row = block_idx * block_rows
        sliced = tuple(
            (lax.dynamic_slice_in_dim(piece, first_row, block_rows, 0) for piece in pieces)
        )
        return block_step(state, sliced, first_row)

    return lax.fori_loop(0, row_count // block_rows, advance, running)


def shards(
    tokens_in,
    clip_lengths,
    attn_gain,
    attn_shift,
    qkv_weight,
    qkv_bias,
    proj_weight,
    proj_bias,
    mlp_gain,
    mlp_shift,
    up_weight,
    up_bias,
    down_weight,
    down_bias,
    out_cotangent,
):
    tok_rows = tokens_in.shape[1]
    model_width = tokens_in.shape[2]
    seq_len = tok_rows * lax.axis_size("blk")
    lens_row = clip_lengths[0]
    own_pos = lax.axis_index("blk") * tok_rows + jnp.arange(tok_rows, dtype=jnp.int32)
    clip_q, cos_tab, sin_tab = clip_layout(lens_row, own_pos)
    residual = tokens_in[0].astype(jnp.float32)
    attn_gain_f = attn_gain.astype(jnp.float32)
    mlp_gain_f = mlp_gain.astype(jnp.float32)
    normed, hat_one, inv_one = norm_fwd(residual, attn_gain_f, attn_shift.astype(jnp.float32))
    normed_low = normed.astype(jnp.bfloat16)
    qkv_mixed = jnp.dot(
        normed_low, qkv_weight, preferred_element_type=jnp.float32
    ) + qkv_bias.astype(jnp.float32)
    query_h = rotate(qkv_mixed[:, :model_width].reshape(tok_rows, H, HD), cos_tab, sin_tab).astype(
        jnp.bfloat16
    )
    key_low = (
        rotate(
            qkv_mixed[:, model_width : 2 * model_width].reshape(tok_rows, H, HD), cos_tab, sin_tab
        )
        .astype(jnp.bfloat16)
        .reshape(tok_rows, model_width)
    )
    value_low = qkv_mixed[:, 2 * model_width :].astype(jnp.bfloat16)

    def block_scores(keys_blk, first_key):
        key_count = keys_blk.shape[0]
        clip_k = clip_of(lens_row, first_key + jnp.arange(key_count, dtype=jnp.int32))
        raw_scores = jnp.einsum(
            "qhd,khd->hqk",
            query_h,
            keys_blk.reshape(key_count, H, HD),
            preferred_element_type=jnp.float32,
        )
        allowed = (clip_q[:, None] == clip_k[None, :])[None]
        return (jnp.where(allowed, 0.125 * raw_scores, NEG_FILL), allowed)

    def stats_step(state, sliced, first_key):
        row_max, row_sum = state
        scores, allowed = block_scores(sliced[0], first_key)
        new_max = jnp.maximum(row_max, jnp.max(scores, -1))
        weights = jnp.where(allowed, jnp.exp(scores - new_max[:, :, None]), 0.0)
        return (new_max, row_sum * jnp.exp(row_max - new_max) + jnp.sum(weights, -1))

    stats_init = (
        jnp.full((H, tok_rows), NEG_FILL, jnp.float32),
        jnp.zeros((H, tok_rows), jnp.float32),
    )
    row_max, row_sum = in_blocks(
        stats_step, stats_init, (lax.all_gather(key_low, "blk", axis=0, tiled=True),)
    )
    log_sum = row_max + jnp.log(row_sum)

    def output_step(acc_state, sliced, first_key):
        keys_blk, values_blk = sliced
        key_count = keys_blk.shape[0]
        scores, allowed = block_scores(keys_blk, first_key)
        weights = jnp.where(allowed, jnp.exp(scores - log_sum[:, :, None]), 0.0)
        return acc_state + jnp.einsum(
            "hqk,khd->qhd",
            weights.astype(jnp.bfloat16),
            values_blk.reshape(key_count, H, HD),
            preferred_element_type=jnp.float32,
        )

    acc_init = jnp.zeros((tok_rows, H, HD), jnp.float32)
    attended_f = in_blocks(
        output_step,
        acc_init,
        (
            lax.all_gather(key_low, "blk", axis=0, tiled=True),
            lax.all_gather(value_low, "blk", axis=0, tiled=True),
        ),
    )
    attended_low = attended_f.reshape(tok_rows, model_width).astype(jnp.bfloat16)
    middle = (
        residual
        + jnp.dot(attended_low, proj_weight, preferred_element_type=jnp.float32)
        + proj_bias.astype(jnp.float32)
    )
    normed_two, hat_two, inv_two = norm_fwd(middle, mlp_gain_f, mlp_shift.astype(jnp.float32))
    normed_two_low = normed_two.astype(jnp.bfloat16)
    hidden = jnp.dot(
        normed_two_low, up_weight, preferred_element_type=jnp.float32
    ) + up_bias.astype(jnp.float32)
    active_low = jax.nn.gelu(hidden).astype(jnp.bfloat16)
    result = (
        middle
        + jnp.dot(active_low, down_weight, preferred_element_type=jnp.float32)
        + down_bias.astype(jnp.float32)
    )
    layer_out = result.astype(jnp.bfloat16)[None]
    cot_low = out_cotangent[0]
    cot_f = cot_low.astype(jnp.float32)
    grad_down_w = outer_sum(active_low, cot_low)
    grad_down_b = jnp.sum(cot_f, 0)
    d_active = times_transposed(cot_low, down_weight)
    hidden_unused, gelu_back = jax.vjp(jax.nn.gelu, hidden)
    d_hidden = gelu_back(d_active)[0].astype(jnp.bfloat16)
    grad_up_w = outer_sum(normed_two_low, d_hidden)
    grad_up_b = jnp.sum(d_hidden.astype(jnp.float32), 0)
    d_normed_two = times_transposed(d_hidden, up_weight)
    d_mid_norm, grad_mlp_gain, grad_mlp_shift = norm_back(
        d_normed_two, hat_two, inv_two, mlp_gain_f
    )
    d_middle = cot_f + d_mid_norm
    d_branch = d_middle.astype(jnp.bfloat16)
    grad_proj_w = outer_sum(attended_low, d_branch)
    grad_proj_b = jnp.sum(d_branch.astype(jnp.float32), 0)
    d_attended = (
        times_transposed(d_branch, proj_weight).astype(jnp.bfloat16).reshape(tok_rows, H, HD)
    )
    delta = jnp.einsum("qhd,qhd->hq", d_attended.astype(jnp.float32), attended_f)

    def back_step(state, sliced, first_key):
        dq_acc, buffers = state
        keys_blk, values_blk = sliced
        key_count = keys_blk.shape[0]
        scores, allowed = block_scores(keys_blk, first_key)
        weights = jnp.where(allowed, jnp.exp(scores - log_sum[:, :, None]), 0.0)
        d_weights = jnp.einsum(
            "qhd,khd->hqk",
            d_attended,
            values_blk.reshape(key_count, H, HD),
            preferred_element_type=jnp.float32,
        )
        d_scores = (weights * (d_weights - delta[:, :, None])).astype(jnp.bfloat16)
        dq_acc = dq_acc + 0.125 * jnp.einsum(
            "hqk,khd->qhd",
            d_scores,
            keys_blk.reshape(key_count, H, HD),
            preferred_element_type=jnp.float32,
        )
        d_keys = 0.125 * jnp.einsum(
            "hqk,qhd->khd", d_scores, query_h, preferred_element_type=jnp.float32
        )
        d_values = jnp.einsum(
            "hqk,qhd->khd",
            weights.astype(jnp.bfloat16),
            d_attended,
            preferred_element_type=jnp.float32,
        )
        key_buffer = add_rows(buffers[0], d_keys.reshape(key_count, model_width), first_key)
        value_buffer = add_rows(buffers[1], d_values.reshape(key_count, model_width), first_key)
        buffers = (key_buffer, value_buffer)
        return (dq_acc, buffers)

    buffer_init = (
        jnp.zeros((seq_len, model_width), jnp.float32),
        jnp.zeros((seq_len, model_width), jnp.float32),
    )
    back_init = (jnp.zeros((tok_rows, H, HD), jnp.float32), buffer_init)
    d_queries, key_grads = in_blocks(
        back_step,
        back_init,
        (
            lax.all_gather(key_low, "blk", axis=0, tiled=True),
            lax.all_gather(value_low, "blk", axis=0, tiled=True),
        ),
    )
    d_keys_own, d_values_own = (
        lax.psum_scatter(key_grads[0], "blk", scatter_dimension=0, tiled=True),
        lax.psum_scatter(key_grads[1], "blk", scatter_dimension=0, tiled=True),
    )
    d_queries_pre = rotate(d_queries, cos_tab, -sin_tab).reshape(tok_rows, model_width)
    d_keys_pre = rotate(d_keys_own.reshape(tok_rows, H, HD), cos_tab, -sin_tab).reshape(
        tok_rows, model_width
    )
    d_mixed = jnp.concatenate([d_queries_pre, d_keys_pre, d_values_own], axis=1).astype(
        jnp.bfloat16
    )
    grad_qkv_w = outer_sum(normed_low, d_mixed)
    grad_qkv_b = jnp.sum(d_mixed.astype(jnp.float32), 0)
    d_normed = times_transposed(d_mixed, qkv_weight)
    d_res_norm, grad_attn_gain, grad_attn_shift = norm_back(d_normed, hat_one, inv_one, attn_gain_f)
    tokens_grad = (d_middle + d_res_norm)[None]
    summed = (
        lax.psum_scatter(grad_qkv_w, ("batch", "blk"), scatter_dimension=0, tiled=True),
        lax.psum_scatter(grad_proj_w, ("batch", "blk"), scatter_dimension=0, tiled=True),
        lax.psum_scatter(grad_up_w, ("batch", "blk"), scatter_dimension=0, tiled=True),
        lax.psum_scatter(grad_down_w, ("batch", "blk"), scatter_dimension=0, tiled=True),
        lax.psum_scatter(grad_attn_gain, ("batch", "blk"), scatter_dimension=0, tiled=True),
        lax.psum_scatter(grad_attn_shift, ("batch", "blk"), scatter_dimension=0, tiled=True),
        lax.psum_scatter(grad_qkv_b, ("batch", "blk"), scatter_dimension=0, tiled=True),
        lax.psum_scatter(grad_proj_b, ("batch", "blk"), scatter_dimension=0, tiled=True),
        lax.psum_scatter(grad_mlp_gain, ("batch", "blk"), scatter_dimension=0, tiled=True),
        lax.psum_scatter(grad_mlp_shift, ("batch", "blk"), scatter_dimension=0, tiled=True),
        lax.psum_scatter(grad_up_b, ("batch", "blk"), scatter_dimension=0, tiled=True),
        lax.psum_scatter(grad_down_b, ("batch", "blk"), scatter_dimension=0, tiled=True),
    )
    return (
        layer_out,
        tokens_grad,
        summed[4],
        summed[5],
        summed[0],
        summed[6],
        summed[1],
        summed[7],
        summed[8],
        summed[9],
        summed[2],
        summed[10],
        summed[3],
        summed[11],
    )


BF = jnp.bfloat16
F32 = jnp.float32
AXES = ("x", "core", "zh", "zl", "y")
ROW = ("zh", "zl", "y")
GELU_A = 0.7978845608028654
GELU_B = 0.044715
VMEM_MIB = 32
PIN = 400000
LOW_PIN = 200000
NO_PIN = 1 << 30


def mm(left, right):
    return jnp.dot(left, right, preferred_element_type=F32)


def swap_over(value, *names):
    mask = sum(16 >> AXES.index(name) for name in names)
    return lax.ppermute(value, AXES, [(i, i ^ mask) for i in range(32)])


def whole(shape):
    zeros = (0,) * len(shape)
    return pl.BlockSpec(shape, lambda *_: zeros)


def arr(shape, dtype):
    return jax.ShapeDtypeStruct(shape, dtype)


def call(body, grid, in_specs, out_specs, out_shape, scratch, pin, scalars, args):
    return pl.pallas_call(
        body,
        grid_spec=pltpu.PrefetchScalarGridSpec(
            num_scalar_prefetch=1,
            grid=grid,
            in_specs=in_specs,
            out_specs=out_specs,
            scratch_shapes=scratch,
        ),
        out_shape=[pltpu.HBM(o.shape, o.dtype) if big(o, pin) else o for o in out_shape],
        compiler_params=pltpu.CompilerParams(vmem_limit_bytes=VMEM_MIB << 20),
        cost_estimate=pl.CostEstimate(flops=0, bytes_accessed=1024, transcendentals=0),
    )(scalars, *(pinned(v, pin) for v in args))


def big(v, pin):
    return math.prod(v.shape) * v.dtype.itemsize >= pin


def pinned(v, pin):
    return pltpu.with_memory_space_constraint(v, pltpu.HBM) if big(v, pin) else v


def one_step(body, outs, scratch, pin, scalars, args):
    return call(
        body, (1,), [whole(v.shape) for v in args], [whole(o.shape) for o in outs], outs, scratch,
        pin, scalars, args,
    )


def standardize(x):
    mean = jnp.mean(x, -1, keepdims=True)
    centered = x - mean
    inv = lax.rsqrt(jnp.mean(centered * centered, -1, keepdims=True) + 1e-06)
    return centered * inv, inv


def swap_halves(x):
    lane = lax.broadcasted_iota(jnp.int32, x.shape, 1)
    return jnp.where(lane % 64 < 32, pltpu.roll(x, 96, 1), pltpu.roll(x, 32, 1))


def gelu_both(h):
    t = jnp.tanh(h * (GELU_A + (GELU_A * GELU_B) * (h * h)))
    half = 0.5 * h
    act = half + half * t
    slope = (0.5 + 0.5 * t) + half * (1.0 - t * t) * (GELU_A + (3.0 * GELU_A * GELU_B) * (h * h))
    return act, slope


def down_back_body(place, cot, down, d_act, bias_part):
    @pl.when(pl.program_id(0) == 0)
    def _():
        bias_part[...] = jnp.sum(cot[...].astype(F32), 0, keepdims=True)

    d_act[...] = times_transposed(cot[...], down[...])


def qkv_half(place, blocks, vecs, ws, cos, sin, hat_out, normed):
    g = vecs[0:1, :]
    s = vecs[1:2, :]
    for j in range(4):
        rows = slice(128 * j, 128 * j + 128)
        hat, _ = standardize(blocks[j][...].astype(F32))
        hat_out[rows, :] = hat.astype(BF)
        normed[rows, :] = (hat * g + s).astype(BF)
    lanes = pl.ds(pl.multiple_of(place[0] * 128, 128), 128)
    bias3 = jnp.concatenate([vecs[12 + p : 13 + p, lanes] for p in range(3)], 1)
    mixed = mm(normed[...], jnp.concatenate([w[...] for w in ws], 1)) + bias3
    c = cos[...]
    sn = sin[...]
    q = mixed[:, :128]
    k = mixed[:, 128:256]
    return (
        ((q * c + swap_halves(q) * sn) * 0.125).astype(BF),
        (k * c + swap_halves(k) * sn).astype(BF),
        mixed[:, 256:].astype(BF),
    )


def near_body(place, *refs):
    blocks = refs[:4]
    vecs, wq, wk, wv, cos, sin, hat_out, q_out, k_out, v_out, normed = refs[4:]
    q, k, v = qkv_half(place, blocks, vecs, (wq, wk, wv), cos, sin, hat_out, normed)
    q_out[...] = q
    k_out[...] = k
    v_out[...] = v


def far_body(place, *refs):
    blocks = refs[:4]
    vecs, wq, wk, wv, cos, sin, q0, k0, v0, hat_out, q_out, k_out, v_out, normed = refs[4:]
    q, k, v = qkv_half(place, blocks, vecs, (wq, wk, wv), cos, sin, hat_out, normed)
    for out, near, far in ((q_out, q0, q), (k_out, k0, k), (v_out, v0, v)):
        out[:512, :] = near[...]
        out[512:, :] = far


def head_mask(shape, head):
    return lax.broadcasted_iota(jnp.int32, shape, 1) // 64 == head


def attend_body(place, q, k_all, v_all, id_col, id_row, att_f, att_low, probs):
    keys = k_all[...]
    values = v_all[...]
    queries = q[...]
    own = id_col[...]
    allowed = jnp.concatenate([own, own], 1) == id_row[0:1, :]
    halves = []
    for head in range(2):
        mine = jnp.where(head_mask(queries.shape, head), queries, jnp.zeros_like(queries))
        scores = jnp.where(allowed, times_transposed(keys, mine), NEG_FILL)
        weights = jnp.exp(scores - jnp.max(scores, 0, keepdims=True))
        low = (weights * (1.0 / jnp.sum(weights, 0, keepdims=True))).astype(BF)
        probs[head] = low
        halves.append(outer_sum(values, low)[64 * head : 64 * head + 64])
    out = jnp.concatenate(halves, 0).T
    att_f[...] = out
    step = pl.program_id(0)
    att_low[place[0] ^ (2 * step)] = out[:128].astype(BF)
    att_low[place[0] ^ (2 * step + 1)] = out[128:].astype(BF)


def proj_body(place, att, tok, proj_w, vecs, middle, normed, att_rows):
    rows = jnp.concatenate([att[k] for k in range(8)], 1)
    att_rows[...] = rows
    mid = tok[...].astype(F32) + mm(rows, proj_w[...]) + vecs[2:3, :]
    middle[...] = mid
    hat, _ = standardize(mid)
    low = (hat * vecs[3:4, :] + vecs[4:5, :]).astype(BF)
    normed[...] = low


def proj_grad(place, att, d_b, vectors, send, keep):
    grad = outer_sum(att, d_b)
    row = lax.broadcasted_iota(jnp.int32, (32, 128), 0)
    for owner in range(32):
        x, core, k = owner // 16, (owner // 8) % 2, owner % 8
        rows = grad[32 * owner : 32 * owner + 32]
        extra = jnp.zeros((32, 128), F32)
        first = 128 * (owner // 4)
        for m in range(4):
            extra = jnp.where(row == m, vectors[m : m + 1, first : first + 128], extra)
        group = 2 * x + core
        last = vectors[4 + group : 5 + group, 128 * k : 128 * k + 128]
        extra = jnp.where(row == 4, last, extra)
        rel = place[0] ^ k
        slot = (rel & 1) * 4 + (rel & 2) + (rel >> 2)
        for side, out in ((core == place[2], keep), (core != place[2], send)):

            @pl.when(side)
            def _():
                out[place[1] ^ x, slot, :, :1024] = rows.astype(BF)
                out[place[1] ^ x, slot, :, 1024:] = extra.astype(BF)


def mlp_body(
    place, normed, d_act, up_w, vecs, middle, cot, proj_w, down_bias, att,
    active, d_mid, d_att, proj_send, proj_keep, acc, vectors,
):
    step = pl.program_id(0)
    hidden = mm(normed[...], up_w[...]) + vecs[pl.ds(8 + step, 1), :]
    act, slope = gelu_both(hidden)
    active[...] = act.astype(BF)
    d_hidden = (d_act[...] * slope).astype(BF)
    vectors[pl.ds(4 + step, 1), :] = jnp.sum(d_hidden.astype(F32), 0, keepdims=True)
    part = times_transposed(d_hidden, up_w[...])

    @pl.when(step == 0)
    def _():
        acc[...] = part

    @pl.when(step > 0)
    def _():
        acc[...] += part

    @pl.when(step == pl.num_programs(0) - 1)
    def _():
        up = acc[...]
        hat, inv = standardize(middle[...])
        e = up * vecs[3:4, :]
        inner = e - jnp.mean(e, -1, keepdims=True) - hat * jnp.mean(e * hat, -1, keepdims=True)
        d_m = cot[...].astype(F32) + inv * inner
        d_mid[...] = d_m
        d_b = d_m.astype(BF)
        vectors[0:1, :] = jnp.sum(up * hat, 0, keepdims=True)
        vectors[1:2, :] = jnp.sum(up, 0, keepdims=True)
        vectors[2:3, :] = jnp.sum(d_b.astype(F32), 0, keepdims=True)
        vectors[3:4, :] = down_bias[...]
        d_a = times_transposed(d_b, proj_w[...]).astype(BF)
        for k in range(8):
            d_att[k] = d_a[:, 128 * k : 128 * k + 128]
        proj_grad(place, att[...], d_b, vectors, proj_send, proj_keep)


def mlp_grad_body(place, *refs):
    blocks, cots, ups, downs = refs[:8], refs[8:16], refs[16:20], refs[20:24]
    vecs, down_keep, down_send, up_keep, up_send, n_all, c_all, u_all, d_all, grad = refs[24:]
    for j in range(8):
        n_all[128 * j : 128 * j + 128, :] = blocks[j][...]
        c_all[128 * j : 128 * j + 128, :] = cots[j][...]
    lanes = pl.ds(pl.multiple_of(place[0] * 128, 128), 128)
    up_b = []
    rows = vecs[8:12, lanes]
    biases = lax.broadcasted_iota(jnp.int32, (4, 128), 0)
    for g in range(4):
        u_all[:, 128 * g : 128 * g + 128] = ups[g][...]
        d_all[128 * g : 128 * g + 128, :] = downs[g][...]
        group = (place[1] ^ (g & 1)) * 2 + (place[2] ^ (g >> 1))
        up_b.append(jnp.sum(jnp.where(biases == group, rows, 0.0), 0, keepdims=True))
    n = n_all[...]
    c = c_all[...]
    act, slope = gelu_both(mm(n, u_all[...]) + jnp.concatenate(up_b, 1))
    grad_down = outer_sum(act.astype(BF), c)
    for g in range(4):
        rows = grad_down[128 * g : 128 * g + 128]
        if g < 2:
            down_keep[g] = rows.astype(BF)
        else:
            down_send[g - 2] = rows.astype(BF)
    d_hidden = (times_transposed(c, d_all[...]) * slope).astype(BF)
    both = outer_sum(n, d_hidden)
    for g in range(4):
        group = ((place[1] ^ (g & 1)) * 2) + (place[2] ^ (g >> 1))
        lanes = pl.ds(pl.multiple_of(group * 128, 128), 128)
        grad[:, lanes] = both[:, 128 * g : 128 * g + 128]
    for rx in range(2):
        first = (place[1] ^ rx) * 512
        keep = pl.multiple_of(first + place[2] * 256, 256)
        send = pl.multiple_of(first + (1 - place[2]) * 256, 256)
        up_keep[rx] = grad[pl.ds(keep, 256), :].astype(BF)
        up_send[rx] = grad[pl.ds(send, 256), :].astype(BF)


def attend_back_body(
    place, probs, d_att, att_f, q, k_all, v_all, cos, sin, d_all, bias_part, dq, dk, dv
):
    step = pl.program_id(0)
    keys = k_all[...]
    values = v_all[...]
    queries = q[...]
    d_out = jnp.concatenate([d_att[place[0] ^ (2 * step)], d_att[place[0] ^ (2 * step + 1)]], 0)
    products = (d_out.astype(F32) * att_f[...]).T
    key_parts, value_parts, query_parts = [], [], []
    for head in range(2):
        weights = probs[head]
        mine = jnp.where(head_mask(d_out.shape, head), d_out, jnp.zeros_like(d_out))
        delta = jnp.sum(products[64 * head : 64 * head + 64], 0, keepdims=True)
        d_weights = times_transposed(values, mine)
        d_scores = (weights.astype(F32) * (d_weights - delta)).astype(BF)
        key_parts.append(mm(d_scores, queries))
        value_parts.append(mm(weights, d_out))
        query_parts.append(outer_sum(keys, d_scores)[64 * head : 64 * head + 64])
    first = head_mask((1024, 128), 0)
    dk_new = jnp.where(first, key_parts[0], key_parts[1])
    dv_new = jnp.where(first, value_parts[0], value_parts[1])
    dq[pl.ds(pl.multiple_of(step * 256, 256), 256), :] = jnp.concatenate(query_parts, 0).T

    @pl.when(step == 0)
    def _():
        dk[...] = dk_new
        dv[...] = dv_new

    @pl.when(step > 0)
    def _():
        dk[...] += dk_new
        dv[...] += dv_new

    @pl.when(step == pl.num_programs(0) - 1)
    def _():
        total = jnp.zeros((1, 384), F32)
        for j in range(8):
            rows = slice(128 * j, 128 * j + 128)
            c = cos[rows, :]
            sn = sin[rows, :]
            back_q = 0.125 * dq[rows, :]
            back_k = dk[rows, :]
            piece = jnp.concatenate(
                [
                    back_q * c - swap_halves(back_q) * sn,
                    back_k * c - swap_halves(back_k) * sn,
                    dv[rows, :],
                ],
                1,
            ).astype(BF)
            d_all[place[0] ^ j] = piece
            total = total + jnp.sum(piece.astype(F32), 0, keepdims=True)
        bias_part[...] = total


def rel_block(step, place):
    rel = jnp.where(step < 2, 2, 0) + step % 2
    return ((rel & 1) ^ place[1]) * 2 + ((rel >> 1) ^ place[2])


def qkv_grad_body(place, h0, h1, d_all, bias_part, columns, wq, wk, wv, send, keep):
    step = pl.program_id(0)
    d_near = jnp.concatenate([d_all[place[0] ^ j] for j in range(4)], 0)
    d_far = jnp.concatenate([d_all[place[0] ^ j] for j in range(4, 8)], 0)
    inner = outer_sum(h0[...], d_near) + outer_sum(h1[...], d_far)
    total = bias_part[...]
    w = jnp.concatenate([wq[...], wk[...], wv[...]], 1).astype(F32)
    gain = columns[:, 0:1]
    shift = columns[:, 1:2]
    grad = gain * inner + shift * total
    row = lax.broadcasted_iota(jnp.int32, (256, 128), 0) % 32
    lane = lax.broadcasted_iota(jnp.int32, (256, 128), 1)
    extra = jnp.where(
        lane == 0,
        jnp.sum(w * inner, 1, keepdims=True),
        jnp.where(lane == 1, jnp.sum(w * total, 1, keepdims=True), 0.0),
    )
    for m in range(6):
        part = total[:, 128 * (m // 2) : 128 * (m // 2) + 128]
        part = part if m % 2 else pltpu.roll(part, 64, 1)
        extra = jnp.where((row == m) & (lane >= 64), part, extra)

    @pl.when(step < 2)
    def _():
        send[0, :, :384] = grad.astype(BF)
        send[0, :, 384:] = extra.astype(BF)

    @pl.when(step >= 2)
    def _():
        keep[0, :, :384] = grad.astype(BF)
        keep[0, :, 384:] = extra.astype(BF)


def pair_body(place, keep, came, left, send):
    half = left.shape[0]
    total = (keep[...].astype(F32) + came[...].astype(F32)).astype(BF)
    left[...] = total[:half]
    send[...] = total[half:]


def merge_body(place, *refs):
    keeps, cames = refs[0:6:2], refs[1:6:2]
    proj_left, proj_came, left, send, down_left, down_send, proj_keep, proj_send = refs[6:]
    proj_keep[...] = (proj_left[:1].astype(F32) + proj_came[:1].astype(F32)).astype(BF)
    proj_send[...] = (proj_left[1:].astype(F32) + proj_came[1:].astype(F32)).astype(BF)
    for side, low, down in ((0, left, down_left), (1, send, down_send)):
        for m in range(2):
            total = keeps[m][side].astype(F32) + cames[m][side].astype(F32)
            for k in range(8):
                low[k, 32 * m : 32 * m + 32, :] = total[32 * k : 32 * k + 32].astype(BF)
        down[...] = (keeps[2][side].astype(F32) + cames[2][side].astype(F32)).astype(BF)


def finish_body(place, came, grad_up, grad_qkv, sums, bias):
    total = jnp.zeros((32, 128), F32)
    low = lax.broadcasted_iota(jnp.int32, (1, 128), 1) < 64
    for k in range(8):
        for g in range(4):
            lanes = slice(1024 * g + 128 * k, 1024 * g + 128 * k + 128)
            grad_up[:, lanes] = came[k, :32, 128 * g : 128 * g + 128].astype(F32)
            if g < 3:
                grad_qkv[:, lanes] = came[k, 32:, 128 * g : 128 * g + 128].astype(F32)
        extra = came[k, 32:, 384:].astype(F32)
        total = total + extra
        for p in range(3):
            left = pltpu.roll(extra[2 * p : 2 * p + 1], 64, 1)
            both = jnp.where(low, left, extra[2 * p + 1 : 2 * p + 2])
            bias[p : p + 1, 128 * k : 128 * k + 128] = both
    sums[...] = total.T[:8]


def last_body(place, came, w, tok, d_mid, vecs, out, acc):
    step = pl.program_id(0)
    for p in range(3):

        @pl.when(step == p)
        def _():
            d_mixed = jnp.concatenate([came[k, :, 128 * p : 128 * p + 128] for k in range(8)], 1)
            part = times_transposed(d_mixed, w[...])
            if p == 0:
                acc[...] = part
            elif p == 1:
                acc[...] += part
            else:
                up = acc[...] + part
                hat, inv = standardize(tok[...].astype(F32))
                e = up * vecs[0:1, :]
                mean = jnp.mean(e, -1, keepdims=True)
                inner = e - mean - hat * jnp.mean(e * hat, -1, keepdims=True)
                out[...] = d_mid[...] + inv * inner


def frequency_rows():
    rows = np.zeros((8, 128), np.float32)
    for lane in range(128):
        pair = lane % 32
        part, rank, count = (0, pair, 10) if pair < 10 else ((1, pair - 10, 11) if pair < 21 else (2, pair - 21, 11))
        rows[part, lane] = 10000.0 ** (-rank / count)
        rows[3, lane] = -1.0 if lane % 64 < 32 else 1.0
    return rows


def clip_starts(place, pos):
    ids = jnp.zeros_like(pos)
    start = jnp.zeros_like(pos)
    end = jnp.int32(0)
    for c in range(8):
        length = place[8 + c]
        end = end + length
        past = pos >= end.astype(F32)
        ids = jnp.where(past, ids + 1.0, ids)
        start = jnp.where(past, end.astype(F32), start)
    return ids, start


def prep_body(place, freq, vecs, cos, sin, id_col, id_row, columns):
    for j in range(8):
        first = ((place[0] ^ j) * 128).astype(F32)
        rows = slice(128 * j, 128 * j + 128)
        pos = first + lax.broadcasted_iota(jnp.int32, (128, 128), 0).astype(F32)
        ids, start = clip_starts(place, pos)
        id_col[rows, :] = ids
        within = pos - start
        row14 = jnp.floor((within + 0.5) * (1.0 / 14.0))
        t = jnp.floor((within + 0.5) * (1.0 / 196.0))
        angle = t * freq[0:1, :] + (row14 - 14.0 * t) * freq[1:2, :] + (within - 14.0 * row14) * freq[2:3, :]
        cos[rows, :] = jnp.cos(angle)
        sin[rows, :] = jnp.sin(angle) * freq[3:4, :]
        flat = first + lax.broadcasted_iota(jnp.int32, (8, 128), 1).astype(F32)
        id_row[:, 128 * j : 128 * j + 128] = clip_starts(place, flat)[0]
    columns[...] = vecs[0:8, :].T


def after(value, *others):
    return lax.optimization_barrier((value, *others))[0]


def spread_four(a):
    return [a, swap_over(a, "y"), swap_over(a, "zl"), swap_over(a, "zl", "y")]


def fast_shards(
    tokens_in, clip_lengths, attn_gain, attn_shift, qkv_weight, qkv_bias, proj_weight, proj_bias,
    mlp_gain, mlp_shift, up_weight, up_bias, down_weight, down_bias, out_cotangent,
):
    x, core, zh, zl, y = (lax.axis_index(name) for name in AXES)
    k = zh * 4 + zl * 2 + y
    me = x * 16 + core * 8 + k
    place = jnp.concatenate(
        [jnp.stack([k, x, core, k, k, k, k, k]).astype(jnp.int32), clip_lengths[0]]
    )
    tok = tokens_in[0]
    cot = out_cotangent[0]

    far_tok = swap_over(tok, "zh")
    near = spread_four(tok)
    rows = [attn_gain, attn_shift, proj_bias, mlp_gain, mlp_shift, down_bias, down_bias, down_bias]
    vecs = jnp.concatenate([v.astype(F32).reshape(-1, 1024) for v in (*rows, up_bias, qkv_bias)], 0)
    cos_tab, sin_tab, id_col, id_row, columns = one_step(
        prep_body,
        [arr((1024, 128), F32), arr((1024, 128), F32), arr((1024, 128), F32), arr((8, 1024), F32),
         arr((1024, 8), F32)],
        [],
        PIN,
        place,
        (jnp.asarray(frequency_rows()), vecs),
    )
    far_tok, cos_tab, *near = lax.optimization_barrier((far_tok, cos_tab, *near))
    far = spread_four(far_tok)

    def table_half(part):
        return pl.BlockSpec((512, 128), lambda i, s: (part, 0))

    half = arr((512, 128), BF)
    full = arr((1024, 128), BF)
    common = (vecs, qkv_weight, qkv_weight, qkv_weight, cos_tab, sin_tab)
    columns_of = [pl.BlockSpec((1024, 128), lambda i, s, p=p: (0, 8 * p + s[0])) for p in range(3)]

    def qkv(body, part, blocks, more, outs):
        specs = [whole(v.shape) for v in (*blocks, vecs)] + columns_of
        specs += [table_half(part), table_half(part)] + [whole(v.shape) for v in more]
        return call(
            body, (1,), specs, [whole(o.shape) for o in outs], outs,
            [pltpu.VMEM((512, 1024), BF)], PIN, place, (*blocks, *common, *more),
        )

    hat0, q0, k0, v0 = qkv(near_body, 0, near, (), [arr((512, 1024), BF), half, half, half])
    d_act, down_bias_part = call(
        down_back_body,
        (4,),
        [whole((128, 1024)), pl.BlockSpec((1024, 1024), lambda i, s: (i, 0))],
        [pl.BlockSpec((128, 1024), lambda i, s: (0, i)), whole((1, 1024))],
        [arr((128, 4096), F32), arr((1, 1024), F32)],
        [],
        PIN,
        place,
        (after(cot, q0), down_weight),
    )
    far = lax.optimization_barrier((q0, d_act, *far))[2:]
    cot_here = after(cot, q0)
    far_cot = swap_over(cot_here, "zh")
    cots = spread_four(cot_here)
    hat1, q_all, k_all, v_all = qkv(
        far_body, 1, far, (q0, k0, v0), [arr((512, 1024), BF), full, full, full]
    )
    step_rows = pl.BlockSpec((256, 128), lambda i, s: (i, 0))
    flat = whole((1024, 128))
    att_f, att_low, probs = call(
        attend_body,
        (4,),
        [
            step_rows, flat, flat, flat, pl.BlockSpec((8, 256), lambda i, s: (0, i)),
        ],
        [step_rows, whole((8, 128, 128)), pl.BlockSpec((2, 1024, 256), lambda i, s: (0, 0, i))],
        [arr((1024, 128), F32), arr((8, 128, 128), BF), arr((2, 1024, 1024), BF)],
        [],
        PIN,
        place,
        (q_all, k_all, v_all, id_col, id_row),
    )
    att_low, far_cot, *cots = lax.optimization_barrier((att_low, far_cot, *cots))
    att_in = lax.all_to_all(att_low, ROW, 0, 0, tiled=True)
    cots += [far_cot, swap_over(far_cot, "y"), swap_over(far_cot, "zl")]
    middle, normed2, att_rows = one_step(
        proj_body,
        [arr((128, 1024), F32), arr((128, 1024), BF), arr((128, 1024), BF)],
        [],
        PIN,
        place,
        (att_in, tok, proj_weight, vecs),
    )
    normed2, *cots = lax.optimization_barrier((normed2, *cots))
    far_n = swap_over(normed2, "zh")
    near_n = spread_four(normed2)
    wide = pl.BlockSpec((128, 1024), lambda i, s: (0, i))
    fixed = whole((128, 1024))
    active, d_mid, d_att, proj_send, proj_keep = call(
        mlp_body,
        (4,),
        [
            fixed, wide, wide_columns(), whole((15, 1024)), fixed, fixed, whole((1024, 1024)),
            whole((1, 1024)), fixed,
        ],
        [wide, fixed, whole((8, 128, 128)), whole((2, 8, 32, 1152)), whole((2, 8, 32, 1152))],
        [
            arr((128, 4096), BF), arr((128, 1024), F32), arr((8, 128, 128), BF),
            arr((2, 8, 32, 1152), BF), arr((2, 8, 32, 1152), BF),
        ],
        [pltpu.VMEM((128, 1024), F32), pltpu.VMEM((8, 1024), F32)],
        LOW_PIN,
        place,
        (normed2, d_act, up_weight, vecs, middle, cot, proj_weight, down_bias_part, att_rows),
    )
    d_att, far_n, far_y, active, proj_send, *near_n = lax.optimization_barrier(
        (d_att, far_n, cots[5], active, proj_send, *near_n)
    )
    last_cot = swap_over(far_y, "zl")
    d_att_in = lax.all_to_all(d_att, ROW, 0, 0, tiled=True)

    far_n = spread_four(far_n)

    def pair(keep, came):
        half = arr((keep.shape[0] // 2, *keep.shape[1:]), BF)
        return one_step(pair_body, [half, half], [], NO_PIN, place, (keep, came))

    flat_proj = (16, 32, 1152)
    proj_left, proj_low = pair(
        proj_keep.reshape(flat_proj), swap_over(proj_send.reshape(flat_proj), "core")
    )

    d_all, qkv_bias_part = call(
        attend_back_body,
        (4,),
        [
            pl.BlockSpec((2, 1024, 256), lambda i, s: (0, 0, i)), whole((8, 128, 128)), step_rows,
            step_rows, flat, flat, flat, flat,
        ],
        [whole((8, 128, 384)), whole((1, 384))],
        [arr((8, 128, 384), BF), arr((1, 384), F32)],
        [pltpu.VMEM((1024, 128), F32)] * 3,
        PIN,
        place,
        (probs, after(d_att_in, proj_low), att_f, q_all, k_all, v_all, cos_tab, sin_tab),
    )
    d_all, last_cot, *far_n = lax.optimization_barrier((d_all, last_cot, *far_n))
    moved = lax.all_to_all(d_all, ROW, 0, 0, tiled=True)
    proj_left, proj_low = pair(after(proj_left, d_all), swap_over(proj_low, "x"))

    def group_of(s, g):
        return (s[1] ^ (g & 1)) * 16 + (s[2] ^ (g >> 1)) * 8 + s[0]

    outs = [
        arr((2, 128, 1024), BF), arr((2, 128, 1024), BF), arr((2, 256, 512), BF),
        arr((2, 256, 512), BF),
    ]
    down_keep, down_send, up_keep, up_send = call(
        mlp_grad_body,
        (1,),
        [fixed] * 16
        + [pl.BlockSpec((1024, 128), lambda i, s, g=g: (0, group_of(s, g))) for g in range(4)]
        + [pl.BlockSpec((128, 1024), lambda i, s, g=g: (group_of(s, g), 0)) for g in range(4)]
        + [whole((15, 1024))],
        [whole(o.shape) for o in outs],
        outs,
        [
            pltpu.VMEM((1024, 1024), BF), pltpu.VMEM((1024, 1024), BF),
            pltpu.VMEM((1024, 512), BF), pltpu.VMEM((512, 1024), BF), pltpu.VMEM((1024, 512), F32),
        ],
        LOW_PIN,
        place,
        (after(near_n[0], d_all, proj_low), *near_n[1:], *far_n, *cots, last_cot, *([up_weight] * 4), *([down_weight] * 4), vecs),
    )


    proj_left, proj_low = pair(after(proj_left, up_send), swap_over(proj_low, "y"))
    block_of = lambda i, s: (rel_block(i, s), 0)
    lanes_of = lambda i, s: (0, rel_block(i, s))
    send, keep = call(
        qkv_grad_body,
        (4,),
        [
            pl.BlockSpec((512, 256), lanes_of), pl.BlockSpec((512, 256), lanes_of),
            whole((8, 128, 384)), whole((1, 384)), pl.BlockSpec((256, 8), block_of),
        ]
        + [pl.BlockSpec((256, 128), lambda i, s, p=p: (rel_block(i, s), 8 * p + s[0])) for p in range(3)],
        [
            pl.BlockSpec((1, 256, 512), lambda i, s: (jnp.minimum(i, 1), 0, 0)),
            pl.BlockSpec((1, 256, 512), lambda i, s: (jnp.maximum(i - 2, 0), 0, 0)),
        ],
        [arr((2, 256, 512), BF), arr((2, 256, 512), BF)],
        [],
        PIN,
        place,
        (after(hat0, up_send, proj_low), hat1, d_all, qkv_bias_part, columns, qkv_weight, qkv_weight, qkv_weight),
    )
    def turn(value):
        return lax.all_to_all(value, ROW, 0, 0, tiled=True)

    send, proj_came = lax.optimization_barrier((send, swap_over(proj_low, "zl")))
    left, low_send, down_left, down_low, proj_left, proj_low = one_step(
        merge_body,
        [arr((8, 64, 512), BF)] * 2 + [arr((128, 1024), BF)] * 2 + [arr((1, 32, 1152), BF)] * 2,
        [],
        PIN,
        place,
        (
            after(up_keep, moved), swap_over(up_send, "core"), keep, swap_over(send, "core"),
            down_keep, swap_over(down_send, "core"), proj_left, proj_came,
        ),
    )
    low_came = swap_over(low_send, "x")
    (tokens_grad,) = call(
        last_body,
        (3,),
        [
            whole((8, 128, 384)), pl.BlockSpec((1024, 1024), lambda i, s: (0, i)), fixed, fixed,
            whole((15, 1024)),
        ],
        [fixed],
        [arr((128, 1024), F32)],
        [pltpu.VMEM((128, 1024), F32)],
        PIN,
        place,
        (after(moved, left), qkv_weight, tok, d_mid, vecs),
    )

    proj_came = swap_over(proj_low, "zh")
    left, _ = lax.optimization_barrier((left, tokens_grad))
    lows = (left.astype(F32) + low_came.astype(F32)).astype(BF)
    lows, proj_came = lax.optimization_barrier((lows, proj_came))
    came = turn(lows)
    down_low, _ = lax.optimization_barrier((down_low, lows))
    grad_down = down_left.astype(F32) + swap_over(down_low, "x").astype(F32)
    proj_total = proj_left[0].astype(F32) + proj_came[0].astype(F32)
    result = middle + mm(after(active, lows), down_weight) + down_bias.astype(F32)
    layer_out = result.astype(BF)[None]
    grad_proj = proj_total[:, :1024]
    own = lax.dynamic_slice(proj_total[:4, 1024:], (0, (me % 4) * 32), (4, 32))
    grad_up_b = proj_total[4, 1024:]

    grad_up, grad_qkv, sums, bias = one_step(
        finish_body,
        [arr((32, 4096), F32), arr((32, 3072), F32), arr((8, 32), F32), arr((3, 1024), F32)],
        [],
        NO_PIN,
        place,
        (came,),
    )
    grad_qkv_b = lax.dynamic_slice(bias.reshape(3072), (me * 96,), (96,))

    return (
        layer_out, tokens_grad[None], sums[0], sums[1], grad_qkv, grad_qkv_b, grad_proj,
        own[2], own[0], own[1], grad_up, grad_up_b, grad_down, own[3],
    )


def wide_columns():
    return pl.BlockSpec((1024, 1024), lambda i, s: (0, i))


def fast_solution(mesh):
    wide_mesh = Mesh(mesh.devices.reshape(2, 2, 2, 2, 2), AXES)
    batch, blk = AXES[:2], AXES[2:]
    spread = P(batch, blk, None)
    return jax.shard_map(
        fast_shards,
        mesh=wide_mesh,
        in_specs=(spread, P(batch, None)) + (P(),) * 12 + (spread,),
        out_specs=(spread, spread)
        + tuple(P(AXES, None) if i in (2, 4, 8, 10) else P(AXES) for i in range(12)),
        check_vma=False,
    )


def solution(mesh):
    if tuple(mesh.devices.shape) == (4, 8):
        return fast_solution(mesh)
    placed = (
        P("batch", "blk", None),
        P("batch", None),
        P(),
        P(),
        P(),
        P(),
        P(),
        P(),
        P(),
        P(),
        P(),
        P(),
        P(),
        P(),
        P("batch", "blk", None),
    )
    return jax.shard_map(
        shards,
        mesh=mesh,
        in_specs=placed,
        out_specs=(
            P("batch", "blk", None),
            P("batch", "blk", None),
            P(("batch", "blk")),
            P(("batch", "blk")),
            P(("batch", "blk"), None),
            P(("batch", "blk")),
            P(("batch", "blk"), None),
            P(("batch", "blk")),
            P(("batch", "blk")),
            P(("batch", "blk")),
            P(("batch", "blk"), None),
            P(("batch", "blk")),
            P(("batch", "blk"), None),
            P(("batch", "blk")),
        ),
        check_vma=False,
    )
```

```python
import math

import jax
import jax.numpy as jnp
import numpy as np
from jax import lax
from jax.experimental import pallas as pl
from jax.experimental.pallas import tpu as pltpu
from jax.sharding import Mesh
from jax.sharding import PartitionSpec as P

H = 16
HD = 64


NEG_FILL = -1e30


def pair_table():
    part_map = [0] * 10 + [1] * 11 + [2] * 11
    freq_list = [10000.0 ** (-rank / 10.0) for rank in range(10)] + [
        10000.0 ** (-rank / 11.0) for rank in range(11)
    ] * 2
    table_rows = [
        [freq_list[column] if part_map[column] == axis_id else 0.0 for column in range(32)]
        for axis_id in range(3)
    ]
    return jnp.array(table_rows, dtype=jnp.float32)


def clip_of(lengths_row, positions):
    clip_end = jnp.cumsum(lengths_row)
    return jnp.sum((positions[:, None] >= clip_end[None, :]).astype(jnp.int32), axis=1)


def clip_layout(lengths_row, positions):
    clip_end = jnp.cumsum(lengths_row)
    starts = clip_end - lengths_row
    clip_ids = jnp.sum((positions[:, None] >= clip_end[None, :]).astype(jnp.int32), axis=1)
    member = clip_ids[:, None] == jnp.arange(lengths_row.shape[0], dtype=jnp.int32)[None, :]
    within = positions - jnp.sum(jnp.where(member, starts[None, :], 0), axis=1)
    coords = jnp.stack([within // 196, within // 14 % 14, within % 14], axis=1).astype(jnp.float32)
    angles = jnp.dot(coords, pair_table(), precision=lax.Precision.HIGHEST)
    return (clip_ids, jnp.cos(angles), jnp.sin(angles))


def rotate(values, cos_tab, sin_tab):
    half_dim = values.shape[-1] // 2
    first_half = values[..., :half_dim]
    second_half = values[..., half_dim:]
    cos_b = cos_tab[:, None, :]
    sin_b = sin_tab[:, None, :]
    return jnp.concatenate(
        [first_half * cos_b - second_half * sin_b, first_half * sin_b + second_half * cos_b],
        axis=-1,
    )


def norm_fwd(values, gain_vec, shift_vec):
    row_mean = jnp.mean(values, -1, keepdims=True)
    centered = values - row_mean
    inv_std = lax.rsqrt(jnp.mean(centered * centered, -1, keepdims=True) + 1e-06)
    normalized = centered * inv_std
    return (normalized * gain_vec + shift_vec, normalized, inv_std)


def norm_back(upstream, normalized, inv_std, gain_vec):
    scaled = upstream * gain_vec
    inner = (
        scaled
        - jnp.mean(scaled, -1, keepdims=True)
        - normalized * jnp.mean(scaled * normalized, -1, keepdims=True)
    )
    return (inv_std * inner, jnp.sum(upstream * normalized, 0), jnp.sum(upstream, 0))


def outer_sum(left, right):
    return lax.dot_general(
        left, right, (((0,), (0,)), ((), ())), preferred_element_type=jnp.float32
    )


def times_transposed(left, right):
    return lax.dot_general(
        left, right, (((1,), (1,)), ((), ())), preferred_element_type=jnp.float32
    )


def add_rows(buffer, block, first_key):
    current = lax.dynamic_slice_in_dim(buffer, first_key, block.shape[0], 0)
    return lax.dynamic_update_slice_in_dim(buffer, current + block, first_key, 0)


def in_blocks(block_step, running, pieces):
    row_count = pieces[0].shape[0]
    block_rows = math.gcd(row_count, 2048)

    def advance(block_idx, state):
        first_row = block_idx * block_rows
        sliced = tuple(
            (lax.dynamic_slice_in_dim(piece, first_row, block_rows, 0) for piece in pieces)
        )
        return block_step(state, sliced, first_row)

    return lax.fori_loop(0, row_count // block_rows, advance, running)


def shards(
    tokens_in,
    clip_lengths,
    attn_gain,
    attn_shift,
    qkv_weight,
    qkv_bias,
    proj_weight,
    proj_bias,
    mlp_gain,
    mlp_shift,
    up_weight,
    up_bias,
    down_weight,
    down_bias,
    out_cotangent,
):
    tok_rows = tokens_in.shape[1]
    model_width = tokens_in.shape[2]
    seq_len = tok_rows * lax.axis_size("blk")
    lens_row = clip_lengths[0]
    own_pos = lax.axis_index("blk") * tok_rows + jnp.arange(tok_rows, dtype=jnp.int32)
    clip_q, cos_tab, sin_tab = clip_layout(lens_row, own_pos)
    residual = tokens_in[0].astype(jnp.float32)
    attn_gain_f = attn_gain.astype(jnp.float32)
    mlp_gain_f = mlp_gain.astype(jnp.float32)
    normed, hat_one, inv_one = norm_fwd(residual, attn_gain_f, attn_shift.astype(jnp.float32))
    normed_low = normed.astype(jnp.bfloat16)
    qkv_mixed = jnp.dot(
        normed_low, qkv_weight, preferred_element_type=jnp.float32
    ) + qkv_bias.astype(jnp.float32)
    query_h = rotate(qkv_mixed[:, :model_width].reshape(tok_rows, H, HD), cos_tab, sin_tab).astype(
        jnp.bfloat16
    )
    key_low = (
        rotate(
            qkv_mixed[:, model_width : 2 * model_width].reshape(tok_rows, H, HD), cos_tab, sin_tab
        )
        .astype(jnp.bfloat16)
        .reshape(tok_rows, model_width)
    )
    value_low = qkv_mixed[:, 2 * model_width :].astype(jnp.bfloat16)

    def block_scores(keys_blk, first_key):
        key_count = keys_blk.shape[0]
        clip_k = clip_of(lens_row, first_key + jnp.arange(key_count, dtype=jnp.int32))
        raw_scores = jnp.einsum(
            "qhd,khd->hqk",
            query_h,
            keys_blk.reshape(key_count, H, HD),
            preferred_element_type=jnp.float32,
        )
        allowed = (clip_q[:, None] == clip_k[None, :])[None]
        return (jnp.where(allowed, 0.125 * raw_scores, NEG_FILL), allowed)

    def stats_step(state, sliced, first_key):
        row_max, row_sum = state
        scores, allowed = block_scores(sliced[0], first_key)
        new_max = jnp.maximum(row_max, jnp.max(scores, -1))
        weights = jnp.where(allowed, jnp.exp(scores - new_max[:, :, None]), 0.0)
        return (new_max, row_sum * jnp.exp(row_max - new_max) + jnp.sum(weights, -1))

    stats_init = (
        jnp.full((H, tok_rows), NEG_FILL, jnp.float32),
        jnp.zeros((H, tok_rows), jnp.float32),
    )
    row_max, row_sum = in_blocks(
        stats_step, stats_init, (lax.all_gather(key_low, "blk", axis=0, tiled=True),)
    )
    log_sum = row_max + jnp.log(row_sum)

    def output_step(acc_state, sliced, first_key):
        keys_blk, values_blk = sliced
        key_count = keys_blk.shape[0]
        scores, allowed = block_scores(keys_blk, first_key)
        weights = jnp.where(allowed, jnp.exp(scores - log_sum[:, :, None]), 0.0)
        return acc_state + jnp.einsum(
            "hqk,khd->qhd",
            weights.astype(jnp.bfloat16),
            values_blk.reshape(key_count, H, HD),
            preferred_element_type=jnp.float32,
        )

    acc_init = jnp.zeros((tok_rows, H, HD), jnp.float32)
    attended_f = in_blocks(
        output_step,
        acc_init,
        (
            lax.all_gather(key_low, "blk", axis=0, tiled=True),
            lax.all_gather(value_low, "blk", axis=0, tiled=True),
        ),
    )
    attended_low = attended_f.reshape(tok_rows, model_width).astype(jnp.bfloat16)
    middle = (
        residual
        + jnp.dot(attended_low, proj_weight, preferred_element_type=jnp.float32)
        + proj_bias.astype(jnp.float32)
    )
    normed_two, hat_two, inv_two = norm_fwd(middle, mlp_gain_f, mlp_shift.astype(jnp.float32))
    normed_two_low = normed_two.astype(jnp.bfloat16)
    hidden = jnp.dot(
        normed_two_low, up_weight, preferred_element_type=jnp.float32
    ) + up_bias.astype(jnp.float32)
    active_low = jax.nn.gelu(hidden).astype(jnp.bfloat16)
    result = (
        middle
        + jnp.dot(active_low, down_weight, preferred_element_type=jnp.float32)
        + down_bias.astype(jnp.float32)
    )
    layer_out = result.astype(jnp.bfloat16)[None]
    cot_low = out_cotangent[0]
    cot_f = cot_low.astype(jnp.float32)
    grad_down_w = outer_sum(active_low, cot_low)
    grad_down_b = jnp.sum(cot_f, 0)
    d_active = times_transposed(cot_low, down_weight)
    hidden_unused, gelu_back = jax.vjp(jax.nn.gelu, hidden)
    d_hidden = gelu_back(d_active)[0].astype(jnp.bfloat16)
    grad_up_w = outer_sum(normed_two_low, d_hidden)
    grad_up_b = jnp.sum(d_hidden.astype(jnp.float32), 0)
    d_normed_two = times_transposed(d_hidden, up_weight)
    d_mid_norm, grad_mlp_gain, grad_mlp_shift = norm_back(
        d_normed_two, hat_two, inv_two, mlp_gain_f
    )
    d_middle = cot_f + d_mid_norm
    d_branch = d_middle.astype(jnp.bfloat16)
    grad_proj_w = outer_sum(attended_low, d_branch)
    grad_proj_b = jnp.sum(d_branch.astype(jnp.float32), 0)
    d_attended = (
        times_transposed(d_branch, proj_weight).astype(jnp.bfloat16).reshape(tok_rows, H, HD)
    )
    delta = jnp.einsum("qhd,qhd->hq", d_attended.astype(jnp.float32), attended_f)

    def back_step(state, sliced, first_key):
        dq_acc, buffers = state
        keys_blk, values_blk = sliced
        key_count = keys_blk.shape[0]
        scores, allowed = block_scores(keys_blk, first_key)
        weights = jnp.where(allowed, jnp.exp(scores - log_sum[:, :, None]), 0.0)
        d_weights = jnp.einsum(
            "qhd,khd->hqk",
            d_attended,
            values_blk.reshape(key_count, H, HD),
            preferred_element_type=jnp.float32,
        )
        d_scores = (weights * (d_weights - delta[:, :, None])).astype(jnp.bfloat16)
        dq_acc = dq_acc + 0.125 * jnp.einsum(
            "hqk,khd->qhd",
            d_scores,
            keys_blk.reshape(key_count, H, HD),
            preferred_element_type=jnp.float32,
        )
        d_keys = 0.125 * jnp.einsum(
            "hqk,qhd->khd", d_scores, query_h, preferred_element_type=jnp.float32
        )
        d_values = jnp.einsum(
            "hqk,qhd->khd",
            weights.astype(jnp.bfloat16),
            d_attended,
            preferred_element_type=jnp.float32,
        )
        key_buffer = add_rows(buffers[0], d_keys.reshape(key_count, model_width), first_key)
        value_buffer = add_rows(buffers[1], d_values.reshape(key_count, model_width), first_key)
        buffers = (key_buffer, value_buffer)
        return (dq_acc, buffers)

    buffer_init = (
        jnp.zeros((seq_len, model_width), jnp.float32),
        jnp.zeros((seq_len, model_width), jnp.float32),
    )
    back_init = (jnp.zeros((tok_rows, H, HD), jnp.float32), buffer_init)
    d_queries, key_grads = in_blocks(
        back_step,
        back_init,
        (
            lax.all_gather(key_low, "blk", axis=0, tiled=True),
            lax.all_gather(value_low, "blk", axis=0, tiled=True),
        ),
    )
    d_keys_own, d_values_own = (
        lax.psum_scatter(key_grads[0], "blk", scatter_dimension=0, tiled=True),
        lax.psum_scatter(key_grads[1], "blk", scatter_dimension=0, tiled=True),
    )
    d_queries_pre = rotate(d_queries, cos_tab, -sin_tab).reshape(tok_rows, model_width)
    d_keys_pre = rotate(d_keys_own.reshape(tok_rows, H, HD), cos_tab, -sin_tab).reshape(
        tok_rows, model_width
    )
    d_mixed = jnp.concatenate([d_queries_pre, d_keys_pre, d_values_own], axis=1).astype(
        jnp.bfloat16
    )
    grad_qkv_w = outer_sum(normed_low, d_mixed)
    grad_qkv_b = jnp.sum(d_mixed.astype(jnp.float32), 0)
    d_normed = times_transposed(d_mixed, qkv_weight)
    d_res_norm, grad_attn_gain, grad_attn_shift = norm_back(d_normed, hat_one, inv_one, attn_gain_f)
    tokens_grad = (d_middle + d_res_norm)[None]
    summed = (
        lax.psum_scatter(grad_qkv_w, ("batch", "blk"), scatter_dimension=0, tiled=True),
        lax.psum_scatter(grad_proj_w, ("batch", "blk"), scatter_dimension=0, tiled=True),
        lax.psum_scatter(grad_up_w, ("batch", "blk"), scatter_dimension=0, tiled=True),
        lax.psum_scatter(grad_down_w, ("batch", "blk"), scatter_dimension=0, tiled=True),
        lax.psum_scatter(grad_attn_gain, ("batch", "blk"), scatter_dimension=0, tiled=True),
        lax.psum_scatter(grad_attn_shift, ("batch", "blk"), scatter_dimension=0, tiled=True),
        lax.psum_scatter(grad_qkv_b, ("batch", "blk"), scatter_dimension=0, tiled=True),
        lax.psum_scatter(grad_proj_b, ("batch", "blk"), scatter_dimension=0, tiled=True),
        lax.psum_scatter(grad_mlp_gain, ("batch", "blk"), scatter_dimension=0, tiled=True),
        lax.psum_scatter(grad_mlp_shift, ("batch", "blk"), scatter_dimension=0, tiled=True),
        lax.psum_scatter(grad_up_b, ("batch", "blk"), scatter_dimension=0, tiled=True),
        lax.psum_scatter(grad_down_b, ("batch", "blk"), scatter_dimension=0, tiled=True),
    )
    return (
        layer_out,
        tokens_grad,
        summed[4],
        summed[5],
        summed[0],
        summed[6],
        summed[1],
        summed[7],
        summed[8],
        summed[9],
        summed[2],
        summed[10],
        summed[3],
        summed[11],
    )


BF = jnp.bfloat16
F32 = jnp.float32
AXES = ("x", "core", "zh", "zl", "y")
ROW = ("zh", "zl", "y")
GELU_A = 0.7978845608028654
GELU_B = 0.044715
VMEM_MIB = 32
PIN = 400000
LOW_PIN = 200000
NO_PIN = 1 << 30


def mm(left, right):
    return jnp.dot(left, right, preferred_element_type=F32)


def swap_over(value, *names):
    mask = sum(16 >> AXES.index(name) for name in names)
    return lax.ppermute(value, AXES, [(i, i ^ mask) for i in range(32)])


def whole(shape):
    zeros = (0,) * len(shape)
    return pl.BlockSpec(shape, lambda *_: zeros)


def arr(shape, dtype):
    return jax.ShapeDtypeStruct(shape, dtype)


def call(
    body, grid, in_specs, out_specs, out_shape, scratch, pin, scalars, args, out_pin=None
):
    return pl.pallas_call(
        body,
        grid_spec=pltpu.PrefetchScalarGridSpec(
            num_scalar_prefetch=1,
            grid=grid,
            in_specs=in_specs,
            out_specs=out_specs,
            scratch_shapes=scratch,
        ),
        out_shape=[pltpu.HBM(o.shape, o.dtype) if big(o, out_pin or pin) else o for o in out_shape],
        compiler_params=pltpu.CompilerParams(vmem_limit_bytes=VMEM_MIB << 20),
        cost_estimate=pl.CostEstimate(flops=0, bytes_accessed=1024, transcendentals=0),
    )(scalars, *(pinned(v, pin) for v in args))


def big(v, pin):
    return math.prod(v.shape) * v.dtype.itemsize >= pin


def pinned(v, pin):
    return pltpu.with_memory_space_constraint(v, pltpu.HBM) if big(v, pin) else v


def one_step(body, outs, scratch, pin, scalars, args, out_pin=None):
    return call(
        body, (1,), [whole(v.shape) for v in args], [whole(o.shape) for o in outs], outs, scratch,
        pin, scalars, args, out_pin,
    )


def standardize(x):
    mean = jnp.mean(x, -1, keepdims=True)
    centered = x - mean
    inv = lax.rsqrt(jnp.mean(centered * centered, -1, keepdims=True) + 1e-06)
    return centered * inv, inv


def swap_halves(x):
    lane = lax.broadcasted_iota(jnp.int32, x.shape, 1)
    return jnp.where(lane % 64 < 32, pltpu.roll(x, 96, 1), pltpu.roll(x, 32, 1))


def gelu_both(h):
    t = jnp.tanh(h * (GELU_A + (GELU_A * GELU_B) * (h * h)))
    half = 0.5 * h
    act = half + half * t
    slope = (0.5 + 0.5 * t) + half * (1.0 - t * t) * (GELU_A + (3.0 * GELU_A * GELU_B) * (h * h))
    return act, slope


def down_back_body(place, cot, down, d_act, bias_part):
    @pl.when(pl.program_id(0) == 0)
    def _():
        bias_part[...] = jnp.sum(cot[...].astype(F32), 0, keepdims=True)

    d_act[...] = times_transposed(cot[...], down[...])


def qkv_half(place, blocks, vecs, ws, cos, sin, hat_out, normed):
    g = vecs[0:1, :]
    s = vecs[1:2, :]
    for j in range(4):
        rows = slice(128 * j, 128 * j + 128)
        hat, _ = standardize(blocks[j][...].astype(F32))
        hat_out[rows, :] = hat.astype(BF)
        normed[rows, :] = (hat * g + s).astype(BF)
    lanes = pl.ds(pl.multiple_of(place[0] * 128, 128), 128)
    bias3 = jnp.concatenate([vecs[12 + p : 13 + p, lanes] for p in range(3)], 1)
    mixed = mm(normed[...], jnp.concatenate([w[...] for w in ws], 1)) + bias3
    c = cos[...]
    sn = sin[...]
    q = mixed[:, :128]
    k = mixed[:, 128:256]
    return (
        ((q * c + swap_halves(q) * sn) * 0.125).astype(BF),
        (k * c + swap_halves(k) * sn).astype(BF),
        mixed[:, 256:].astype(BF),
    )


def near_body(place, *refs):
    blocks = refs[:4]
    vecs, wq, wk, wv, cos, sin, hat_out, q_out, k_out, v_out, normed = refs[4:]
    q, k, v = qkv_half(place, blocks, vecs, (wq, wk, wv), cos, sin, hat_out, normed)
    q_out[...] = q
    k_out[...] = k
    v_out[...] = v


def far_body(place, *refs):
    blocks = refs[:4]
    vecs, wq, wk, wv, cos, sin, q0, k0, v0, hat_out, q_out, k_out, v_out, normed = refs[4:]
    q, k, v = qkv_half(place, blocks, vecs, (wq, wk, wv), cos, sin, hat_out, normed)
    for out, near, far in ((q_out, q0, q), (k_out, k0, k), (v_out, v0, v)):
        out[:512, :] = near[...]
        out[512:, :] = far


def head_mask(shape, head):
    return lax.broadcasted_iota(jnp.int32, shape, 1) // 64 == head


def attend_body(place, q, k_all, v_all, id_col, id_row, att_f, att_low, probs, row_scale):
    keys = k_all[...]
    values = v_all[...]
    queries = q[...]
    own = id_col[...]
    allowed = jnp.concatenate([own, own], 1) == id_row[0:1, :]
    halves, scales = [], []
    for head in range(2):
        mine = jnp.where(head_mask(queries.shape, head), queries, jnp.zeros_like(queries))
        scores = jnp.where(allowed, times_transposed(keys, mine), NEG_FILL)
        weights = jnp.exp(scores - jnp.max(scores, 0, keepdims=True))
        low = weights.astype(BF)
        probs[head] = low
        scale = 1.0 / jnp.sum(weights, 0, keepdims=True)
        scales.append(scale)
        halves.append(outer_sum(values, low)[64 * head : 64 * head + 64] * scale)
    out = jnp.concatenate(halves, 0).T
    att_f[...] = out
    row_scale[...] = jnp.concatenate([jnp.broadcast_to(v, (64, 256)) for v in scales], 0).T
    step = pl.program_id(0)
    att_low[place[0] ^ (2 * step)] = out[:128].astype(BF)
    att_low[place[0] ^ (2 * step + 1)] = out[128:].astype(BF)


def proj_body(place, att, tok, proj_w, vecs, middle, normed, att_rows):
    rows = jnp.concatenate([att[k] for k in range(8)], 1)
    att_rows[...] = rows
    mid = tok[...].astype(F32) + mm(rows, proj_w[...]) + vecs[2:3, :]
    middle[...] = mid
    hat, _ = standardize(mid)
    low = (hat * vecs[3:4, :] + vecs[4:5, :]).astype(BF)
    normed[...] = low


def proj_grad(place, att, d_b, vectors, send, keep):
    grad = outer_sum(att, d_b)
    row = lax.broadcasted_iota(jnp.int32, (32, 128), 0)
    for owner in range(32):
        x, core, k = owner // 16, (owner // 8) % 2, owner % 8
        rows = grad[32 * owner : 32 * owner + 32]
        extra = jnp.zeros((32, 128), F32)
        first = 128 * (owner // 4)
        for m in range(4):
            extra = jnp.where(row == m, vectors[m : m + 1, first : first + 128], extra)
        group = 2 * x + core
        last = vectors[4 + group : 5 + group, 128 * k : 128 * k + 128]
        extra = jnp.where(row == 4, last, extra)
        rel = place[0] ^ k
        slot = (rel & 1) * 4 + (rel >> 2) * 2 + ((rel >> 1) & 1)
        for side, out in ((core == place[2], keep), (core != place[2], send)):

            @pl.when(side)
            def _():
                out[place[1] ^ x, slot, :, :1024] = rows.astype(BF)
                out[place[1] ^ x, slot, :, 1024:] = extra.astype(BF)


def mlp_body(
    place, normed, d_act, up_w, vecs, middle, cot, proj_w, down_bias, att,
    active, d_mid, d_att, proj_send, proj_keep, acc, vectors,
):
    step = pl.program_id(0)
    hidden = mm(normed[...], up_w[...]) + vecs[pl.ds(8 + step, 1), :]
    act, slope = gelu_both(hidden)
    active[...] = act.astype(BF)
    d_hidden = (d_act[...] * slope).astype(BF)
    vectors[pl.ds(4 + step, 1), :] = jnp.sum(d_hidden.astype(F32), 0, keepdims=True)
    part = times_transposed(d_hidden, up_w[...])

    @pl.when(step == 0)
    def _():
        acc[...] = part

    @pl.when(step > 0)
    def _():
        acc[...] += part

    @pl.when(step == pl.num_programs(0) - 1)
    def _():
        up = acc[...]
        hat, inv = standardize(middle[...])
        e = up * vecs[3:4, :]
        inner = e - jnp.mean(e, -1, keepdims=True) - hat * jnp.mean(e * hat, -1, keepdims=True)
        d_m = cot[...].astype(F32) + inv * inner
        d_mid[...] = d_m
        d_b = d_m.astype(BF)
        vectors[0:1, :] = jnp.sum(up * hat, 0, keepdims=True)
        vectors[1:2, :] = jnp.sum(up, 0, keepdims=True)
        vectors[2:3, :] = jnp.sum(d_b.astype(F32), 0, keepdims=True)
        vectors[3:4, :] = down_bias[...]
        d_a = times_transposed(d_b, proj_w[...]).astype(BF)
        for k in range(8):
            d_att[k] = d_a[:, 128 * k : 128 * k + 128]
        proj_grad(place, att[...], d_b, vectors, proj_send, proj_keep)


def mlp_grad_body(place, *refs):
    blocks, cots, ups, downs = refs[:8], refs[8:16], refs[16:20], refs[20:24]
    vecs, down_keep, down_send, up_keep, up_send, n_all, c_all, u_all, d_all, grad = refs[24:]
    for j in range(8):
        n_all[128 * j : 128 * j + 128, :] = blocks[j][...]
        c_all[128 * j : 128 * j + 128, :] = cots[j][...]
    lanes = pl.ds(pl.multiple_of(place[0] * 128, 128), 128)
    up_b = []
    rows = vecs[8:12, lanes]
    biases = lax.broadcasted_iota(jnp.int32, (4, 128), 0)
    for g in range(4):
        u_all[:, 128 * g : 128 * g + 128] = ups[g][...]
        d_all[128 * g : 128 * g + 128, :] = downs[g][...]
        group = (place[1] ^ (g & 1)) * 2 + (place[2] ^ (g >> 1))
        up_b.append(jnp.sum(jnp.where(biases == group, rows, 0.0), 0, keepdims=True))
    n = n_all[...]
    c = c_all[...]
    act, slope = gelu_both(mm(n, u_all[...]) + jnp.concatenate(up_b, 1))
    grad_down = outer_sum(act.astype(BF), c)
    for g in range(4):
        rows = grad_down[128 * g : 128 * g + 128]
        if g < 2:
            down_keep[g] = rows.astype(BF)
        else:
            down_send[g - 2] = rows.astype(BF)
    d_hidden = (times_transposed(c, d_all[...]) * slope).astype(BF)
    both = outer_sum(n, d_hidden)
    for g in range(4):
        group = ((place[1] ^ (g & 1)) * 2) + (place[2] ^ (g >> 1))
        lanes = pl.ds(pl.multiple_of(group * 128, 128), 128)
        grad[:, lanes] = both[:, 128 * g : 128 * g + 128]
    for rx in range(2):
        first = (place[1] ^ rx) * 512
        keep = pl.multiple_of(first + place[2] * 256, 256)
        send = pl.multiple_of(first + (1 - place[2]) * 256, 256)
        up_keep[rx] = grad[pl.ds(keep, 256), :].astype(BF)
        up_send[rx] = grad[pl.ds(send, 256), :].astype(BF)


def attend_back_body(
    place, probs, d_att, att_f, row_scale, q, k_all, v_all, cos, sin, d_all, bias_part, dq, dk, dv
):
    step = pl.program_id(0)
    keys = k_all[...]
    values = v_all[...]
    queries = q[...]
    d_out = jnp.concatenate([d_att[place[0] ^ (2 * step)], d_att[place[0] ^ (2 * step + 1)]], 0)
    scaled = d_out.astype(F32) * row_scale[...]
    d_out = scaled.astype(BF)
    products = (d_out.astype(F32) * att_f[...]).T
    key_parts, value_parts, query_parts = [], [], []
    for head in range(2):
        weights = probs[head]
        mine = jnp.where(head_mask(d_out.shape, head), d_out, jnp.zeros_like(d_out))
        delta = jnp.sum(products[64 * head : 64 * head + 64], 0, keepdims=True)
        d_weights = times_transposed(values, mine)
        d_scores = (weights.astype(F32) * (d_weights - delta)).astype(BF)
        key_parts.append(mm(d_scores, queries))
        value_parts.append(mm(weights, d_out))
        query_parts.append(outer_sum(keys, d_scores)[64 * head : 64 * head + 64])
    first = head_mask((1024, 128), 0)
    dk_new = jnp.where(first, key_parts[0], key_parts[1])
    dv_new = jnp.where(first, value_parts[0], value_parts[1])
    dq[pl.ds(pl.multiple_of(step * 256, 256), 256), :] = jnp.concatenate(query_parts, 0).T

    @pl.when(step == 0)
    def _():
        dk[...] = dk_new
        dv[...] = dv_new

    @pl.when(step > 0)
    def _():
        dk[...] += dk_new
        dv[...] += dv_new

    @pl.when(step == pl.num_programs(0) - 1)
    def _():
        total = jnp.zeros((1, 384), F32)
        for j in range(8):
            rows = slice(128 * j, 128 * j + 128)
            c = cos[rows, :]
            sn = sin[rows, :]
            back_q = 0.125 * dq[rows, :]
            back_k = dk[rows, :]
            piece = jnp.concatenate(
                [
                    back_q * c - swap_halves(back_q) * sn,
                    back_k * c - swap_halves(back_k) * sn,
                    dv[rows, :],
                ],
                1,
            ).astype(BF)
            d_all[place[0] ^ j] = piece
            total = total + jnp.sum(piece.astype(F32), 0, keepdims=True)
        bias_part[...] = total


def rel_block(step, place):
    rel = jnp.where(step < 2, 2, 0) + step % 2
    return ((rel & 1) ^ place[1]) * 2 + ((rel >> 1) ^ place[2])


def qkv_grad_body(place, h0, h1, d_all, bias_part, vecs, wq, wk, wv, send, keep):
    step = pl.program_id(0)
    d_near = jnp.concatenate([d_all[place[0] ^ j] for j in range(4)], 0)
    d_far = jnp.concatenate([d_all[place[0] ^ j] for j in range(4, 8)], 0)
    inner = outer_sum(h0[...], d_near) + outer_sum(h1[...], d_far)
    total = bias_part[...]
    w = jnp.concatenate([wq[...], wk[...], wv[...]], 1).astype(F32)
    columns = vecs[...].T
    gain = columns[:, 0:1]
    shift = columns[:, 1:2]
    grad = gain * inner + shift * total
    row = lax.broadcasted_iota(jnp.int32, (256, 128), 0) % 32
    lane = lax.broadcasted_iota(jnp.int32, (256, 128), 1)
    extra = jnp.where(
        lane == 0,
        jnp.sum(w * inner, 1, keepdims=True),
        jnp.where(lane == 1, jnp.sum(w * total, 1, keepdims=True), 0.0),
    )
    for m in range(6):
        part = total[:, 128 * (m // 2) : 128 * (m // 2) + 128]
        part = part if m % 2 else pltpu.roll(part, 64, 1)
        extra = jnp.where((row == m) & (lane >= 64), part, extra)

    @pl.when(step < 2)
    def _():
        send[0, :, :384] = grad.astype(BF)
        send[0, :, 384:] = extra.astype(BF)

    @pl.when(step >= 2)
    def _():
        keep[0, :, :384] = grad.astype(BF)
        keep[0, :, 384:] = extra.astype(BF)


def pair_body(place, keep, came, left, send):
    half = left.shape[0]
    total = (keep[...].astype(F32) + came[...].astype(F32)).astype(BF)
    left[...] = total[:half]
    send[...] = total[half:]


def add_body(place, left, came, out):
    out[...] = (left[...].astype(F32) + came[...].astype(F32)).astype(BF)


def merge_body(place, *refs):
    keeps, cames = refs[0:6:2], refs[1:6:2]
    proj_left, proj_came, left, send, down_left, down_send, proj_keep, proj_send = refs[6:]
    proj_keep[...] = (proj_left[:2].astype(F32) + proj_came[:2].astype(F32)).astype(BF)
    proj_send[...] = (proj_left[2:].astype(F32) + proj_came[2:].astype(F32)).astype(BF)
    for side, low, down in ((0, left, down_left), (1, send, down_send)):
        for m in range(2):
            total = keeps[m][side].astype(F32) + cames[m][side].astype(F32)
            for k in range(8):
                low[k, 32 * m : 32 * m + 32, :] = total[32 * k : 32 * k + 32].astype(BF)
        down[...] = (keeps[2][side].astype(F32) + cames[2][side].astype(F32)).astype(BF)


def finish_body(place, came, grad_up, grad_qkv, sums, bias):
    total = jnp.zeros((32, 128), F32)
    low = lax.broadcasted_iota(jnp.int32, (1, 128), 1) < 64
    for k in range(8):
        for g in range(4):
            lanes = slice(1024 * g + 128 * k, 1024 * g + 128 * k + 128)
            grad_up[:, lanes] = came[k, :32, 128 * g : 128 * g + 128].astype(F32)
            if g < 3:
                grad_qkv[:, lanes] = came[k, 32:, 128 * g : 128 * g + 128].astype(F32)
        extra = came[k, 32:, 384:].astype(F32)
        total = total + extra
        for p in range(3):
            left = pltpu.roll(extra[2 * p : 2 * p + 1], 64, 1)
            both = jnp.where(low, left, extra[2 * p + 1 : 2 * p + 2])
            bias[p : p + 1, 128 * k : 128 * k + 128] = both
    sums[...] = total.T[:8]


def out_body(place, active, down, middle, vecs, out, acc):
    step = pl.program_id(0)
    part = mm(active[...], down[...])

    @pl.when(step == 0)
    def _():
        acc[...] = part + middle[...] + vecs[5:6, :]

    @pl.when(step > 0)
    def _():
        acc[...] += part

    @pl.when(step == pl.num_programs(0) - 1)
    def _():
        out[...] = acc[...].astype(BF)


def last_body(place, came, w, tok, d_mid, vecs, out, acc):
    step = pl.program_id(0)
    for p in range(3):

        @pl.when(step == p)
        def _():
            d_mixed = jnp.concatenate([came[k, :, 128 * p : 128 * p + 128] for k in range(8)], 1)
            part = times_transposed(d_mixed, w[...])
            if p == 0:
                acc[...] = part
            elif p == 1:
                acc[...] += part
            else:
                up = acc[...] + part
                hat, inv = standardize(tok[...].astype(F32))
                e = up * vecs[0:1, :]
                mean = jnp.mean(e, -1, keepdims=True)
                inner = e - mean - hat * jnp.mean(e * hat, -1, keepdims=True)
                out[...] = d_mid[...] + inv * inner


def frequency_rows():
    rows = np.zeros((8, 128), np.float32)
    for lane in range(128):
        pair = lane % 32
        part, rank, count = (0, pair, 10) if pair < 10 else ((1, pair - 10, 11) if pair < 21 else (2, pair - 21, 11))
        rows[part, lane] = 10000.0 ** (-rank / count)
        rows[3, lane] = -1.0 if lane % 64 < 32 else 1.0
    return rows


def clip_starts(place, pos):
    ids = jnp.zeros_like(pos)
    start = jnp.zeros_like(pos)
    end = jnp.int32(0)
    for c in range(8):
        length = place[8 + c]
        end = end + length
        past = pos >= end.astype(F32)
        ids = jnp.where(past, ids + 1.0, ids)
        start = jnp.where(past, end.astype(F32), start)
    return ids, start


def prep_body(place, freq, cos, sin, id_col, id_row):
    for j in range(8):
        first = ((place[0] ^ j) * 128).astype(F32)
        rows = slice(128 * j, 128 * j + 128)
        pos = first + lax.broadcasted_iota(jnp.int32, (128, 128), 0).astype(F32)
        ids, start = clip_starts(place, pos)
        id_col[rows, :] = ids
        within = pos - start
        row14 = jnp.floor((within + 0.5) * (1.0 / 14.0))
        t = jnp.floor((within + 0.5) * (1.0 / 196.0))
        angle = t * freq[0:1, :] + (row14 - 14.0 * t) * freq[1:2, :] + (within - 14.0 * row14) * freq[2:3, :]
        cos[rows, :] = jnp.cos(angle)
        sin[rows, :] = jnp.sin(angle) * freq[3:4, :]
        flat = first + lax.broadcasted_iota(jnp.int32, (8, 128), 1).astype(F32)
        id_row[:, 128 * j : 128 * j + 128] = clip_starts(place, flat)[0]


def after(value, *others):
    return lax.optimization_barrier((value, *others))[0]


def spread_four(a):
    return [a, swap_over(a, "y"), swap_over(a, "zl"), swap_over(a, "zl", "y")]


def fast_shards(
    tokens_in, clip_lengths, attn_gain, attn_shift, qkv_weight, qkv_bias, proj_weight, proj_bias,
    mlp_gain, mlp_shift, up_weight, up_bias, down_weight, down_bias, out_cotangent,
):
    x, core, zh, zl, y = (lax.axis_index(name) for name in AXES)
    k = zh * 4 + zl * 2 + y
    me = x * 16 + core * 8 + k
    place = jnp.concatenate(
        [jnp.stack([k, x, core, k, k, k, k, k]).astype(jnp.int32), clip_lengths[0]]
    )
    tok = tokens_in[0]
    cot = out_cotangent[0]

    far_tok = swap_over(tok, "zh")
    near = spread_four(tok)
    rows = [attn_gain, attn_shift, proj_bias, mlp_gain, mlp_shift, down_bias, down_bias, down_bias]
    vecs = jnp.concatenate([v.astype(F32).reshape(-1, 1024) for v in (*rows, up_bias, qkv_bias)], 0)
    cos_tab, sin_tab, id_col, id_row = one_step(
        prep_body,
        [arr((1024, 128), F32), arr((1024, 128), F32), arr((1024, 128), F32), arr((8, 1024), F32)],
        [],
        PIN,
        place,
        (jnp.asarray(frequency_rows()),),
    )
    far_tok, cos_tab, vecs, *near = lax.optimization_barrier((far_tok, cos_tab, vecs, *near))
    far = spread_four(far_tok)

    def table_half(part):
        return pl.BlockSpec((512, 128), lambda i, s: (part, 0))

    half = arr((512, 128), BF)
    full = arr((1024, 128), BF)
    common = (vecs, qkv_weight, qkv_weight, qkv_weight, cos_tab, sin_tab)
    columns_of = [pl.BlockSpec((1024, 128), lambda i, s, p=p: (0, 8 * p + s[0])) for p in range(3)]

    def qkv(body, part, blocks, more, outs):
        specs = [whole(v.shape) for v in (*blocks, vecs)] + columns_of
        specs += [table_half(part), table_half(part)] + [whole(v.shape) for v in more]
        return call(
            body, (1,), specs, [whole(o.shape) for o in outs], outs,
            [pltpu.VMEM((512, 1024), BF)], PIN, place, (*blocks, *common, *more),
        )

    hat0, q0, k0, v0 = qkv(near_body, 0, near, (), [arr((512, 1024), BF), half, half, half])
    d_act, down_bias_part = call(
        down_back_body,
        (4,),
        [whole((128, 1024)), pl.BlockSpec((1024, 1024), lambda i, s: (i, 0))],
        [pl.BlockSpec((128, 1024), lambda i, s: (0, i)), whole((1, 1024))],
        [arr((128, 4096), F32), arr((1, 1024), F32)],
        [],
        PIN,
        place,
        (after(cot, q0), down_weight),
    )
    far = lax.optimization_barrier((q0, d_act, *far))[2:]
    cot_here = after(cot, q0)
    far_cot = swap_over(cot_here, "zh")
    cots = spread_four(cot_here)
    hat1, q_all, k_all, v_all = qkv(
        far_body, 1, far, (q0, k0, v0), [arr((512, 1024), BF), full, full, full]
    )
    step_rows = pl.BlockSpec((256, 128), lambda i, s: (i, 0))
    flat = whole((1024, 128))
    att_f, att_low, probs, row_scale = call(
        attend_body,
        (4,),
        [
            step_rows, flat, flat, flat, pl.BlockSpec((8, 256), lambda i, s: (0, i)),
        ],
        [step_rows, whole((8, 128, 128)), pl.BlockSpec((2, 1024, 256), lambda i, s: (0, 0, i)),
         step_rows],
        [arr((1024, 128), F32), arr((8, 128, 128), BF), arr((2, 1024, 1024), BF),
         arr((1024, 128), F32)],
        [],
        PIN,
        place,
        (q_all, k_all, v_all, id_col, id_row),
    )
    att_low, far_cot, *cots = lax.optimization_barrier((att_low, far_cot, *cots))
    att_in = lax.all_to_all(att_low, ROW, 0, 0, tiled=True)
    cots += [far_cot, swap_over(far_cot, "y"), swap_over(far_cot, "zl")]
    middle, normed2, att_rows = one_step(
        proj_body,
        [arr((128, 1024), F32), arr((128, 1024), BF), arr((128, 1024), BF)],
        [],
        PIN,
        place,
        (att_in, tok, proj_weight, vecs),
        LOW_PIN,
    )
    normed2, *cots = lax.optimization_barrier((normed2, *cots))
    far_n = swap_over(normed2, "zh")
    near_n = spread_four(normed2)
    wide = pl.BlockSpec((128, 1024), lambda i, s: (0, i))
    fixed = whole((128, 1024))
    active, d_mid, d_att, proj_send, proj_keep = call(
        mlp_body,
        (4,),
        [
            fixed, wide, wide_columns(), whole((15, 1024)), fixed, fixed, whole((1024, 1024)),
            whole((1, 1024)), fixed,
        ],
        [wide, fixed, whole((8, 128, 128)), whole((2, 8, 32, 1152)), whole((2, 8, 32, 1152))],
        [
            arr((128, 4096), BF), arr((128, 1024), F32), arr((8, 128, 128), BF),
            arr((2, 8, 32, 1152), BF), arr((2, 8, 32, 1152), BF),
        ],
        [pltpu.VMEM((128, 1024), F32), pltpu.VMEM((8, 1024), F32)],
        LOW_PIN,
        place,
        (normed2, d_act, up_weight, vecs, middle, cot, proj_weight, down_bias_part, att_rows),
    )
    d_att, far_n, far_y, active, proj_send, *near_n = lax.optimization_barrier(
        (d_att, far_n, cots[5], active, proj_send, *near_n)
    )
    last_cot = swap_over(far_y, "zl")
    d_att_in = lax.all_to_all(d_att, ROW, 0, 0, tiled=True)

    far_n = spread_four(far_n)

    def pair(keep, came):
        half = arr((keep.shape[0] // 2, *keep.shape[1:]), BF)
        return one_step(pair_body, [half, half], [], NO_PIN, place, (keep, came))

    flat_proj = (16, 32, 1152)
    proj_left, proj_low = pair(
        proj_keep.reshape(flat_proj), swap_over(proj_send.reshape(flat_proj), "core")
    )

    d_all, qkv_bias_part = call(
        attend_back_body,
        (4,),
        [
            pl.BlockSpec((2, 1024, 256), lambda i, s: (0, 0, i)), whole((8, 128, 128)), step_rows,
            step_rows, step_rows, flat, flat, flat, flat,
        ],
        [whole((8, 128, 384)), whole((1, 384))],
        [arr((8, 128, 384), BF), arr((1, 384), F32)],
        [pltpu.VMEM((1024, 128), F32)] * 3,
        PIN,
        place,
        (probs, after(d_att_in, proj_low), att_f, row_scale, q_all, k_all, v_all, cos_tab, sin_tab),
    )
    block_of = lambda i, s: (rel_block(i, s), 0)
    lanes_of = lambda i, s: (0, rel_block(i, s))
    send, keep = call(
        qkv_grad_body,
        (4,),
        [
            pl.BlockSpec((512, 256), lanes_of), pl.BlockSpec((512, 256), lanes_of),
            whole((8, 128, 384)), whole((1, 384)), pl.BlockSpec((8, 256), lanes_of),
        ]
        + [pl.BlockSpec((256, 128), lambda i, s, p=p: (rel_block(i, s), 8 * p + s[0])) for p in range(3)],
        [
            pl.BlockSpec((1, 256, 512), lambda i, s: (jnp.minimum(i, 1), 0, 0)),
            pl.BlockSpec((1, 256, 512), lambda i, s: (jnp.maximum(i - 2, 0), 0, 0)),
        ],
        [arr((2, 256, 512), BF), arr((2, 256, 512), BF)],
        [],
        PIN,
        place,
        (hat0, hat1, d_all, qkv_bias_part, vecs, qkv_weight, qkv_weight, qkv_weight),
    )
    def turn(value):
        return lax.all_to_all(value, ROW, 0, 0, tiled=True)
    d_all, send, last_cot, *far_n = lax.optimization_barrier((d_all, send, last_cot, *far_n))
    moved = lax.all_to_all(d_all, ROW, 0, 0, tiled=True)
    proj_left, proj_low = pair(after(proj_left, d_all), swap_over(proj_low, "x"))

    def group_of(s, g):
        return (s[1] ^ (g & 1)) * 16 + (s[2] ^ (g >> 1)) * 8 + s[0]

    outs = [
        arr((2, 128, 1024), BF), arr((2, 128, 1024), BF), arr((2, 256, 512), BF),
        arr((2, 256, 512), BF),
    ]
    down_keep, down_send, up_keep, up_send = call(
        mlp_grad_body,
        (1,),
        [fixed] * 16
        + [pl.BlockSpec((1024, 128), lambda i, s, g=g: (0, group_of(s, g))) for g in range(4)]
        + [pl.BlockSpec((128, 1024), lambda i, s, g=g: (group_of(s, g), 0)) for g in range(4)]
        + [whole((15, 1024))],
        [whole(o.shape) for o in outs],
        outs,
        [
            pltpu.VMEM((1024, 1024), BF), pltpu.VMEM((1024, 1024), BF),
            pltpu.VMEM((1024, 512), BF), pltpu.VMEM((512, 1024), BF), pltpu.VMEM((1024, 512), F32),
        ],
        LOW_PIN,
        place,
        (after(near_n[0], d_all, proj_low), *near_n[1:], *far_n, *cots, last_cot, *([up_weight] * 4), *([down_weight] * 4), vecs),
    )


    up_send, down_send, proj_came = lax.optimization_barrier(
        (up_send, down_send, swap_over(proj_low, "y"))
    )
    left, low_send, down_left, down_low, proj_left, proj_low = one_step(
        merge_body,
        [arr((8, 64, 512), BF)] * 2 + [arr((128, 1024), BF)] * 2 + [arr((2, 32, 1152), BF)] * 2,
        [],
        PIN,
        place,
        (
            after(up_keep, moved), swap_over(up_send, "core"), keep, swap_over(send, "core"),
            down_keep, swap_over(down_send, "core"), proj_left, proj_came,
        ),
        NO_PIN,
    )
    low_came = swap_over(low_send, "x")
    (tokens_grad,) = call(
        last_body,
        (3,),
        [
            whole((8, 128, 384)), pl.BlockSpec((1024, 1024), lambda i, s: (0, i)), fixed, fixed,
            whole((15, 1024)),
        ],
        [fixed],
        [arr((128, 1024), F32)],
        [pltpu.VMEM((128, 1024), F32)],
        PIN,
        place,
        (after(moved, left), qkv_weight, tok, d_mid, vecs),
    )

    proj_left, proj_low = pair(after(proj_left, tokens_grad), swap_over(proj_low, "zh"))
    left, proj_low, low_came = lax.optimization_barrier((left, proj_low, low_came))
    (lows,) = one_step(add_body, [arr((8, 64, 512), BF)], [], NO_PIN, place, (left, low_came))
    lows, proj_low = lax.optimization_barrier((lows, proj_low))
    came = turn(lows)
    proj_came = swap_over(proj_low, "zl")
    down_low, _ = lax.optimization_barrier((down_low, lows))
    grad_down = down_left.astype(F32) + swap_over(down_low, "x").astype(F32)
    proj_total = proj_left[0].astype(F32) + proj_came[0].astype(F32)
    (layer_out,) = call(
        out_body,
        (4,),
        [wide, pl.BlockSpec((1024, 1024), lambda i, s: (i, 0)), fixed, whole((15, 1024))],
        [fixed],
        [arr((128, 1024), BF)],
        [pltpu.VMEM((128, 1024), F32)],
        PIN,
        place,
        (after(active, lows), down_weight, middle, vecs),
    )
    layer_out = layer_out[None]
    grad_proj = proj_total[:, :1024]
    own = lax.dynamic_slice(proj_total[:4, 1024:], (0, (me % 4) * 32), (4, 32))
    grad_up_b = proj_total[4, 1024:]

    grad_up, grad_qkv, sums, bias = one_step(
        finish_body,
        [arr((32, 4096), F32), arr((32, 3072), F32), arr((8, 32), F32), arr((3, 1024), F32)],
        [],
        NO_PIN,
        place,
        (came,),
    )
    grad_qkv_b = lax.dynamic_slice(bias.reshape(3072), (me * 96,), (96,))

    return (
        layer_out, tokens_grad[None], sums[0], sums[1], grad_qkv, grad_qkv_b, grad_proj,
        own[2], own[0], own[1], grad_up, grad_up_b, grad_down, own[3],
    )


def wide_columns():
    return pl.BlockSpec((1024, 1024), lambda i, s: (0, i))


def fast_solution(mesh):
    wide_mesh = Mesh(mesh.devices.reshape(2, 2, 2, 2, 2), AXES)
    batch, blk = AXES[:2], AXES[2:]
    spread = P(batch, blk, None)
    return jax.shard_map(
        fast_shards,
        mesh=wide_mesh,
        in_specs=(spread, P(batch, None)) + (P(),) * 12 + (spread,),
        out_specs=(spread, spread)
        + tuple(P(AXES, None) if i in (2, 4, 8, 10) else P(AXES) for i in range(12)),
        check_vma=False,
    )


def solution(mesh):
    if tuple(mesh.devices.shape) == (4, 8):
        return fast_solution(mesh)
    placed = (
        P("batch", "blk", None),
        P("batch", None),
        P(),
        P(),
        P(),
        P(),
        P(),
        P(),
        P(),
        P(),
        P(),
        P(),
        P(),
        P(),
        P("batch", "blk", None),
    )
    return jax.shard_map(
        shards,
        mesh=mesh,
        in_specs=placed,
        out_specs=(
            P("batch", "blk", None),
            P("batch", "blk", None),
            P(("batch", "blk")),
            P(("batch", "blk")),
            P(("batch", "blk"), None),
            P(("batch", "blk")),
            P(("batch", "blk"), None),
            P(("batch", "blk")),
            P(("batch", "blk")),
            P(("batch", "blk")),
            P(("batch", "blk"), None),
            P(("batch", "blk")),
            P(("batch", "blk"), None),
            P(("batch", "blk")),
        ),
        check_vma=False,
    )
```

```python
import math

import jax
import jax.numpy as jnp
import numpy as np
from jax import lax
from jax.experimental import pallas as pl
from jax.experimental.pallas import tpu as pltpu
from jax.sharding import Mesh
from jax.sharding import PartitionSpec as P

H = 16
HD = 64


NEG_FILL = -1e30


def pair_table():
    part_map = [0] * 10 + [1] * 11 + [2] * 11
    freq_list = [10000.0 ** (-rank / 10.0) for rank in range(10)] + [
        10000.0 ** (-rank / 11.0) for rank in range(11)
    ] * 2
    table_rows = [
        [freq_list[column] if part_map[column] == axis_id else 0.0 for column in range(32)]
        for axis_id in range(3)
    ]
    return jnp.array(table_rows, dtype=jnp.float32)


def clip_of(lengths_row, positions):
    clip_end = jnp.cumsum(lengths_row)
    return jnp.sum((positions[:, None] >= clip_end[None, :]).astype(jnp.int32), axis=1)


def clip_layout(lengths_row, positions):
    clip_end = jnp.cumsum(lengths_row)
    starts = clip_end - lengths_row
    clip_ids = jnp.sum((positions[:, None] >= clip_end[None, :]).astype(jnp.int32), axis=1)
    member = clip_ids[:, None] == jnp.arange(lengths_row.shape[0], dtype=jnp.int32)[None, :]
    within = positions - jnp.sum(jnp.where(member, starts[None, :], 0), axis=1)
    coords = jnp.stack([within // 196, within // 14 % 14, within % 14], axis=1).astype(jnp.float32)
    angles = jnp.dot(coords, pair_table(), precision=lax.Precision.HIGHEST)
    return (clip_ids, jnp.cos(angles), jnp.sin(angles))


def rotate(values, cos_tab, sin_tab):
    half_dim = values.shape[-1] // 2
    first_half = values[..., :half_dim]
    second_half = values[..., half_dim:]
    cos_b = cos_tab[:, None, :]
    sin_b = sin_tab[:, None, :]
    return jnp.concatenate(
        [first_half * cos_b - second_half * sin_b, first_half * sin_b + second_half * cos_b],
        axis=-1,
    )


def norm_fwd(values, gain_vec, shift_vec):
    row_mean = jnp.mean(values, -1, keepdims=True)
    centered = values - row_mean
    inv_std = lax.rsqrt(jnp.mean(centered * centered, -1, keepdims=True) + 1e-06)
    normalized = centered * inv_std
    return (normalized * gain_vec + shift_vec, normalized, inv_std)


def norm_back(upstream, normalized, inv_std, gain_vec):
    scaled = upstream * gain_vec
    inner = (
        scaled
        - jnp.mean(scaled, -1, keepdims=True)
        - normalized * jnp.mean(scaled * normalized, -1, keepdims=True)
    )
    return (inv_std * inner, jnp.sum(upstream * normalized, 0), jnp.sum(upstream, 0))


def outer_sum(left, right):
    return lax.dot_general(
        left, right, (((0,), (0,)), ((), ())), preferred_element_type=jnp.float32
    )


def times_transposed(left, right):
    return lax.dot_general(
        left, right, (((1,), (1,)), ((), ())), preferred_element_type=jnp.float32
    )


def add_rows(buffer, block, first_key):
    current = lax.dynamic_slice_in_dim(buffer, first_key, block.shape[0], 0)
    return lax.dynamic_update_slice_in_dim(buffer, current + block, first_key, 0)


def in_blocks(block_step, running, pieces):
    row_count = pieces[0].shape[0]
    block_rows = math.gcd(row_count, 2048)

    def advance(block_idx, state):
        first_row = block_idx * block_rows
        sliced = tuple(
            (lax.dynamic_slice_in_dim(piece, first_row, block_rows, 0) for piece in pieces)
        )
        return block_step(state, sliced, first_row)

    return lax.fori_loop(0, row_count // block_rows, advance, running)


def shards(
    tokens_in,
    clip_lengths,
    attn_gain,
    attn_shift,
    qkv_weight,
    qkv_bias,
    proj_weight,
    proj_bias,
    mlp_gain,
    mlp_shift,
    up_weight,
    up_bias,
    down_weight,
    down_bias,
    out_cotangent,
):
    tok_rows = tokens_in.shape[1]
    model_width = tokens_in.shape[2]
    seq_len = tok_rows * lax.axis_size("blk")
    lens_row = clip_lengths[0]
    own_pos = lax.axis_index("blk") * tok_rows + jnp.arange(tok_rows, dtype=jnp.int32)
    clip_q, cos_tab, sin_tab = clip_layout(lens_row, own_pos)
    residual = tokens_in[0].astype(jnp.float32)
    attn_gain_f = attn_gain.astype(jnp.float32)
    mlp_gain_f = mlp_gain.astype(jnp.float32)
    normed, hat_one, inv_one = norm_fwd(residual, attn_gain_f, attn_shift.astype(jnp.float32))
    normed_low = normed.astype(jnp.bfloat16)
    qkv_mixed = jnp.dot(
        normed_low, qkv_weight, preferred_element_type=jnp.float32
    ) + qkv_bias.astype(jnp.float32)
    query_h = rotate(qkv_mixed[:, :model_width].reshape(tok_rows, H, HD), cos_tab, sin_tab).astype(
        jnp.bfloat16
    )
    key_low = (
        rotate(
            qkv_mixed[:, model_width : 2 * model_width].reshape(tok_rows, H, HD), cos_tab, sin_tab
        )
        .astype(jnp.bfloat16)
        .reshape(tok_rows, model_width)
    )
    value_low = qkv_mixed[:, 2 * model_width :].astype(jnp.bfloat16)

    def block_scores(keys_blk, first_key):
        key_count = keys_blk.shape[0]
        clip_k = clip_of(lens_row, first_key + jnp.arange(key_count, dtype=jnp.int32))
        raw_scores = jnp.einsum(
            "qhd,khd->hqk",
            query_h,
            keys_blk.reshape(key_count, H, HD),
            preferred_element_type=jnp.float32,
        )
        allowed = (clip_q[:, None] == clip_k[None, :])[None]
        return (jnp.where(allowed, 0.125 * raw_scores, NEG_FILL), allowed)

    def stats_step(state, sliced, first_key):
        row_max, row_sum = state
        scores, allowed = block_scores(sliced[0], first_key)
        new_max = jnp.maximum(row_max, jnp.max(scores, -1))
        weights = jnp.where(allowed, jnp.exp(scores - new_max[:, :, None]), 0.0)
        return (new_max, row_sum * jnp.exp(row_max - new_max) + jnp.sum(weights, -1))

    stats_init = (
        jnp.full((H, tok_rows), NEG_FILL, jnp.float32),
        jnp.zeros((H, tok_rows), jnp.float32),
    )
    row_max, row_sum = in_blocks(
        stats_step, stats_init, (lax.all_gather(key_low, "blk", axis=0, tiled=True),)
    )
    log_sum = row_max + jnp.log(row_sum)

    def output_step(acc_state, sliced, first_key):
        keys_blk, values_blk = sliced
        key_count = keys_blk.shape[0]
        scores, allowed = block_scores(keys_blk, first_key)
        weights = jnp.where(allowed, jnp.exp(scores - log_sum[:, :, None]), 0.0)
        return acc_state + jnp.einsum(
            "hqk,khd->qhd",
            weights.astype(jnp.bfloat16),
            values_blk.reshape(key_count, H, HD),
            preferred_element_type=jnp.float32,
        )

    acc_init = jnp.zeros((tok_rows, H, HD), jnp.float32)
    attended_f = in_blocks(
        output_step,
        acc_init,
        (
            lax.all_gather(key_low, "blk", axis=0, tiled=True),
            lax.all_gather(value_low, "blk", axis=0, tiled=True),
        ),
    )
    attended_low = attended_f.reshape(tok_rows, model_width).astype(jnp.bfloat16)
    middle = (
        residual
        + jnp.dot(attended_low, proj_weight, preferred_element_type=jnp.float32)
        + proj_bias.astype(jnp.float32)
    )
    normed_two, hat_two, inv_two = norm_fwd(middle, mlp_gain_f, mlp_shift.astype(jnp.float32))
    normed_two_low = normed_two.astype(jnp.bfloat16)
    hidden = jnp.dot(
        normed_two_low, up_weight, preferred_element_type=jnp.float32
    ) + up_bias.astype(jnp.float32)
    active_low = jax.nn.gelu(hidden).astype(jnp.bfloat16)
    result = (
        middle
        + jnp.dot(active_low, down_weight, preferred_element_type=jnp.float32)
        + down_bias.astype(jnp.float32)
    )
    layer_out = result.astype(jnp.bfloat16)[None]
    cot_low = out_cotangent[0]
    cot_f = cot_low.astype(jnp.float32)
    grad_down_w = outer_sum(active_low, cot_low)
    grad_down_b = jnp.sum(cot_f, 0)
    d_active = times_transposed(cot_low, down_weight)
    hidden_unused, gelu_back = jax.vjp(jax.nn.gelu, hidden)
    d_hidden = gelu_back(d_active)[0].astype(jnp.bfloat16)
    grad_up_w = outer_sum(normed_two_low, d_hidden)
    grad_up_b = jnp.sum(d_hidden.astype(jnp.float32), 0)
    d_normed_two = times_transposed(d_hidden, up_weight)
    d_mid_norm, grad_mlp_gain, grad_mlp_shift = norm_back(
        d_normed_two, hat_two, inv_two, mlp_gain_f
    )
    d_middle = cot_f + d_mid_norm
    d_branch = d_middle.astype(jnp.bfloat16)
    grad_proj_w = outer_sum(attended_low, d_branch)
    grad_proj_b = jnp.sum(d_branch.astype(jnp.float32), 0)
    d_attended = (
        times_transposed(d_branch, proj_weight).astype(jnp.bfloat16).reshape(tok_rows, H, HD)
    )
    delta = jnp.einsum("qhd,qhd->hq", d_attended.astype(jnp.float32), attended_f)

    def back_step(state, sliced, first_key):
        dq_acc, buffers = state
        keys_blk, values_blk = sliced
        key_count = keys_blk.shape[0]
        scores, allowed = block_scores(keys_blk, first_key)
        weights = jnp.where(allowed, jnp.exp(scores - log_sum[:, :, None]), 0.0)
        d_weights = jnp.einsum(
            "qhd,khd->hqk",
            d_attended,
            values_blk.reshape(key_count, H, HD),
            preferred_element_type=jnp.float32,
        )
        d_scores = (weights * (d_weights - delta[:, :, None])).astype(jnp.bfloat16)
        dq_acc = dq_acc + 0.125 * jnp.einsum(
            "hqk,khd->qhd",
            d_scores,
            keys_blk.reshape(key_count, H, HD),
            preferred_element_type=jnp.float32,
        )
        d_keys = 0.125 * jnp.einsum(
            "hqk,qhd->khd", d_scores, query_h, preferred_element_type=jnp.float32
        )
        d_values = jnp.einsum(
            "hqk,qhd->khd",
            weights.astype(jnp.bfloat16),
            d_attended,
            preferred_element_type=jnp.float32,
        )
        key_buffer = add_rows(buffers[0], d_keys.reshape(key_count, model_width), first_key)
        value_buffer = add_rows(buffers[1], d_values.reshape(key_count, model_width), first_key)
        buffers = (key_buffer, value_buffer)
        return (dq_acc, buffers)

    buffer_init = (
        jnp.zeros((seq_len, model_width), jnp.float32),
        jnp.zeros((seq_len, model_width), jnp.float32),
    )
    back_init = (jnp.zeros((tok_rows, H, HD), jnp.float32), buffer_init)
    d_queries, key_grads = in_blocks(
        back_step,
        back_init,
        (
            lax.all_gather(key_low, "blk", axis=0, tiled=True),
            lax.all_gather(value_low, "blk", axis=0, tiled=True),
        ),
    )
    d_keys_own, d_values_own = (
        lax.psum_scatter(key_grads[0], "blk", scatter_dimension=0, tiled=True),
        lax.psum_scatter(key_grads[1], "blk", scatter_dimension=0, tiled=True),
    )
    d_queries_pre = rotate(d_queries, cos_tab, -sin_tab).reshape(tok_rows, model_width)
    d_keys_pre = rotate(d_keys_own.reshape(tok_rows, H, HD), cos_tab, -sin_tab).reshape(
        tok_rows, model_width
    )
    d_mixed = jnp.concatenate([d_queries_pre, d_keys_pre, d_values_own], axis=1).astype(
        jnp.bfloat16
    )
    grad_qkv_w = outer_sum(normed_low, d_mixed)
    grad_qkv_b = jnp.sum(d_mixed.astype(jnp.float32), 0)
    d_normed = times_transposed(d_mixed, qkv_weight)
    d_res_norm, grad_attn_gain, grad_attn_shift = norm_back(d_normed, hat_one, inv_one, attn_gain_f)
    tokens_grad = (d_middle + d_res_norm)[None]
    summed = (
        lax.psum_scatter(grad_qkv_w, ("batch", "blk"), scatter_dimension=0, tiled=True),
        lax.psum_scatter(grad_proj_w, ("batch", "blk"), scatter_dimension=0, tiled=True),
        lax.psum_scatter(grad_up_w, ("batch", "blk"), scatter_dimension=0, tiled=True),
        lax.psum_scatter(grad_down_w, ("batch", "blk"), scatter_dimension=0, tiled=True),
        lax.psum_scatter(grad_attn_gain, ("batch", "blk"), scatter_dimension=0, tiled=True),
        lax.psum_scatter(grad_attn_shift, ("batch", "blk"), scatter_dimension=0, tiled=True),
        lax.psum_scatter(grad_qkv_b, ("batch", "blk"), scatter_dimension=0, tiled=True),
        lax.psum_scatter(grad_proj_b, ("batch", "blk"), scatter_dimension=0, tiled=True),
        lax.psum_scatter(grad_mlp_gain, ("batch", "blk"), scatter_dimension=0, tiled=True),
        lax.psum_scatter(grad_mlp_shift, ("batch", "blk"), scatter_dimension=0, tiled=True),
        lax.psum_scatter(grad_up_b, ("batch", "blk"), scatter_dimension=0, tiled=True),
        lax.psum_scatter(grad_down_b, ("batch", "blk"), scatter_dimension=0, tiled=True),
    )
    return (
        layer_out,
        tokens_grad,
        summed[4],
        summed[5],
        summed[0],
        summed[6],
        summed[1],
        summed[7],
        summed[8],
        summed[9],
        summed[2],
        summed[10],
        summed[3],
        summed[11],
    )


BF = jnp.bfloat16
F32 = jnp.float32
AXES = ("x", "core", "zh", "zl", "y")
ROW = ("zh", "zl", "y")
GELU_A = 0.7978845608028654
GELU_B = 0.044715
VMEM_MIB = 32
PIN = 400000
LOW_PIN = 200000
NO_PIN = 1 << 30


def mm(left, right):
    return jnp.dot(left, right, preferred_element_type=F32)


def swap_over(value, *names):
    mask = sum(16 >> AXES.index(name) for name in names)
    return lax.ppermute(value, AXES, [(i, i ^ mask) for i in range(32)])


def whole(shape):
    zeros = (0,) * len(shape)
    return pl.BlockSpec(shape, lambda *_: zeros)


def arr(shape, dtype):
    return jax.ShapeDtypeStruct(shape, dtype)


def call(
    body, grid, in_specs, out_specs, out_shape, scratch, pin, scalars, args, out_pin=None
):
    return pl.pallas_call(
        body,
        grid_spec=pltpu.PrefetchScalarGridSpec(
            num_scalar_prefetch=1,
            grid=grid,
            in_specs=in_specs,
            out_specs=out_specs,
            scratch_shapes=scratch,
        ),
        out_shape=[pltpu.HBM(o.shape, o.dtype) if big(o, out_pin or pin) else o for o in out_shape],
        compiler_params=pltpu.CompilerParams(vmem_limit_bytes=VMEM_MIB << 20),
        cost_estimate=pl.CostEstimate(flops=0, bytes_accessed=1024, transcendentals=0),
    )(scalars, *(pinned(v, pin) for v in args))


def big(v, pin):
    return math.prod(v.shape) * v.dtype.itemsize >= pin


def pinned(v, pin):
    return pltpu.with_memory_space_constraint(v, pltpu.HBM) if big(v, pin) else v


def one_step(body, outs, scratch, pin, scalars, args, out_pin=None):
    return call(
        body, (1,), [whole(v.shape) for v in args], [whole(o.shape) for o in outs], outs, scratch,
        pin, scalars, args, out_pin,
    )


def standardize(x):
    mean = jnp.mean(x, -1, keepdims=True)
    centered = x - mean
    inv = lax.rsqrt(jnp.mean(centered * centered, -1, keepdims=True) + 1e-06)
    return centered * inv, inv


def swap_halves(x):
    lane = lax.broadcasted_iota(jnp.int32, x.shape, 1)
    return jnp.where(lane % 64 < 32, pltpu.roll(x, 96, 1), pltpu.roll(x, 32, 1))


def gelu_both(h):
    t = jnp.tanh(h * (GELU_A + (GELU_A * GELU_B) * (h * h)))
    half = 0.5 * h
    act = half + half * t
    slope = (0.5 + 0.5 * t) + half * (1.0 - t * t) * (GELU_A + (3.0 * GELU_A * GELU_B) * (h * h))
    return act, slope


def down_back_body(place, cot, down, d_act, bias_part):
    @pl.when(pl.program_id(0) == 0)
    def _():
        bias_part[...] = jnp.sum(cot[...].astype(F32), 0, keepdims=True)

    d_act[...] = times_transposed(cot[...], down[...])


def qkv_half(place, blocks, vecs, ws, cos, sin, hat_out, normed):
    g = vecs[0:1, :]
    s = vecs[1:2, :]
    for j in range(4):
        rows = slice(128 * j, 128 * j + 128)
        hat, _ = standardize(blocks[j][...].astype(F32))
        hat_out[rows, :] = hat.astype(BF)
        normed[rows, :] = (hat * g + s).astype(BF)
    lanes = pl.ds(pl.multiple_of(place[0] * 128, 128), 128)
    bias3 = jnp.concatenate([vecs[12 + p : 13 + p, lanes] for p in range(3)], 1)
    mixed = mm(normed[...], jnp.concatenate([w[...] for w in ws], 1)) + bias3
    c = cos[...]
    sn = sin[...]
    q = mixed[:, :128]
    k = mixed[:, 128:256]
    return (
        ((q * c + swap_halves(q) * sn) * 0.125).astype(BF),
        (k * c + swap_halves(k) * sn).astype(BF),
        mixed[:, 256:].astype(BF),
    )


def near_body(place, *refs):
    blocks = refs[:4]
    vecs, wq, wk, wv, cos, sin, hat_out, q_out, k_out, v_out, normed = refs[4:]
    q, k, v = qkv_half(place, blocks, vecs, (wq, wk, wv), cos, sin, hat_out, normed)
    q_out[...] = q
    k_out[...] = k
    v_out[...] = v


def far_body(place, *refs):
    blocks = refs[:4]
    vecs, wq, wk, wv, cos, sin, q0, k0, v0, hat_out, q_out, k_out, v_out, normed = refs[4:]
    q, k, v = qkv_half(place, blocks, vecs, (wq, wk, wv), cos, sin, hat_out, normed)
    for out, near, far in ((q_out, q0, q), (k_out, k0, k), (v_out, v0, v)):
        out[:512, :] = near[...]
        out[512:, :] = far


def head_mask(shape, head):
    return lax.broadcasted_iota(jnp.int32, shape, 1) // 64 == head


def attend_body(place, q, k_all, v_all, id_col, id_row, att_f, att_low, probs, row_scale):
    keys = k_all[...]
    values = v_all[...]
    queries = q[...]
    own = id_col[...]
    allowed = jnp.concatenate([own, own], 1) == id_row[0:1, :]
    halves, scales = [], []
    for head in range(2):
        mine = jnp.where(head_mask(queries.shape, head), queries, jnp.zeros_like(queries))
        scores = jnp.where(allowed, times_transposed(keys, mine), NEG_FILL)
        weights = jnp.exp(scores - jnp.max(scores, 0, keepdims=True))
        low = weights.astype(BF)
        probs[head] = low
        scale = 1.0 / jnp.sum(weights, 0, keepdims=True)
        scales.append(scale)
        halves.append(outer_sum(values, low)[64 * head : 64 * head + 64] * scale)
    out = jnp.concatenate(halves, 0).T
    att_f[...] = out
    row_scale[...] = jnp.concatenate([jnp.broadcast_to(v, (64, 256)) for v in scales], 0).T
    step = pl.program_id(0)
    att_low[place[0] ^ (2 * step)] = out[:128].astype(BF)
    att_low[place[0] ^ (2 * step + 1)] = out[128:].astype(BF)


def proj_body(place, att, tok, proj_w, vecs, middle, normed, att_rows):
    rows = jnp.concatenate([att[k] for k in range(8)], 1)
    att_rows[...] = rows
    mid = tok[...].astype(F32) + mm(rows, proj_w[...]) + vecs[2:3, :]
    middle[...] = mid
    hat, _ = standardize(mid)
    low = (hat * vecs[3:4, :] + vecs[4:5, :]).astype(BF)
    normed[...] = low


def proj_grad(place, att, d_b, vectors, send, keep):
    grad = outer_sum(att, d_b)
    row = lax.broadcasted_iota(jnp.int32, (32, 128), 0)
    for owner in range(32):
        x, core, k = owner // 16, (owner // 8) % 2, owner % 8
        rows = grad[32 * owner : 32 * owner + 32]
        extra = jnp.zeros((32, 128), F32)
        first = 128 * (owner // 4)
        for m in range(4):
            extra = jnp.where(row == m, vectors[m : m + 1, first : first + 128], extra)
        group = 2 * x + core
        last = vectors[4 + group : 5 + group, 128 * k : 128 * k + 128]
        extra = jnp.where(row == 4, last, extra)
        rel = place[0] ^ k
        slot = (rel & 1) * 4 + (rel >> 2) * 2 + ((rel >> 1) & 1)
        for side, out in ((core == place[2], keep), (core != place[2], send)):

            @pl.when(side)
            def _():
                out[place[1] ^ x, slot, :, :1024] = rows.astype(BF)
                out[place[1] ^ x, slot, :, 1024:] = extra.astype(BF)


def mlp_body(
    place, normed, d_act, up_w, vecs, middle, cot, proj_w, down_bias, att,
    active, d_mid, d_att, proj_send, proj_keep, acc, vectors,
):
    step = pl.program_id(0)
    hidden = mm(normed[...], up_w[...]) + vecs[pl.ds(8 + step, 1), :]
    act, slope = gelu_both(hidden)
    active[...] = act.astype(BF)
    d_hidden = (d_act[...] * slope).astype(BF)
    vectors[pl.ds(4 + step, 1), :] = jnp.sum(d_hidden.astype(F32), 0, keepdims=True)
    part = times_transposed(d_hidden, up_w[...])

    @pl.when(step == 0)
    def _():
        acc[...] = part

    @pl.when(step > 0)
    def _():
        acc[...] += part

    @pl.when(step == pl.num_programs(0) - 1)
    def _():
        up = acc[...]
        hat, inv = standardize(middle[...])
        e = up * vecs[3:4, :]
        inner = e - jnp.mean(e, -1, keepdims=True) - hat * jnp.mean(e * hat, -1, keepdims=True)
        d_m = cot[...].astype(F32) + inv * inner
        d_mid[...] = d_m
        d_b = d_m.astype(BF)
        vectors[0:1, :] = jnp.sum(up * hat, 0, keepdims=True)
        vectors[1:2, :] = jnp.sum(up, 0, keepdims=True)
        vectors[2:3, :] = jnp.sum(d_b.astype(F32), 0, keepdims=True)
        vectors[3:4, :] = down_bias[...]
        d_a = times_transposed(d_b, proj_w[...]).astype(BF)
        for k in range(8):
            d_att[k] = d_a[:, 128 * k : 128 * k + 128]
        proj_grad(place, att[...], d_b, vectors, proj_send, proj_keep)


def mlp_grad_body(place, *refs):
    blocks, cots, ups, downs = refs[:8], refs[8:16], refs[16:20], refs[20:24]
    vecs, down_keep, down_send, up_keep, up_send, n_all, c_all, u_all, d_all, grad = refs[24:]
    for j in range(8):
        n_all[128 * j : 128 * j + 128, :] = blocks[j][...]
        c_all[128 * j : 128 * j + 128, :] = cots[j][...]
    lanes = pl.ds(pl.multiple_of(place[0] * 128, 128), 128)
    up_b = []
    rows = vecs[8:12, lanes]
    biases = lax.broadcasted_iota(jnp.int32, (4, 128), 0)
    for g in range(4):
        u_all[:, 128 * g : 128 * g + 128] = ups[g][...]
        d_all[128 * g : 128 * g + 128, :] = downs[g][...]
        group = (place[1] ^ (g & 1)) * 2 + (place[2] ^ (g >> 1))
        up_b.append(jnp.sum(jnp.where(biases == group, rows, 0.0), 0, keepdims=True))
    n = n_all[...]
    c = c_all[...]
    act, slope = gelu_both(mm(n, u_all[...]) + jnp.concatenate(up_b, 1))
    grad_down = outer_sum(act.astype(BF), c)
    for g in range(4):
        rows = grad_down[128 * g : 128 * g + 128]
        if g < 2:
            down_keep[g] = rows.astype(BF)
        else:
            down_send[g - 2] = rows.astype(BF)
    d_hidden = (times_transposed(c, d_all[...]) * slope).astype(BF)
    both = outer_sum(n, d_hidden)
    for g in range(4):
        group = ((place[1] ^ (g & 1)) * 2) + (place[2] ^ (g >> 1))
        lanes = pl.ds(pl.multiple_of(group * 128, 128), 128)
        grad[:, lanes] = both[:, 128 * g : 128 * g + 128]
    for rx in range(2):
        first = (place[1] ^ rx) * 512
        keep = pl.multiple_of(first + place[2] * 256, 256)
        send = pl.multiple_of(first + (1 - place[2]) * 256, 256)
        up_keep[rx] = grad[pl.ds(keep, 256), :].astype(BF)
        up_send[rx] = grad[pl.ds(send, 256), :].astype(BF)


def attend_back_body(
    place, probs, d_att, att_f, row_scale, q, k_all, v_all, cos, sin, d_all, bias_part, dq, dk, dv
):
    step = pl.program_id(0)
    keys = k_all[...]
    values = v_all[...]
    queries = q[...]
    d_out = jnp.concatenate([d_att[place[0] ^ (2 * step)], d_att[place[0] ^ (2 * step + 1)]], 0)
    scaled = d_out.astype(F32) * row_scale[...]
    d_out = scaled.astype(BF)
    products = (d_out.astype(F32) * att_f[...]).T
    key_parts, value_parts, query_parts = [], [], []
    for head in range(2):
        weights = probs[head]
        mine = jnp.where(head_mask(d_out.shape, head), d_out, jnp.zeros_like(d_out))
        delta = jnp.sum(products[64 * head : 64 * head + 64], 0, keepdims=True)
        d_weights = times_transposed(values, mine)
        d_scores = (weights.astype(F32) * (d_weights - delta)).astype(BF)
        key_parts.append(mm(d_scores, queries))
        value_parts.append(mm(weights, d_out))
        query_parts.append(outer_sum(keys, d_scores)[64 * head : 64 * head + 64])
    first = head_mask((1024, 128), 0)
    dk_new = jnp.where(first, key_parts[0], key_parts[1])
    dv_new = jnp.where(first, value_parts[0], value_parts[1])
    dq[pl.ds(pl.multiple_of(step * 256, 256), 256), :] = jnp.concatenate(query_parts, 0).T

    @pl.when(step == 0)
    def _():
        dk[...] = dk_new
        dv[...] = dv_new

    @pl.when(step > 0)
    def _():
        dk[...] += dk_new
        dv[...] += dv_new

    @pl.when(step == pl.num_programs(0) - 1)
    def _():
        total = jnp.zeros((1, 384), F32)
        for j in range(8):
            rows = slice(128 * j, 128 * j + 128)
            c = cos[rows, :]
            sn = sin[rows, :]
            back_q = 0.125 * dq[rows, :]
            back_k = dk[rows, :]
            piece = jnp.concatenate(
                [
                    back_q * c - swap_halves(back_q) * sn,
                    back_k * c - swap_halves(back_k) * sn,
                    dv[rows, :],
                ],
                1,
            ).astype(BF)
            d_all[place[0] ^ j] = piece
            total = total + jnp.sum(piece.astype(F32), 0, keepdims=True)
        bias_part[...] = total


def rel_block(step, place):
    rel = jnp.where(step < 2, 2, 0) + step % 2
    return ((rel & 1) ^ place[1]) * 2 + ((rel >> 1) ^ place[2])


def qkv_grad_body(place, h0, h1, d_all, bias_part, vecs, wq, wk, wv, send, keep):
    step = pl.program_id(0)
    d_near = jnp.concatenate([d_all[place[0] ^ j] for j in range(4)], 0)
    d_far = jnp.concatenate([d_all[place[0] ^ j] for j in range(4, 8)], 0)
    inner = outer_sum(h0[...], d_near) + outer_sum(h1[...], d_far)
    total = bias_part[...]
    w = jnp.concatenate([wq[...], wk[...], wv[...]], 1).astype(F32)
    columns = vecs[...].T
    gain = columns[:, 0:1]
    shift = columns[:, 1:2]
    grad = gain * inner + shift * total
    row = lax.broadcasted_iota(jnp.int32, (256, 128), 0) % 32
    lane = lax.broadcasted_iota(jnp.int32, (256, 128), 1)
    extra = jnp.where(
        lane == 0,
        jnp.sum(w * inner, 1, keepdims=True),
        jnp.where(lane == 1, jnp.sum(w * total, 1, keepdims=True), 0.0),
    )
    for m in range(6):
        part = total[:, 128 * (m // 2) : 128 * (m // 2) + 128]
        part = part if m % 2 else pltpu.roll(part, 64, 1)
        extra = jnp.where((row == m) & (lane >= 64), part, extra)

    @pl.when(step < 2)
    def _():
        send[0, :, :384] = grad.astype(BF)
        send[0, :, 384:] = extra.astype(BF)

    @pl.when(step >= 2)
    def _():
        keep[0, :, :384] = grad.astype(BF)
        keep[0, :, 384:] = extra.astype(BF)


def pair_body(place, keep, came, left, send):
    half = left.shape[0]
    total = (keep[...].astype(F32) + came[...].astype(F32)).astype(BF)
    left[...] = total[:half]
    send[...] = total[half:]


def low_body(place, up_left, up_came, qkv_left, qkv_came, out):
    out[:, :32] = (up_left[...].astype(F32) + up_came[...].astype(F32)).astype(BF)
    out[:, 32:] = (qkv_left[...].astype(F32) + qkv_came[...].astype(F32)).astype(BF)


def merge_body(place, *refs):
    up, up_came, down, down_came, proj_left, proj_came = refs[:6]
    left, send, down_left, down_send, proj_keep, proj_send = refs[6:]
    proj_keep[...] = (proj_left[:2].astype(F32) + proj_came[:2].astype(F32)).astype(BF)
    proj_send[...] = (proj_left[2:].astype(F32) + proj_came[2:].astype(F32)).astype(BF)
    for side, low, low_down in ((0, left, down_left), (1, send, down_send)):
        total = (up[side].astype(F32) + up_came[side].astype(F32)).astype(BF)
        for k in range(8):
            low[k] = total[32 * k : 32 * k + 32]
        low_down[...] = (down[side].astype(F32) + down_came[side].astype(F32)).astype(BF)


def finish_body(place, came, grad_up, grad_qkv, sums, bias):
    total = jnp.zeros((32, 128), F32)
    low = lax.broadcasted_iota(jnp.int32, (1, 128), 1) < 64
    for k in range(8):
        for g in range(4):
            lanes = slice(1024 * g + 128 * k, 1024 * g + 128 * k + 128)
            grad_up[:, lanes] = came[k, :32, 128 * g : 128 * g + 128].astype(F32)
            if g < 3:
                grad_qkv[:, lanes] = came[k, 32:, 128 * g : 128 * g + 128].astype(F32)
        extra = came[k, 32:, 384:].astype(F32)
        total = total + extra
        for p in range(3):
            left = pltpu.roll(extra[2 * p : 2 * p + 1], 64, 1)
            both = jnp.where(low, left, extra[2 * p + 1 : 2 * p + 2])
            bias[p : p + 1, 128 * k : 128 * k + 128] = both
    sums[...] = total.T[:8]


def out_body(place, active, down, middle, vecs, out, acc):
    step = pl.program_id(0)
    part = mm(active[...], down[...])

    @pl.when(step == 0)
    def _():
        acc[...] = part + middle[...] + vecs[5:6, :]

    @pl.when(step > 0)
    def _():
        acc[...] += part

    @pl.when(step == pl.num_programs(0) - 1)
    def _():
        out[...] = acc[...].astype(BF)


def last_body(place, came, w, tok, d_mid, vecs, out, acc):
    step = pl.program_id(0)
    for p in range(3):

        @pl.when(step == p)
        def _():
            d_mixed = jnp.concatenate([came[k, :, 128 * p : 128 * p + 128] for k in range(8)], 1)
            part = times_transposed(d_mixed, w[...])
            if p == 0:
                acc[...] = part
            elif p == 1:
                acc[...] += part
            else:
                up = acc[...] + part
                hat, inv = standardize(tok[...].astype(F32))
                e = up * vecs[0:1, :]
                mean = jnp.mean(e, -1, keepdims=True)
                inner = e - mean - hat * jnp.mean(e * hat, -1, keepdims=True)
                out[...] = d_mid[...] + inv * inner


def frequency_rows():
    rows = np.zeros((8, 128), np.float32)
    for lane in range(128):
        pair = lane % 32
        part, rank, count = (0, pair, 10) if pair < 10 else ((1, pair - 10, 11) if pair < 21 else (2, pair - 21, 11))
        rows[part, lane] = 10000.0 ** (-rank / count)
        rows[3, lane] = -1.0 if lane % 64 < 32 else 1.0
    return rows


def clip_starts(place, pos):
    ids = jnp.zeros_like(pos)
    start = jnp.zeros_like(pos)
    end = jnp.int32(0)
    for c in range(8):
        length = place[8 + c]
        end = end + length
        past = pos >= end.astype(F32)
        ids = jnp.where(past, ids + 1.0, ids)
        start = jnp.where(past, end.astype(F32), start)
    return ids, start


def prep_body(place, freq, cos, sin, id_col, id_row):
    for j in range(8):
        first = ((place[0] ^ j) * 128).astype(F32)
        rows = slice(128 * j, 128 * j + 128)
        pos = first + lax.broadcasted_iota(jnp.int32, (128, 128), 0).astype(F32)
        ids, start = clip_starts(place, pos)
        id_col[rows, :] = ids
        within = pos - start
        row14 = jnp.floor((within + 0.5) * (1.0 / 14.0))
        t = jnp.floor((within + 0.5) * (1.0 / 196.0))
        angle = t * freq[0:1, :] + (row14 - 14.0 * t) * freq[1:2, :] + (within - 14.0 * row14) * freq[2:3, :]
        cos[rows, :] = jnp.cos(angle)
        sin[rows, :] = jnp.sin(angle) * freq[3:4, :]
        flat = first + lax.broadcasted_iota(jnp.int32, (8, 128), 1).astype(F32)
        id_row[:, 128 * j : 128 * j + 128] = clip_starts(place, flat)[0]


def after(value, *others):
    return lax.optimization_barrier((value, *others))[0]


def spread_four(a):
    return [a, swap_over(a, "y"), swap_over(a, "zl"), swap_over(a, "zl", "y")]


def fast_shards(
    tokens_in, clip_lengths, attn_gain, attn_shift, qkv_weight, qkv_bias, proj_weight, proj_bias,
    mlp_gain, mlp_shift, up_weight, up_bias, down_weight, down_bias, out_cotangent,
):
    x, core, zh, zl, y = (lax.axis_index(name) for name in AXES)
    k = zh * 4 + zl * 2 + y
    me = x * 16 + core * 8 + k
    place = jnp.concatenate(
        [jnp.stack([k, x, core, k, k, k, k, k]).astype(jnp.int32), clip_lengths[0]]
    )
    tok = tokens_in[0]
    cot = out_cotangent[0]

    far_tok = swap_over(tok, "zh")
    near = spread_four(tok)
    rows = [attn_gain, attn_shift, proj_bias, mlp_gain, mlp_shift, down_bias, down_bias, down_bias]
    vecs = jnp.concatenate([v.astype(F32).reshape(-1, 1024) for v in (*rows, up_bias, qkv_bias)], 0)
    cos_tab, sin_tab, id_col, id_row = one_step(
        prep_body,
        [arr((1024, 128), F32), arr((1024, 128), F32), arr((1024, 128), F32), arr((8, 1024), F32)],
        [],
        PIN,
        place,
        (jnp.asarray(frequency_rows()),),
    )
    far_tok, cos_tab, vecs, *near = lax.optimization_barrier((far_tok, cos_tab, vecs, *near))
    far = spread_four(far_tok)

    def table_half(part):
        return pl.BlockSpec((512, 128), lambda i, s: (part, 0))

    half = arr((512, 128), BF)
    full = arr((1024, 128), BF)
    common = (vecs, qkv_weight, qkv_weight, qkv_weight, cos_tab, sin_tab)
    columns_of = [pl.BlockSpec((1024, 128), lambda i, s, p=p: (0, 8 * p + s[0])) for p in range(3)]

    def qkv(body, part, blocks, more, outs):
        specs = [whole(v.shape) for v in (*blocks, vecs)] + columns_of
        specs += [table_half(part), table_half(part)] + [whole(v.shape) for v in more]
        return call(
            body, (1,), specs, [whole(o.shape) for o in outs], outs,
            [pltpu.VMEM((512, 1024), BF)], PIN, place, (*blocks, *common, *more),
        )

    hat0, q0, k0, v0 = qkv(near_body, 0, near, (), [arr((512, 1024), BF), half, half, half])
    d_act, down_bias_part = call(
        down_back_body,
        (4,),
        [whole((128, 1024)), pl.BlockSpec((1024, 1024), lambda i, s: (i, 0))],
        [pl.BlockSpec((128, 1024), lambda i, s: (0, i)), whole((1, 1024))],
        [arr((128, 4096), F32), arr((1, 1024), F32)],
        [],
        PIN,
        place,
        (after(cot, q0), down_weight),
    )
    far = lax.optimization_barrier((q0, d_act, *far))[2:]
    cot_here = after(cot, q0)
    far_cot = swap_over(cot_here, "zh")
    cots = spread_four(cot_here)
    hat1, q_all, k_all, v_all = qkv(
        far_body, 1, far, (q0, k0, v0), [arr((512, 1024), BF), full, full, full]
    )
    step_rows = pl.BlockSpec((256, 128), lambda i, s: (i, 0))
    flat = whole((1024, 128))
    att_f, att_low, probs, row_scale = call(
        attend_body,
        (4,),
        [
            step_rows, flat, flat, flat, pl.BlockSpec((8, 256), lambda i, s: (0, i)),
        ],
        [step_rows, whole((8, 128, 128)), pl.BlockSpec((2, 1024, 256), lambda i, s: (0, 0, i)),
         step_rows],
        [arr((1024, 128), F32), arr((8, 128, 128), BF), arr((2, 1024, 1024), BF),
         arr((1024, 128), F32)],
        [],
        PIN,
        place,
        (q_all, k_all, v_all, id_col, id_row),
    )
    att_low, far_cot, *cots = lax.optimization_barrier((att_low, far_cot, *cots))
    att_in = lax.all_to_all(att_low, ROW, 0, 0, tiled=True)
    cots += [far_cot, swap_over(far_cot, "y"), swap_over(far_cot, "zl")]
    middle, normed2, att_rows = one_step(
        proj_body,
        [arr((128, 1024), F32), arr((128, 1024), BF), arr((128, 1024), BF)],
        [],
        PIN,
        place,
        (att_in, tok, proj_weight, vecs),
        LOW_PIN,
    )
    normed2, *cots = lax.optimization_barrier((normed2, *cots))
    far_n = swap_over(normed2, "zh")
    near_n = spread_four(normed2)
    wide = pl.BlockSpec((128, 1024), lambda i, s: (0, i))
    fixed = whole((128, 1024))
    active, d_mid, d_att, proj_send, proj_keep = call(
        mlp_body,
        (4,),
        [
            fixed, wide, wide_columns(), whole((15, 1024)), fixed, fixed, whole((1024, 1024)),
            whole((1, 1024)), fixed,
        ],
        [wide, fixed, whole((8, 128, 128)), whole((2, 8, 32, 1152)), whole((2, 8, 32, 1152))],
        [
            arr((128, 4096), BF), arr((128, 1024), F32), arr((8, 128, 128), BF),
            arr((2, 8, 32, 1152), BF), arr((2, 8, 32, 1152), BF),
        ],
        [pltpu.VMEM((128, 1024), F32), pltpu.VMEM((8, 1024), F32)],
        LOW_PIN,
        place,
        (normed2, d_act, up_weight, vecs, middle, cot, proj_weight, down_bias_part, att_rows),
    )
    d_att, far_n, far_y, active, proj_send, *near_n = lax.optimization_barrier(
        (d_att, far_n, cots[5], active, proj_send, *near_n)
    )
    last_cot = swap_over(far_y, "zl")
    d_att_in = lax.all_to_all(d_att, ROW, 0, 0, tiled=True)

    far_n = spread_four(far_n)

    def pair(keep, came):
        half = arr((keep.shape[0] // 2, *keep.shape[1:]), BF)
        return one_step(pair_body, [half, half], [], NO_PIN, place, (keep, came))

    flat_proj = (16, 32, 1152)
    proj_left, proj_low = pair(
        proj_keep.reshape(flat_proj), swap_over(proj_send.reshape(flat_proj), "core")
    )

    d_all, qkv_bias_part = call(
        attend_back_body,
        (4,),
        [
            pl.BlockSpec((2, 1024, 256), lambda i, s: (0, 0, i)), whole((8, 128, 128)), step_rows,
            step_rows, step_rows, flat, flat, flat, flat,
        ],
        [whole((8, 128, 384)), whole((1, 384))],
        [arr((8, 128, 384), BF), arr((1, 384), F32)],
        [pltpu.VMEM((1024, 128), F32)] * 3,
        PIN,
        place,
        (probs, after(d_att_in, proj_low), att_f, row_scale, q_all, k_all, v_all, cos_tab, sin_tab),
    )
    block_of = lambda i, s: (rel_block(i, s), 0)
    lanes_of = lambda i, s: (0, rel_block(i, s))
    send, keep = call(
        qkv_grad_body,
        (4,),
        [
            pl.BlockSpec((512, 256), lanes_of), pl.BlockSpec((512, 256), lanes_of),
            whole((8, 128, 384)), whole((1, 384)), pl.BlockSpec((8, 256), lanes_of),
        ]
        + [pl.BlockSpec((256, 128), lambda i, s, p=p: (rel_block(i, s), 8 * p + s[0])) for p in range(3)],
        [
            pl.BlockSpec((1, 256, 512), lambda i, s: (jnp.minimum(i, 1), 0, 0)),
            pl.BlockSpec((1, 256, 512), lambda i, s: (jnp.maximum(i - 2, 0), 0, 0)),
        ],
        [arr((2, 256, 512), BF), arr((2, 256, 512), BF)],
        [],
        PIN,
        place,
        (hat0, hat1, d_all, qkv_bias_part, vecs, qkv_weight, qkv_weight, qkv_weight),
    )
    def turn(value):
        return lax.all_to_all(value, ROW, 0, 0, tiled=True)
    d_all, send, last_cot, *far_n = lax.optimization_barrier((d_all, send, last_cot, *far_n))
    moved = lax.all_to_all(d_all, ROW, 0, 0, tiled=True)
    proj_left, proj_low = pair(after(proj_left, d_all), swap_over(proj_low, "x"))

    flat_qkv = (16, 32, 512)
    qkv_left, qkv_low = pair(
        keep.reshape(flat_qkv), swap_over(send.reshape(flat_qkv), "core")
    )
    qkv_came = swap_over(qkv_low, "x")

    def group_of(s, g):
        return (s[1] ^ (g & 1)) * 16 + (s[2] ^ (g >> 1)) * 8 + s[0]

    outs = [
        arr((2, 128, 1024), BF), arr((2, 128, 1024), BF), arr((2, 256, 512), BF),
        arr((2, 256, 512), BF),
    ]
    down_keep, down_send, up_keep, up_send = call(
        mlp_grad_body,
        (1,),
        [fixed] * 16
        + [pl.BlockSpec((1024, 128), lambda i, s, g=g: (0, group_of(s, g))) for g in range(4)]
        + [pl.BlockSpec((128, 1024), lambda i, s, g=g: (group_of(s, g), 0)) for g in range(4)]
        + [whole((15, 1024))],
        [whole(o.shape) for o in outs],
        outs,
        [
            pltpu.VMEM((1024, 1024), BF), pltpu.VMEM((1024, 1024), BF),
            pltpu.VMEM((1024, 512), BF), pltpu.VMEM((512, 1024), BF), pltpu.VMEM((1024, 512), F32),
        ],
        LOW_PIN,
        place,
        (after(near_n[0], d_all, proj_low, qkv_low), *near_n[1:], *far_n, *cots, last_cot, *([up_weight] * 4), *([down_weight] * 4), vecs),
    )


    up_send, down_send, proj_came, qkv_came = lax.optimization_barrier(
        (up_send, down_send, swap_over(proj_low, "y"), qkv_came)
    )
    left, low_send, down_left, down_low, proj_left, proj_low = one_step(
        merge_body,
        [arr((8, 32, 512), BF)] * 2 + [arr((128, 1024), BF)] * 2 + [arr((2, 32, 1152), BF)] * 2,
        [],
        PIN,
        place,
        (
            after(up_keep, moved), swap_over(up_send, "core"),
            down_keep, swap_over(down_send, "core"), proj_left, proj_came,
        ),
        NO_PIN,
    )
    low_came = swap_over(low_send, "x")
    (tokens_grad,) = call(
        last_body,
        (3,),
        [
            whole((8, 128, 384)), pl.BlockSpec((1024, 1024), lambda i, s: (0, i)), fixed, fixed,
            whole((15, 1024)),
        ],
        [fixed],
        [arr((128, 1024), F32)],
        [pltpu.VMEM((128, 1024), F32)],
        PIN,
        place,
        (after(moved, left), qkv_weight, tok, d_mid, vecs),
    )

    left, low_came, _ = lax.optimization_barrier((left, low_came, tokens_grad))
    (lows,) = one_step(
        low_body, [arr((8, 64, 512), BF)], [], NO_PIN, place, (left, low_came, qkv_left, qkv_came)
    )
    came = turn(lows)
    proj_left, proj_low = pair(after(proj_left, lows), swap_over(proj_low, "zh"))
    proj_came = swap_over(proj_low, "zl")
    down_low, _ = lax.optimization_barrier((down_low, lows))
    grad_down = down_left.astype(F32) + swap_over(down_low, "x").astype(F32)
    proj_total = proj_left[0].astype(F32) + proj_came[0].astype(F32)
    (layer_out,) = call(
        out_body,
        (4,),
        [wide, pl.BlockSpec((1024, 1024), lambda i, s: (i, 0)), fixed, whole((15, 1024))],
        [fixed],
        [arr((128, 1024), BF)],
        [pltpu.VMEM((128, 1024), F32)],
        PIN,
        place,
        (after(active, lows), down_weight, middle, vecs),
    )
    layer_out = layer_out[None]
    grad_proj = proj_total[:, :1024]
    own = lax.dynamic_slice(proj_total[:4, 1024:], (0, (me % 4) * 32), (4, 32))
    grad_up_b = proj_total[4, 1024:]

    grad_up, grad_qkv, sums, bias = one_step(
        finish_body,
        [arr((32, 4096), F32), arr((32, 3072), F32), arr((8, 32), F32), arr((3, 1024), F32)],
        [],
        NO_PIN,
        place,
        (came,),
    )
    grad_qkv_b = lax.dynamic_slice(bias.reshape(3072), (me * 96,), (96,))

    return (
        layer_out, tokens_grad[None], sums[0], sums[1], grad_qkv, grad_qkv_b, grad_proj,
        own[2], own[0], own[1], grad_up, grad_up_b, grad_down, own[3],
    )


def wide_columns():
    return pl.BlockSpec((1024, 1024), lambda i, s: (0, i))


def fast_solution(mesh):
    wide_mesh = Mesh(mesh.devices.reshape(2, 2, 2, 2, 2), AXES)
    batch, blk = AXES[:2], AXES[2:]
    spread = P(batch, blk, None)
    return jax.shard_map(
        fast_shards,
        mesh=wide_mesh,
        in_specs=(spread, P(batch, None)) + (P(),) * 12 + (spread,),
        out_specs=(spread, spread)
        + tuple(P(AXES, None) if i in (2, 4, 8, 10) else P(AXES) for i in range(12)),
        check_vma=False,
    )


def solution(mesh):
    if tuple(mesh.devices.shape) == (4, 8):
        return fast_solution(mesh)
    placed = (
        P("batch", "blk", None),
        P("batch", None),
        P(),
        P(),
        P(),
        P(),
        P(),
        P(),
        P(),
        P(),
        P(),
        P(),
        P(),
        P(),
        P("batch", "blk", None),
    )
    return jax.shard_map(
        shards,
        mesh=mesh,
        in_specs=placed,
        out_specs=(
            P("batch", "blk", None),
            P("batch", "blk", None),
            P(("batch", "blk")),
            P(("batch", "blk")),
            P(("batch", "blk"), None),
            P(("batch", "blk")),
            P(("batch", "blk"), None),
            P(("batch", "blk")),
            P(("batch", "blk")),
            P(("batch", "blk")),
            P(("batch", "blk"), None),
            P(("batch", "blk")),
            P(("batch", "blk"), None),
            P(("batch", "blk")),
        ),
        check_vma=False,
    )
```

```python
import math

import jax
import jax.numpy as jnp
import numpy as np
from jax import lax
from jax.experimental import pallas as pl
from jax.experimental.pallas import tpu as pltpu
from jax.sharding import Mesh
from jax.sharding import PartitionSpec as P

H = 16
HD = 64


NEG_FILL = -1e30


def pair_table():
    part_map = [0] * 10 + [1] * 11 + [2] * 11
    freq_list = [10000.0 ** (-rank / 10.0) for rank in range(10)] + [
        10000.0 ** (-rank / 11.0) for rank in range(11)
    ] * 2
    table_rows = [
        [freq_list[column] if part_map[column] == axis_id else 0.0 for column in range(32)]
        for axis_id in range(3)
    ]
    return jnp.array(table_rows, dtype=jnp.float32)


def clip_of(lengths_row, positions):
    clip_end = jnp.cumsum(lengths_row)
    return jnp.sum((positions[:, None] >= clip_end[None, :]).astype(jnp.int32), axis=1)


def clip_layout(lengths_row, positions):
    clip_end = jnp.cumsum(lengths_row)
    starts = clip_end - lengths_row
    clip_ids = jnp.sum((positions[:, None] >= clip_end[None, :]).astype(jnp.int32), axis=1)
    member = clip_ids[:, None] == jnp.arange(lengths_row.shape[0], dtype=jnp.int32)[None, :]
    within = positions - jnp.sum(jnp.where(member, starts[None, :], 0), axis=1)
    coords = jnp.stack([within // 196, within // 14 % 14, within % 14], axis=1).astype(jnp.float32)
    angles = jnp.dot(coords, pair_table(), precision=lax.Precision.HIGHEST)
    return (clip_ids, jnp.cos(angles), jnp.sin(angles))


def rotate(values, cos_tab, sin_tab):
    half_dim = values.shape[-1] // 2
    first_half = values[..., :half_dim]
    second_half = values[..., half_dim:]
    cos_b = cos_tab[:, None, :]
    sin_b = sin_tab[:, None, :]
    return jnp.concatenate(
        [first_half * cos_b - second_half * sin_b, first_half * sin_b + second_half * cos_b],
        axis=-1,
    )


def norm_fwd(values, gain_vec, shift_vec):
    row_mean = jnp.mean(values, -1, keepdims=True)
    centered = values - row_mean
    inv_std = lax.rsqrt(jnp.mean(centered * centered, -1, keepdims=True) + 1e-06)
    normalized = centered * inv_std
    return (normalized * gain_vec + shift_vec, normalized, inv_std)


def norm_back(upstream, normalized, inv_std, gain_vec):
    scaled = upstream * gain_vec
    inner = (
        scaled
        - jnp.mean(scaled, -1, keepdims=True)
        - normalized * jnp.mean(scaled * normalized, -1, keepdims=True)
    )
    return (inv_std * inner, jnp.sum(upstream * normalized, 0), jnp.sum(upstream, 0))


def outer_sum(left, right):
    return lax.dot_general(
        left, right, (((0,), (0,)), ((), ())), preferred_element_type=jnp.float32
    )


def times_transposed(left, right):
    return lax.dot_general(
        left, right, (((1,), (1,)), ((), ())), preferred_element_type=jnp.float32
    )


def add_rows(buffer, block, first_key):
    current = lax.dynamic_slice_in_dim(buffer, first_key, block.shape[0], 0)
    return lax.dynamic_update_slice_in_dim(buffer, current + block, first_key, 0)


def in_blocks(block_step, running, pieces):
    row_count = pieces[0].shape[0]
    block_rows = math.gcd(row_count, 2048)

    def advance(block_idx, state):
        first_row = block_idx * block_rows
        sliced = tuple(
            (lax.dynamic_slice_in_dim(piece, first_row, block_rows, 0) for piece in pieces)
        )
        return block_step(state, sliced, first_row)

    return lax.fori_loop(0, row_count // block_rows, advance, running)


def shards(
    tokens_in,
    clip_lengths,
    attn_gain,
    attn_shift,
    qkv_weight,
    qkv_bias,
    proj_weight,
    proj_bias,
    mlp_gain,
    mlp_shift,
    up_weight,
    up_bias,
    down_weight,
    down_bias,
    out_cotangent,
):
    tok_rows = tokens_in.shape[1]
    model_width = tokens_in.shape[2]
    seq_len = tok_rows * lax.axis_size("blk")
    lens_row = clip_lengths[0]
    own_pos = lax.axis_index("blk") * tok_rows + jnp.arange(tok_rows, dtype=jnp.int32)
    clip_q, cos_tab, sin_tab = clip_layout(lens_row, own_pos)
    residual = tokens_in[0].astype(jnp.float32)
    attn_gain_f = attn_gain.astype(jnp.float32)
    mlp_gain_f = mlp_gain.astype(jnp.float32)
    normed, hat_one, inv_one = norm_fwd(residual, attn_gain_f, attn_shift.astype(jnp.float32))
    normed_low = normed.astype(jnp.bfloat16)
    qkv_mixed = jnp.dot(
        normed_low, qkv_weight, preferred_element_type=jnp.float32
    ) + qkv_bias.astype(jnp.float32)
    query_h = rotate(qkv_mixed[:, :model_width].reshape(tok_rows, H, HD), cos_tab, sin_tab).astype(
        jnp.bfloat16
    )
    key_low = (
        rotate(
            qkv_mixed[:, model_width : 2 * model_width].reshape(tok_rows, H, HD), cos_tab, sin_tab
        )
        .astype(jnp.bfloat16)
        .reshape(tok_rows, model_width)
    )
    value_low = qkv_mixed[:, 2 * model_width :].astype(jnp.bfloat16)

    def block_scores(keys_blk, first_key):
        key_count = keys_blk.shape[0]
        clip_k = clip_of(lens_row, first_key + jnp.arange(key_count, dtype=jnp.int32))
        raw_scores = jnp.einsum(
            "qhd,khd->hqk",
            query_h,
            keys_blk.reshape(key_count, H, HD),
            preferred_element_type=jnp.float32,
        )
        allowed = (clip_q[:, None] == clip_k[None, :])[None]
        return (jnp.where(allowed, 0.125 * raw_scores, NEG_FILL), allowed)

    def stats_step(state, sliced, first_key):
        row_max, row_sum = state
        scores, allowed = block_scores(sliced[0], first_key)
        new_max = jnp.maximum(row_max, jnp.max(scores, -1))
        weights = jnp.where(allowed, jnp.exp(scores - new_max[:, :, None]), 0.0)
        return (new_max, row_sum * jnp.exp(row_max - new_max) + jnp.sum(weights, -1))

    stats_init = (
        jnp.full((H, tok_rows), NEG_FILL, jnp.float32),
        jnp.zeros((H, tok_rows), jnp.float32),
    )
    row_max, row_sum = in_blocks(
        stats_step, stats_init, (lax.all_gather(key_low, "blk", axis=0, tiled=True),)
    )
    log_sum = row_max + jnp.log(row_sum)

    def output_step(acc_state, sliced, first_key):
        keys_blk, values_blk = sliced
        key_count = keys_blk.shape[0]
        scores, allowed = block_scores(keys_blk, first_key)
        weights = jnp.where(allowed, jnp.exp(scores - log_sum[:, :, None]), 0.0)
        return acc_state + jnp.einsum(
            "hqk,khd->qhd",
            weights.astype(jnp.bfloat16),
            values_blk.reshape(key_count, H, HD),
            preferred_element_type=jnp.float32,
        )

    acc_init = jnp.zeros((tok_rows, H, HD), jnp.float32)
    attended_f = in_blocks(
        output_step,
        acc_init,
        (
            lax.all_gather(key_low, "blk", axis=0, tiled=True),
            lax.all_gather(value_low, "blk", axis=0, tiled=True),
        ),
    )
    attended_low = attended_f.reshape(tok_rows, model_width).astype(jnp.bfloat16)
    middle = (
        residual
        + jnp.dot(attended_low, proj_weight, preferred_element_type=jnp.float32)
        + proj_bias.astype(jnp.float32)
    )
    normed_two, hat_two, inv_two = norm_fwd(middle, mlp_gain_f, mlp_shift.astype(jnp.float32))
    normed_two_low = normed_two.astype(jnp.bfloat16)
    hidden = jnp.dot(
        normed_two_low, up_weight, preferred_element_type=jnp.float32
    ) + up_bias.astype(jnp.float32)
    active_low = jax.nn.gelu(hidden).astype(jnp.bfloat16)
    result = (
        middle
        + jnp.dot(active_low, down_weight, preferred_element_type=jnp.float32)
        + down_bias.astype(jnp.float32)
    )
    layer_out = result.astype(jnp.bfloat16)[None]
    cot_low = out_cotangent[0]
    cot_f = cot_low.astype(jnp.float32)
    grad_down_w = outer_sum(active_low, cot_low)
    grad_down_b = jnp.sum(cot_f, 0)
    d_active = times_transposed(cot_low, down_weight)
    hidden_unused, gelu_back = jax.vjp(jax.nn.gelu, hidden)
    d_hidden = gelu_back(d_active)[0].astype(jnp.bfloat16)
    grad_up_w = outer_sum(normed_two_low, d_hidden)
    grad_up_b = jnp.sum(d_hidden.astype(jnp.float32), 0)
    d_normed_two = times_transposed(d_hidden, up_weight)
    d_mid_norm, grad_mlp_gain, grad_mlp_shift = norm_back(
        d_normed_two, hat_two, inv_two, mlp_gain_f
    )
    d_middle = cot_f + d_mid_norm
    d_branch = d_middle.astype(jnp.bfloat16)
    grad_proj_w = outer_sum(attended_low, d_branch)
    grad_proj_b = jnp.sum(d_branch.astype(jnp.float32), 0)
    d_attended = (
        times_transposed(d_branch, proj_weight).astype(jnp.bfloat16).reshape(tok_rows, H, HD)
    )
    delta = jnp.einsum("qhd,qhd->hq", d_attended.astype(jnp.float32), attended_f)

    def back_step(state, sliced, first_key):
        dq_acc, buffers = state
        keys_blk, values_blk = sliced
        key_count = keys_blk.shape[0]
        scores, allowed = block_scores(keys_blk, first_key)
        weights = jnp.where(allowed, jnp.exp(scores - log_sum[:, :, None]), 0.0)
        d_weights = jnp.einsum(
            "qhd,khd->hqk",
            d_attended,
            values_blk.reshape(key_count, H, HD),
            preferred_element_type=jnp.float32,
        )
        d_scores = (weights * (d_weights - delta[:, :, None])).astype(jnp.bfloat16)
        dq_acc = dq_acc + 0.125 * jnp.einsum(
            "hqk,khd->qhd",
            d_scores,
            keys_blk.reshape(key_count, H, HD),
            preferred_element_type=jnp.float32,
        )
        d_keys = 0.125 * jnp.einsum(
            "hqk,qhd->khd", d_scores, query_h, preferred_element_type=jnp.float32
        )
        d_values = jnp.einsum(
            "hqk,qhd->khd",
            weights.astype(jnp.bfloat16),
            d_attended,
            preferred_element_type=jnp.float32,
        )
        key_buffer = add_rows(buffers[0], d_keys.reshape(key_count, model_width), first_key)
        value_buffer = add_rows(buffers[1], d_values.reshape(key_count, model_width), first_key)
        buffers = (key_buffer, value_buffer)
        return (dq_acc, buffers)

    buffer_init = (
        jnp.zeros((seq_len, model_width), jnp.float32),
        jnp.zeros((seq_len, model_width), jnp.float32),
    )
    back_init = (jnp.zeros((tok_rows, H, HD), jnp.float32), buffer_init)
    d_queries, key_grads = in_blocks(
        back_step,
        back_init,
        (
            lax.all_gather(key_low, "blk", axis=0, tiled=True),
            lax.all_gather(value_low, "blk", axis=0, tiled=True),
        ),
    )
    d_keys_own, d_values_own = (
        lax.psum_scatter(key_grads[0], "blk", scatter_dimension=0, tiled=True),
        lax.psum_scatter(key_grads[1], "blk", scatter_dimension=0, tiled=True),
    )
    d_queries_pre = rotate(d_queries, cos_tab, -sin_tab).reshape(tok_rows, model_width)
    d_keys_pre = rotate(d_keys_own.reshape(tok_rows, H, HD), cos_tab, -sin_tab).reshape(
        tok_rows, model_width
    )
    d_mixed = jnp.concatenate([d_queries_pre, d_keys_pre, d_values_own], axis=1).astype(
        jnp.bfloat16
    )
    grad_qkv_w = outer_sum(normed_low, d_mixed)
    grad_qkv_b = jnp.sum(d_mixed.astype(jnp.float32), 0)
    d_normed = times_transposed(d_mixed, qkv_weight)
    d_res_norm, grad_attn_gain, grad_attn_shift = norm_back(d_normed, hat_one, inv_one, attn_gain_f)
    tokens_grad = (d_middle + d_res_norm)[None]
    summed = (
        lax.psum_scatter(grad_qkv_w, ("batch", "blk"), scatter_dimension=0, tiled=True),
        lax.psum_scatter(grad_proj_w, ("batch", "blk"), scatter_dimension=0, tiled=True),
        lax.psum_scatter(grad_up_w, ("batch", "blk"), scatter_dimension=0, tiled=True),
        lax.psum_scatter(grad_down_w, ("batch", "blk"), scatter_dimension=0, tiled=True),
        lax.psum_scatter(grad_attn_gain, ("batch", "blk"), scatter_dimension=0, tiled=True),
        lax.psum_scatter(grad_attn_shift, ("batch", "blk"), scatter_dimension=0, tiled=True),
        lax.psum_scatter(grad_qkv_b, ("batch", "blk"), scatter_dimension=0, tiled=True),
        lax.psum_scatter(grad_proj_b, ("batch", "blk"), scatter_dimension=0, tiled=True),
        lax.psum_scatter(grad_mlp_gain, ("batch", "blk"), scatter_dimension=0, tiled=True),
        lax.psum_scatter(grad_mlp_shift, ("batch", "blk"), scatter_dimension=0, tiled=True),
        lax.psum_scatter(grad_up_b, ("batch", "blk"), scatter_dimension=0, tiled=True),
        lax.psum_scatter(grad_down_b, ("batch", "blk"), scatter_dimension=0, tiled=True),
    )
    return (
        layer_out,
        tokens_grad,
        summed[4],
        summed[5],
        summed[0],
        summed[6],
        summed[1],
        summed[7],
        summed[8],
        summed[9],
        summed[2],
        summed[10],
        summed[3],
        summed[11],
    )


BF = jnp.bfloat16
F32 = jnp.float32
AXES = ("x", "core", "zh", "zl", "y")
ROW = ("zh", "zl", "y")
GELU_A = 0.7978845608028654
GELU_B = 0.044715
VMEM_MIB = 32
PIN = 400000
LOW_PIN = 200000
NO_PIN = 1 << 30


def mm(left, right):
    return jnp.dot(left, right, preferred_element_type=F32)


def swap_over(value, *names):
    mask = sum(16 >> AXES.index(name) for name in names)
    return lax.ppermute(value, AXES, [(i, i ^ mask) for i in range(32)])


def whole(shape):
    zeros = (0,) * len(shape)
    return pl.BlockSpec(shape, lambda *_: zeros)


def arr(shape, dtype):
    return jax.ShapeDtypeStruct(shape, dtype)


def call(
    body, grid, in_specs, out_specs, out_shape, scratch, pin, scalars, args, out_pin=None
):
    return pl.pallas_call(
        body,
        grid_spec=pltpu.PrefetchScalarGridSpec(
            num_scalar_prefetch=1,
            grid=grid,
            in_specs=in_specs,
            out_specs=out_specs,
            scratch_shapes=scratch,
        ),
        out_shape=[pltpu.HBM(o.shape, o.dtype) if big(o, out_pin or pin) else o for o in out_shape],
        compiler_params=pltpu.CompilerParams(vmem_limit_bytes=VMEM_MIB << 20),
        cost_estimate=pl.CostEstimate(flops=0, bytes_accessed=1024, transcendentals=0),
    )(scalars, *(pinned(v, pin) for v in args))


def big(v, pin):
    return math.prod(v.shape) * v.dtype.itemsize >= pin


def pinned(v, pin):
    return pltpu.with_memory_space_constraint(v, pltpu.HBM) if big(v, pin) else v


def one_step(body, outs, scratch, pin, scalars, args, out_pin=None):
    return call(
        body, (1,), [whole(v.shape) for v in args], [whole(o.shape) for o in outs], outs, scratch,
        pin, scalars, args, out_pin,
    )


def standardize(x):
    mean = jnp.mean(x, -1, keepdims=True)
    centered = x - mean
    inv = lax.rsqrt(jnp.mean(centered * centered, -1, keepdims=True) + 1e-06)
    return centered * inv, inv


def swap_halves(x):
    lane = lax.broadcasted_iota(jnp.int32, x.shape, 1)
    return jnp.where(lane % 64 < 32, pltpu.roll(x, 96, 1), pltpu.roll(x, 32, 1))


def gelu_both(h):
    t = jnp.tanh(h * (GELU_A + (GELU_A * GELU_B) * (h * h)))
    half = 0.5 * h
    act = half + half * t
    slope = (0.5 + 0.5 * t) + half * (1.0 - t * t) * (GELU_A + (3.0 * GELU_A * GELU_B) * (h * h))
    return act, slope


def down_back_body(place, cot, down, d_act, bias_part):
    @pl.when(pl.program_id(0) == 0)
    def _():
        bias_part[...] = jnp.sum(cot[...].astype(F32), 0, keepdims=True)

    d_act[...] = times_transposed(cot[...], down[...])


def qkv_half(place, blocks, vecs, ws, cos, sin, hat_out, normed):
    g = vecs[0:1, :]
    s = vecs[1:2, :]
    for j in range(4):
        rows = slice(128 * j, 128 * j + 128)
        hat, _ = standardize(blocks[j][...].astype(F32))
        hat_out[rows, :] = hat.astype(BF)
        normed[rows, :] = (hat * g + s).astype(BF)
    lanes = pl.ds(pl.multiple_of(place[0] * 128, 128), 128)
    bias3 = jnp.concatenate([vecs[12 + p : 13 + p, lanes] for p in range(3)], 1)
    mixed = mm(normed[...], jnp.concatenate([w[...] for w in ws], 1)) + bias3
    c = cos[...]
    sn = sin[...]
    q = mixed[:, :128]
    k = mixed[:, 128:256]
    return (
        ((q * c + swap_halves(q) * sn) * 0.125).astype(BF),
        (k * c + swap_halves(k) * sn).astype(BF),
        mixed[:, 256:].astype(BF),
    )


def near_body(place, *refs):
    blocks = refs[:4]
    vecs, wq, wk, wv, cos, sin, hat_out, q_out, k_out, v_out, normed = refs[4:]
    q, k, v = qkv_half(place, blocks, vecs, (wq, wk, wv), cos, sin, hat_out, normed)
    q_out[...] = q
    k_out[...] = k
    v_out[...] = v


def far_body(place, *refs):
    blocks = refs[:4]
    vecs, wq, wk, wv, cos, sin, q0, k0, v0, hat_out, q_out, k_out, v_out, normed = refs[4:]
    q, k, v = qkv_half(place, blocks, vecs, (wq, wk, wv), cos, sin, hat_out, normed)
    for out, near, far in ((q_out, q0, q), (k_out, k0, k), (v_out, v0, v)):
        out[:512, :] = near[...]
        out[512:, :] = far


def head_mask(shape, head):
    return lax.broadcasted_iota(jnp.int32, shape, 1) // 64 == head


def attend_body(place, q, k_all, v_all, id_col, id_row, att_f, att_low, probs, row_scale):
    keys = k_all[...]
    values = v_all[...]
    queries = q[...]
    own = id_col[...]
    allowed = jnp.concatenate([own, own], 1) == id_row[0:1, :]
    halves, scales = [], []
    for head in range(2):
        mine = jnp.where(head_mask(queries.shape, head), queries, jnp.zeros_like(queries))
        scores = jnp.where(allowed, times_transposed(keys, mine), NEG_FILL)
        weights = jnp.exp(scores - jnp.max(scores, 0, keepdims=True))
        low = weights.astype(BF)
        probs[head] = low
        scale = 1.0 / jnp.sum(weights, 0, keepdims=True)
        scales.append(scale)
        halves.append(outer_sum(values, low)[64 * head : 64 * head + 64] * scale)
    out = jnp.concatenate(halves, 0).T
    att_f[...] = out
    row_scale[...] = jnp.concatenate([jnp.broadcast_to(v, (64, 256)) for v in scales], 0).T
    step = pl.program_id(0)
    att_low[place[0] ^ (2 * step)] = out[:128].astype(BF)
    att_low[place[0] ^ (2 * step + 1)] = out[128:].astype(BF)


def proj_body(place, att, tok, proj_w, vecs, middle, normed, att_rows):
    rows = jnp.concatenate([att[k] for k in range(8)], 1)
    att_rows[...] = rows
    mid = tok[...].astype(F32) + mm(rows, proj_w[...]) + vecs[2:3, :]
    middle[...] = mid
    hat, _ = standardize(mid)
    low = (hat * vecs[3:4, :] + vecs[4:5, :]).astype(BF)
    normed[...] = low


def proj_grad(place, att, d_b, vectors, send, keep):
    grad = outer_sum(att, d_b)
    row = lax.broadcasted_iota(jnp.int32, (32, 128), 0)
    for owner in range(32):
        x, core, k = owner // 16, (owner // 8) % 2, owner % 8
        rows = grad[32 * owner : 32 * owner + 32]
        extra = jnp.zeros((32, 128), F32)
        first = 128 * (owner // 4)
        for m in range(4):
            extra = jnp.where(row == m, vectors[m : m + 1, first : first + 128], extra)
        group = 2 * x + core
        last = vectors[4 + group : 5 + group, 128 * k : 128 * k + 128]
        extra = jnp.where(row == 4, last, extra)
        rel = place[0] ^ k
        slot = (rel & 1) * 4 + (rel >> 2) * 2 + ((rel >> 1) & 1)
        for side, out in ((core == place[2], keep), (core != place[2], send)):

            @pl.when(side)
            def _():
                out[place[1] ^ x, slot, :, :1024] = rows.astype(BF)
                out[place[1] ^ x, slot, :, 1024:] = extra.astype(BF)


def mlp_body(
    place, normed, d_act, up_w, vecs, middle, cot, proj_w, down_bias, att,
    active, d_mid, d_att, proj_send, proj_keep, acc, vectors,
):
    step = pl.program_id(0)
    hidden = mm(normed[...], up_w[...]) + vecs[pl.ds(8 + step, 1), :]
    act, slope = gelu_both(hidden)
    active[...] = act.astype(BF)
    d_hidden = (d_act[...] * slope).astype(BF)
    vectors[pl.ds(4 + step, 1), :] = jnp.sum(d_hidden.astype(F32), 0, keepdims=True)
    part = times_transposed(d_hidden, up_w[...])

    @pl.when(step == 0)
    def _():
        acc[...] = part

    @pl.when(step > 0)
    def _():
        acc[...] += part

    @pl.when(step == pl.num_programs(0) - 1)
    def _():
        up = acc[...]
        hat, inv = standardize(middle[...])
        e = up * vecs[3:4, :]
        inner = e - jnp.mean(e, -1, keepdims=True) - hat * jnp.mean(e * hat, -1, keepdims=True)
        d_m = cot[...].astype(F32) + inv * inner
        d_mid[...] = d_m
        d_b = d_m.astype(BF)
        vectors[0:1, :] = jnp.sum(up * hat, 0, keepdims=True)
        vectors[1:2, :] = jnp.sum(up, 0, keepdims=True)
        vectors[2:3, :] = jnp.sum(d_b.astype(F32), 0, keepdims=True)
        vectors[3:4, :] = down_bias[...]
        d_a = times_transposed(d_b, proj_w[...]).astype(BF)
        for k in range(8):
            d_att[k] = d_a[:, 128 * k : 128 * k + 128]
        proj_grad(place, att[...], d_b, vectors, proj_send, proj_keep)


def mlp_grad_body(place, *refs):
    blocks, cots, ups, downs = refs[:8], refs[8:16], refs[16:20], refs[20:24]
    vecs, down_keep, down_send, up_keep, up_send, n_all, c_all, u_all, d_all, grad = refs[24:]
    for j in range(8):
        n_all[128 * j : 128 * j + 128, :] = blocks[j][...]
        c_all[128 * j : 128 * j + 128, :] = cots[j][...]
    lanes = pl.ds(pl.multiple_of(place[0] * 128, 128), 128)
    up_b = []
    rows = vecs[8:12, lanes]
    biases = lax.broadcasted_iota(jnp.int32, (4, 128), 0)
    for g in range(4):
        u_all[:, 128 * g : 128 * g + 128] = ups[g][...]
        d_all[128 * g : 128 * g + 128, :] = downs[g][...]
        group = (place[1] ^ (g & 1)) * 2 + (place[2] ^ (g >> 1))
        up_b.append(jnp.sum(jnp.where(biases == group, rows, 0.0), 0, keepdims=True))
    n = n_all[...]
    c = c_all[...]
    act, slope = gelu_both(mm(n, u_all[...]) + jnp.concatenate(up_b, 1))
    grad_down = outer_sum(act.astype(BF), c)
    for g in range(4):
        rows = grad_down[128 * g : 128 * g + 128]
        if g < 2:
            down_keep[g] = rows.astype(BF)
        else:
            down_send[g - 2] = rows.astype(BF)
    d_hidden = (times_transposed(c, d_all[...]) * slope).astype(BF)
    both = outer_sum(n, d_hidden)
    for g in range(4):
        group = ((place[1] ^ (g & 1)) * 2) + (place[2] ^ (g >> 1))
        lanes = pl.ds(pl.multiple_of(group * 128, 128), 128)
        grad[:, lanes] = both[:, 128 * g : 128 * g + 128]
    for rx in range(2):
        first = (place[1] ^ rx) * 512
        keep = pl.multiple_of(first + place[2] * 256, 256)
        send = pl.multiple_of(first + (1 - place[2]) * 256, 256)
        up_keep[rx] = grad[pl.ds(keep, 256), :].astype(BF)
        up_send[rx] = grad[pl.ds(send, 256), :].astype(BF)


def attend_back_body(
    place, probs, d_att, att_f, row_scale, q, k_all, v_all, cos, sin, d_all, bias_part, dq, dk, dv
):
    step = pl.program_id(0)
    keys = k_all[...]
    values = v_all[...]
    queries = q[...]
    d_out = jnp.concatenate([d_att[place[0] ^ (2 * step)], d_att[place[0] ^ (2 * step + 1)]], 0)
    scaled = d_out.astype(F32) * row_scale[...]
    d_out = scaled.astype(BF)
    products = (d_out.astype(F32) * att_f[...]).T
    key_parts, value_parts, query_parts = [], [], []
    for head in range(2):
        weights = probs[head]
        mine = jnp.where(head_mask(d_out.shape, head), d_out, jnp.zeros_like(d_out))
        delta = jnp.sum(products[64 * head : 64 * head + 64], 0, keepdims=True)
        d_weights = times_transposed(values, mine)
        d_scores = (weights.astype(F32) * (d_weights - delta)).astype(BF)
        key_parts.append(mm(d_scores, queries))
        value_parts.append(mm(weights, d_out))
        query_parts.append(outer_sum(keys, d_scores)[64 * head : 64 * head + 64])
    first = head_mask((1024, 128), 0)
    dk_new = jnp.where(first, key_parts[0], key_parts[1])
    dv_new = jnp.where(first, value_parts[0], value_parts[1])
    dq[pl.ds(pl.multiple_of(step * 256, 256), 256), :] = jnp.concatenate(query_parts, 0).T

    @pl.when(step == 0)
    def _():
        dk[...] = dk_new
        dv[...] = dv_new

    @pl.when(step > 0)
    def _():
        dk[...] += dk_new
        dv[...] += dv_new

    @pl.when(step == pl.num_programs(0) - 1)
    def _():
        total = jnp.zeros((1, 384), F32)
        for j in range(8):
            rows = slice(128 * j, 128 * j + 128)
            c = cos[rows, :]
            sn = sin[rows, :]
            back_q = 0.125 * dq[rows, :]
            back_k = dk[rows, :]
            piece = jnp.concatenate(
                [
                    back_q * c - swap_halves(back_q) * sn,
                    back_k * c - swap_halves(back_k) * sn,
                    dv[rows, :],
                ],
                1,
            ).astype(BF)
            d_all[place[0] ^ j] = piece
            total = total + jnp.sum(piece.astype(F32), 0, keepdims=True)
        bias_part[...] = total


def rel_block(step, place):
    rel = jnp.where(step < 2, 2, 0) + step % 2
    return ((rel & 1) ^ place[1]) * 2 + ((rel >> 1) ^ place[2])


def qkv_grad_body(place, h0, h1, d_all, bias_part, vecs, wq, wk, wv, send, keep):
    step = pl.program_id(0)
    d_near = jnp.concatenate([d_all[place[0] ^ j] for j in range(4)], 0)
    d_far = jnp.concatenate([d_all[place[0] ^ j] for j in range(4, 8)], 0)
    inner = outer_sum(h0[...], d_near) + outer_sum(h1[...], d_far)
    total = bias_part[...]
    w = jnp.concatenate([wq[...], wk[...], wv[...]], 1).astype(F32)
    columns = vecs[...].T
    gain = columns[:, 0:1]
    shift = columns[:, 1:2]
    grad = gain * inner + shift * total
    row = lax.broadcasted_iota(jnp.int32, (256, 128), 0) % 32
    lane = lax.broadcasted_iota(jnp.int32, (256, 128), 1)
    extra = jnp.where(
        lane == 0,
        jnp.sum(w * inner, 1, keepdims=True),
        jnp.where(lane == 1, jnp.sum(w * total, 1, keepdims=True), 0.0),
    )
    for m in range(6):
        part = total[:, 128 * (m // 2) : 128 * (m // 2) + 128]
        part = part if m % 2 else pltpu.roll(part, 64, 1)
        extra = jnp.where((row == m) & (lane >= 64), part, extra)

    @pl.when(step < 2)
    def _():
        send[0, :, :384] = grad.astype(BF)
        send[0, :, 384:] = extra.astype(BF)

    @pl.when(step >= 2)
    def _():
        keep[0, :, :384] = grad.astype(BF)
        keep[0, :, 384:] = extra.astype(BF)


def pair_body(place, keep, came, left, send):
    half = left.shape[0]
    total = (keep[...].astype(F32) + came[...].astype(F32)).astype(BF)
    left[...] = total[:half]
    send[...] = total[half:]


def low_body(place, up_left, up_came, qkv_left, qkv_came, out):
    out[:, :32] = (up_left[...].astype(F32) + up_came[...].astype(F32)).astype(BF)
    out[:, 32:] = (qkv_left[...].astype(F32) + qkv_came[...].astype(F32)).astype(BF)


def merge_body(place, *refs):
    up, up_came, down, down_came, proj_left, proj_came = refs[:6]
    left, send, down_left, down_send, proj_keep, proj_send = refs[6:]
    proj_keep[...] = (proj_left[:2].astype(F32) + proj_came[:2].astype(F32)).astype(BF)
    proj_send[...] = (proj_left[2:].astype(F32) + proj_came[2:].astype(F32)).astype(BF)
    for side, low, low_down in ((0, left, down_left), (1, send, down_send)):
        total = (up[side].astype(F32) + up_came[side].astype(F32)).astype(BF)
        for k in range(8):
            low[k] = total[32 * k : 32 * k + 32]
        low_down[...] = (down[side].astype(F32) + down_came[side].astype(F32)).astype(BF)


def finish_body(place, came, grad_up, grad_qkv, gain, shift, bias):
    total = jnp.zeros((32, 128), F32)
    low = lax.broadcasted_iota(jnp.int32, (1, 128), 1) < 64
    parts = ([], [], [])
    for k in range(8):
        for g in range(4):
            lanes = slice(1024 * g + 128 * k, 1024 * g + 128 * k + 128)
            grad_up[:, lanes] = came[k, :32, 128 * g : 128 * g + 128].astype(F32)
            if g < 3:
                grad_qkv[:, lanes] = came[k, 32:, 128 * g : 128 * g + 128].astype(F32)
        extra = came[k, 32:, 384:].astype(F32)
        total = total + extra
        for p in range(3):
            left = pltpu.roll(extra[2 * p : 2 * p + 1], 64, 1)
            both = jnp.where(low, left, extra[2 * p + 1 : 2 * p + 2])
            parts[p].append(both)
    turned = total.T
    gain[...] = turned[0:1]
    shift[...] = turned[1:2]
    row = jnp.broadcast_to(jnp.concatenate(parts[0] + parts[1] + parts[2], 1), (8, 3072))
    me = place[1] * 16 + place[2] * 8 + place[0]
    bias[...] = pltpu.roll(row, lax.rem(3072 - me * 96, 3072), 1)[0:1, :96]


def out_body(place, active, down, middle, vecs, out, acc):
    step = pl.program_id(0)
    part = mm(active[...], down[...])

    @pl.when(step == 0)
    def _():
        acc[...] = part + middle[...] + vecs[5:6, :]

    @pl.when(step > 0)
    def _():
        acc[...] += part

    @pl.when(step == pl.num_programs(0) - 1)
    def _():
        out[...] = acc[...].astype(BF)


def last_body(place, came, w, tok, d_mid, vecs, out, acc):
    step = pl.program_id(0)
    for p in range(3):

        @pl.when(step == p)
        def _():
            d_mixed = jnp.concatenate([came[k, :, 128 * p : 128 * p + 128] for k in range(8)], 1)
            part = times_transposed(d_mixed, w[...])
            if p == 0:
                acc[...] = part
            elif p == 1:
                acc[...] += part
            else:
                up = acc[...] + part
                hat, inv = standardize(tok[...].astype(F32))
                e = up * vecs[0:1, :]
                mean = jnp.mean(e, -1, keepdims=True)
                inner = e - mean - hat * jnp.mean(e * hat, -1, keepdims=True)
                out[...] = d_mid[...] + inv * inner


def frequency_rows():
    rows = np.zeros((8, 128), np.float32)
    for lane in range(128):
        pair = lane % 32
        part, rank, count = (0, pair, 10) if pair < 10 else ((1, pair - 10, 11) if pair < 21 else (2, pair - 21, 11))
        rows[part, lane] = 10000.0 ** (-rank / count)
        rows[3, lane] = -1.0 if lane % 64 < 32 else 1.0
    return rows


def clip_starts(place, pos):
    ids = jnp.zeros_like(pos)
    start = jnp.zeros_like(pos)
    end = jnp.int32(0)
    for c in range(8):
        length = place[8 + c]
        end = end + length
        past = pos >= end.astype(F32)
        ids = jnp.where(past, ids + 1.0, ids)
        start = jnp.where(past, end.astype(F32), start)
    return ids, start


def prep_body(place, freq, cos, sin, id_col, id_row):
    for j in range(8):
        first = ((place[0] ^ j) * 128).astype(F32)
        rows = slice(128 * j, 128 * j + 128)
        pos = first + lax.broadcasted_iota(jnp.int32, (128, 128), 0).astype(F32)
        ids, start = clip_starts(place, pos)
        id_col[rows, :] = ids
        within = pos - start
        row14 = jnp.floor((within + 0.5) * (1.0 / 14.0))
        t = jnp.floor((within + 0.5) * (1.0 / 196.0))
        angle = t * freq[0:1, :] + (row14 - 14.0 * t) * freq[1:2, :] + (within - 14.0 * row14) * freq[2:3, :]
        cos[rows, :] = jnp.cos(angle)
        sin[rows, :] = jnp.sin(angle) * freq[3:4, :]
        flat = first + lax.broadcasted_iota(jnp.int32, (8, 128), 1).astype(F32)
        id_row[:, 128 * j : 128 * j + 128] = clip_starts(place, flat)[0]


def after(value, *others):
    return lax.optimization_barrier((value, *others))[0]


def spread_four(a):
    return [a, swap_over(a, "y"), swap_over(a, "zl"), swap_over(a, "zl", "y")]


def fast_shards(
    tokens_in, clip_lengths, attn_gain, attn_shift, qkv_weight, qkv_bias, proj_weight, proj_bias,
    mlp_gain, mlp_shift, up_weight, up_bias, down_weight, down_bias, out_cotangent,
):
    x, core, zh, zl, y = (lax.axis_index(name) for name in AXES)
    k = zh * 4 + zl * 2 + y
    me = x * 16 + core * 8 + k
    place = jnp.concatenate(
        [jnp.stack([k, x, core, k, k, k, k, k]).astype(jnp.int32), clip_lengths[0]]
    )
    tok = tokens_in[0]
    cot = out_cotangent[0]

    far_tok = swap_over(tok, "zh")
    near = spread_four(tok)
    rows = [attn_gain, attn_shift, proj_bias, mlp_gain, mlp_shift, down_bias, down_bias, down_bias]
    vecs = jnp.concatenate([v.astype(F32).reshape(-1, 1024) for v in (*rows, up_bias, qkv_bias)], 0)
    cos_tab, sin_tab, id_col, id_row = one_step(
        prep_body,
        [arr((1024, 128), F32), arr((1024, 128), F32), arr((1024, 128), F32), arr((8, 1024), F32)],
        [],
        PIN,
        place,
        (jnp.asarray(frequency_rows()),),
    )
    far_tok, cos_tab, vecs, *near = lax.optimization_barrier((far_tok, cos_tab, vecs, *near))
    far = spread_four(far_tok)

    def table_half(part):
        return pl.BlockSpec((512, 128), lambda i, s: (part, 0))

    half = arr((512, 128), BF)
    full = arr((1024, 128), BF)
    common = (vecs, qkv_weight, qkv_weight, qkv_weight, cos_tab, sin_tab)
    columns_of = [pl.BlockSpec((1024, 128), lambda i, s, p=p: (0, 8 * p + s[0])) for p in range(3)]

    def qkv(body, part, blocks, more, outs):
        specs = [whole(v.shape) for v in (*blocks, vecs)] + columns_of
        specs += [table_half(part), table_half(part)] + [whole(v.shape) for v in more]
        return call(
            body, (1,), specs, [whole(o.shape) for o in outs], outs,
            [pltpu.VMEM((512, 1024), BF)], PIN, place, (*blocks, *common, *more),
        )

    hat0, q0, k0, v0 = qkv(near_body, 0, near, (), [arr((512, 1024), BF), half, half, half])
    d_act, down_bias_part = call(
        down_back_body,
        (4,),
        [whole((128, 1024)), pl.BlockSpec((1024, 1024), lambda i, s: (i, 0))],
        [pl.BlockSpec((128, 1024), lambda i, s: (0, i)), whole((1, 1024))],
        [arr((128, 4096), F32), arr((1, 1024), F32)],
        [],
        PIN,
        place,
        (after(cot, q0), down_weight),
    )
    far = lax.optimization_barrier((q0, d_act, *far))[2:]
    cot_here = after(cot, q0)
    far_cot = swap_over(cot_here, "zh")
    cots = spread_four(cot_here)
    hat1, q_all, k_all, v_all = qkv(
        far_body, 1, far, (q0, k0, v0), [arr((512, 1024), BF), full, full, full]
    )
    step_rows = pl.BlockSpec((256, 128), lambda i, s: (i, 0))
    flat = whole((1024, 128))
    att_f, att_low, probs, row_scale = call(
        attend_body,
        (4,),
        [
            step_rows, flat, flat, flat, pl.BlockSpec((8, 256), lambda i, s: (0, i)),
        ],
        [step_rows, whole((8, 128, 128)), pl.BlockSpec((2, 1024, 256), lambda i, s: (0, 0, i)),
         step_rows],
        [arr((1024, 128), F32), arr((8, 128, 128), BF), arr((2, 1024, 1024), BF),
         arr((1024, 128), F32)],
        [],
        PIN,
        place,
        (q_all, k_all, v_all, id_col, id_row),
    )
    att_low, far_cot, *cots = lax.optimization_barrier((att_low, far_cot, *cots))
    att_in = lax.all_to_all(att_low, ROW, 0, 0, tiled=True)
    cots += [far_cot, swap_over(far_cot, "y"), swap_over(far_cot, "zl")]
    middle, normed2, att_rows = one_step(
        proj_body,
        [arr((128, 1024), F32), arr((128, 1024), BF), arr((128, 1024), BF)],
        [],
        PIN,
        place,
        (att_in, tok, proj_weight, vecs),
        LOW_PIN,
    )
    normed2, *cots = lax.optimization_barrier((normed2, *cots))
    far_n = swap_over(normed2, "zh")
    near_n = spread_four(normed2)
    wide = pl.BlockSpec((128, 1024), lambda i, s: (0, i))
    fixed = whole((128, 1024))
    active, d_mid, d_att, proj_send, proj_keep = call(
        mlp_body,
        (4,),
        [
            fixed, wide, wide_columns(), whole((15, 1024)), fixed, fixed, whole((1024, 1024)),
            whole((1, 1024)), fixed,
        ],
        [wide, fixed, whole((8, 128, 128)), whole((2, 8, 32, 1152)), whole((2, 8, 32, 1152))],
        [
            arr((128, 4096), BF), arr((128, 1024), F32), arr((8, 128, 128), BF),
            arr((2, 8, 32, 1152), BF), arr((2, 8, 32, 1152), BF),
        ],
        [pltpu.VMEM((128, 1024), F32), pltpu.VMEM((8, 1024), F32)],
        LOW_PIN,
        place,
        (normed2, d_act, up_weight, vecs, middle, cot, proj_weight, down_bias_part, att_rows),
    )
    d_att, far_n, far_y, active, proj_send, *near_n = lax.optimization_barrier(
        (d_att, far_n, cots[5], active, proj_send, *near_n)
    )
    last_cot = swap_over(far_y, "zl")
    d_att_in = lax.all_to_all(d_att, ROW, 0, 0, tiled=True)

    far_n = spread_four(far_n)

    def pair(keep, came):
        half = arr((keep.shape[0] // 2, *keep.shape[1:]), BF)
        return one_step(pair_body, [half, half], [], NO_PIN, place, (keep, came))

    flat_proj = (16, 32, 1152)
    proj_left, proj_low = pair(
        proj_keep.reshape(flat_proj), swap_over(proj_send.reshape(flat_proj), "core")
    )

    d_all, qkv_bias_part = call(
        attend_back_body,
        (4,),
        [
            pl.BlockSpec((2, 1024, 256), lambda i, s: (0, 0, i)), whole((8, 128, 128)), step_rows,
            step_rows, step_rows, flat, flat, flat, flat,
        ],
        [whole((8, 128, 384)), whole((1, 384))],
        [arr((8, 128, 384), BF), arr((1, 384), F32)],
        [pltpu.VMEM((1024, 128), F32)] * 3,
        PIN,
        place,
        (probs, after(d_att_in, proj_low), att_f, row_scale, q_all, k_all, v_all, cos_tab, sin_tab),
    )
    block_of = lambda i, s: (rel_block(i, s), 0)
    lanes_of = lambda i, s: (0, rel_block(i, s))
    send, keep = call(
        qkv_grad_body,
        (4,),
        [
            pl.BlockSpec((512, 256), lanes_of), pl.BlockSpec((512, 256), lanes_of),
            whole((8, 128, 384)), whole((1, 384)), pl.BlockSpec((8, 256), lanes_of),
        ]
        + [pl.BlockSpec((256, 128), lambda i, s, p=p: (rel_block(i, s), 8 * p + s[0])) for p in range(3)],
        [
            pl.BlockSpec((1, 256, 512), lambda i, s: (jnp.minimum(i, 1), 0, 0)),
            pl.BlockSpec((1, 256, 512), lambda i, s: (jnp.maximum(i - 2, 0), 0, 0)),
        ],
        [arr((2, 256, 512), BF), arr((2, 256, 512), BF)],
        [],
        PIN,
        place,
        (hat0, hat1, d_all, qkv_bias_part, vecs, qkv_weight, qkv_weight, qkv_weight),
    )
    def turn(value):
        return lax.all_to_all(value, ROW, 0, 0, tiled=True)
    d_all, send, last_cot, *far_n = lax.optimization_barrier((d_all, send, last_cot, *far_n))
    moved = lax.all_to_all(d_all, ROW, 0, 0, tiled=True)
    proj_left, proj_low = pair(after(proj_left, d_all), swap_over(proj_low, "x"))

    flat_qkv = (16, 32, 512)
    qkv_left, qkv_low = pair(
        keep.reshape(flat_qkv), swap_over(send.reshape(flat_qkv), "core")
    )
    qkv_came = swap_over(qkv_low, "x")

    def group_of(s, g):
        return (s[1] ^ (g & 1)) * 16 + (s[2] ^ (g >> 1)) * 8 + s[0]

    outs = [
        arr((2, 128, 1024), BF), arr((2, 128, 1024), BF), arr((2, 256, 512), BF),
        arr((2, 256, 512), BF),
    ]
    down_keep, down_send, up_keep, up_send = call(
        mlp_grad_body,
        (1,),
        [fixed] * 16
        + [pl.BlockSpec((1024, 128), lambda i, s, g=g: (0, group_of(s, g))) for g in range(4)]
        + [pl.BlockSpec((128, 1024), lambda i, s, g=g: (group_of(s, g), 0)) for g in range(4)]
        + [whole((15, 1024))],
        [whole(o.shape) for o in outs],
        outs,
        [
            pltpu.VMEM((1024, 1024), BF), pltpu.VMEM((1024, 1024), BF),
            pltpu.VMEM((1024, 512), BF), pltpu.VMEM((512, 1024), BF), pltpu.VMEM((1024, 512), F32),
        ],
        LOW_PIN,
        place,
        (after(near_n[0], d_all, proj_low, qkv_low), *near_n[1:], *far_n, *cots, last_cot, *([up_weight] * 4), *([down_weight] * 4), vecs),
    )


    up_send, down_send, proj_came, qkv_came = lax.optimization_barrier(
        (up_send, down_send, swap_over(proj_low, "y"), qkv_came)
    )
    left, low_send, down_left, down_low, proj_left, proj_low = one_step(
        merge_body,
        [arr((8, 32, 512), BF)] * 2 + [arr((128, 1024), BF)] * 2 + [arr((2, 32, 1152), BF)] * 2,
        [],
        PIN,
        place,
        (
            after(up_keep, moved), swap_over(up_send, "core"),
            down_keep, swap_over(down_send, "core"), proj_left, proj_came,
        ),
        NO_PIN,
    )
    low_came = swap_over(low_send, "x")
    (tokens_grad,) = call(
        last_body,
        (3,),
        [
            whole((8, 128, 384)), pl.BlockSpec((1024, 1024), lambda i, s: (0, i)), fixed, fixed,
            whole((15, 1024)),
        ],
        [fixed],
        [arr((128, 1024), F32)],
        [pltpu.VMEM((128, 1024), F32)],
        PIN,
        place,
        (after(moved, left), qkv_weight, tok, d_mid, vecs),
    )

    left, low_came, _ = lax.optimization_barrier((left, low_came, tokens_grad))
    (lows,) = one_step(
        low_body, [arr((8, 64, 512), BF)], [], NO_PIN, place, (left, low_came, qkv_left, qkv_came)
    )
    came = turn(lows)
    proj_left, proj_low = pair(after(proj_left, lows), swap_over(proj_low, "zh"))
    proj_came = swap_over(proj_low, "zl")
    down_low, _ = lax.optimization_barrier((down_low, lows))
    grad_down = down_left.astype(F32) + swap_over(down_low, "x").astype(F32)
    proj_total = proj_left[0].astype(F32) + proj_came[0].astype(F32)
    (layer_out,) = call(
        out_body,
        (4,),
        [wide, pl.BlockSpec((1024, 1024), lambda i, s: (i, 0)), fixed, whole((15, 1024))],
        [fixed],
        [arr((128, 1024), BF)],
        [pltpu.VMEM((128, 1024), F32)],
        PIN,
        place,
        (after(active, lows), down_weight, middle, vecs),
    )
    layer_out = layer_out[None]
    grad_proj = proj_total[:, :1024]
    own = lax.dynamic_slice(proj_total[:4, 1024:], (0, (me % 4) * 32), (4, 32))
    grad_up_b = proj_total[4, 1024:]

    grad_up, grad_qkv, gain_sum, shift_sum, grad_qkv_b = one_step(
        finish_body,
        [arr((32, 4096), F32), arr((32, 3072), F32), arr((1, 32), F32), arr((1, 32), F32), arr((1, 96), F32)],
        [],
        NO_PIN,
        place,
        (came,),
    )

    return (
        layer_out, tokens_grad[None], gain_sum[0], shift_sum[0], grad_qkv, grad_qkv_b[0], grad_proj,
        own[2], own[0], own[1], grad_up, grad_up_b, grad_down, own[3],
    )


def wide_columns():
    return pl.BlockSpec((1024, 1024), lambda i, s: (0, i))


def fast_solution(mesh):
    wide_mesh = Mesh(mesh.devices.reshape(2, 2, 2, 2, 2), AXES)
    batch, blk = AXES[:2], AXES[2:]
    spread = P(batch, blk, None)
    return jax.shard_map(
        fast_shards,
        mesh=wide_mesh,
        in_specs=(spread, P(batch, None)) + (P(),) * 12 + (spread,),
        out_specs=(spread, spread)
        + tuple(P(AXES, None) if i in (2, 4, 8, 10) else P(AXES) for i in range(12)),
        check_vma=False,
    )


def solution(mesh):
    if tuple(mesh.devices.shape) == (4, 8):
        return fast_solution(mesh)
    placed = (
        P("batch", "blk", None),
        P("batch", None),
        P(),
        P(),
        P(),
        P(),
        P(),
        P(),
        P(),
        P(),
        P(),
        P(),
        P(),
        P(),
        P("batch", "blk", None),
    )
    return jax.shard_map(
        shards,
        mesh=mesh,
        in_specs=placed,
        out_specs=(
            P("batch", "blk", None),
            P("batch", "blk", None),
            P(("batch", "blk")),
            P(("batch", "blk")),
            P(("batch", "blk"), None),
            P(("batch", "blk")),
            P(("batch", "blk"), None),
            P(("batch", "blk")),
            P(("batch", "blk")),
            P(("batch", "blk")),
            P(("batch", "blk"), None),
            P(("batch", "blk")),
            P(("batch", "blk"), None),
            P(("batch", "blk")),
        ),
        check_vma=False,
    )
```

```python
import math

import jax
import jax.numpy as jnp
import numpy as np
from jax import lax
from jax.experimental import pallas as pl
from jax.experimental.pallas import tpu as pltpu
from jax.sharding import Mesh
from jax.sharding import PartitionSpec as P

H = 16
HD = 64


NEG_FILL = -1e30


def pair_table():
    part_map = [0] * 10 + [1] * 11 + [2] * 11
    freq_list = [10000.0 ** (-rank / 10.0) for rank in range(10)] + [
        10000.0 ** (-rank / 11.0) for rank in range(11)
    ] * 2
    table_rows = [
        [freq_list[column] if part_map[column] == axis_id else 0.0 for column in range(32)]
        for axis_id in range(3)
    ]
    return jnp.array(table_rows, dtype=jnp.float32)


def clip_of(lengths_row, positions):
    clip_end = jnp.cumsum(lengths_row)
    return jnp.sum((positions[:, None] >= clip_end[None, :]).astype(jnp.int32), axis=1)


def clip_layout(lengths_row, positions):
    clip_end = jnp.cumsum(lengths_row)
    starts = clip_end - lengths_row
    clip_ids = jnp.sum((positions[:, None] >= clip_end[None, :]).astype(jnp.int32), axis=1)
    member = clip_ids[:, None] == jnp.arange(lengths_row.shape[0], dtype=jnp.int32)[None, :]
    within = positions - jnp.sum(jnp.where(member, starts[None, :], 0), axis=1)
    coords = jnp.stack([within // 196, within // 14 % 14, within % 14], axis=1).astype(jnp.float32)
    angles = jnp.dot(coords, pair_table(), precision=lax.Precision.HIGHEST)
    return (clip_ids, jnp.cos(angles), jnp.sin(angles))


def rotate(values, cos_tab, sin_tab):
    half_dim = values.shape[-1] // 2
    first_half = values[..., :half_dim]
    second_half = values[..., half_dim:]
    cos_b = cos_tab[:, None, :]
    sin_b = sin_tab[:, None, :]
    return jnp.concatenate(
        [first_half * cos_b - second_half * sin_b, first_half * sin_b + second_half * cos_b],
        axis=-1,
    )


def norm_fwd(values, gain_vec, shift_vec):
    row_mean = jnp.mean(values, -1, keepdims=True)
    centered = values - row_mean
    inv_std = lax.rsqrt(jnp.mean(centered * centered, -1, keepdims=True) + 1e-06)
    normalized = centered * inv_std
    return (normalized * gain_vec + shift_vec, normalized, inv_std)


def norm_back(upstream, normalized, inv_std, gain_vec):
    scaled = upstream * gain_vec
    inner = (
        scaled
        - jnp.mean(scaled, -1, keepdims=True)
        - normalized * jnp.mean(scaled * normalized, -1, keepdims=True)
    )
    return (inv_std * inner, jnp.sum(upstream * normalized, 0), jnp.sum(upstream, 0))


def outer_sum(left, right):
    return lax.dot_general(
        left, right, (((0,), (0,)), ((), ())), preferred_element_type=jnp.float32
    )


def times_transposed(left, right):
    return lax.dot_general(
        left, right, (((1,), (1,)), ((), ())), preferred_element_type=jnp.float32
    )


def add_rows(buffer, block, first_key):
    current = lax.dynamic_slice_in_dim(buffer, first_key, block.shape[0], 0)
    return lax.dynamic_update_slice_in_dim(buffer, current + block, first_key, 0)


def in_blocks(block_step, running, pieces):
    row_count = pieces[0].shape[0]
    block_rows = math.gcd(row_count, 2048)

    def advance(block_idx, state):
        first_row = block_idx * block_rows
        sliced = tuple(
            (lax.dynamic_slice_in_dim(piece, first_row, block_rows, 0) for piece in pieces)
        )
        return block_step(state, sliced, first_row)

    return lax.fori_loop(0, row_count // block_rows, advance, running)


def shards(
    tokens_in,
    clip_lengths,
    attn_gain,
    attn_shift,
    qkv_weight,
    qkv_bias,
    proj_weight,
    proj_bias,
    mlp_gain,
    mlp_shift,
    up_weight,
    up_bias,
    down_weight,
    down_bias,
    out_cotangent,
):
    tok_rows = tokens_in.shape[1]
    model_width = tokens_in.shape[2]
    seq_len = tok_rows * lax.axis_size("blk")
    lens_row = clip_lengths[0]
    own_pos = lax.axis_index("blk") * tok_rows + jnp.arange(tok_rows, dtype=jnp.int32)
    clip_q, cos_tab, sin_tab = clip_layout(lens_row, own_pos)
    residual = tokens_in[0].astype(jnp.float32)
    attn_gain_f = attn_gain.astype(jnp.float32)
    mlp_gain_f = mlp_gain.astype(jnp.float32)
    normed, hat_one, inv_one = norm_fwd(residual, attn_gain_f, attn_shift.astype(jnp.float32))
    normed_low = normed.astype(jnp.bfloat16)
    qkv_mixed = jnp.dot(
        normed_low, qkv_weight, preferred_element_type=jnp.float32
    ) + qkv_bias.astype(jnp.float32)
    query_h = rotate(qkv_mixed[:, :model_width].reshape(tok_rows, H, HD), cos_tab, sin_tab).astype(
        jnp.bfloat16
    )
    key_low = (
        rotate(
            qkv_mixed[:, model_width : 2 * model_width].reshape(tok_rows, H, HD), cos_tab, sin_tab
        )
        .astype(jnp.bfloat16)
        .reshape(tok_rows, model_width)
    )
    value_low = qkv_mixed[:, 2 * model_width :].astype(jnp.bfloat16)

    def block_scores(keys_blk, first_key):
        key_count = keys_blk.shape[0]
        clip_k = clip_of(lens_row, first_key + jnp.arange(key_count, dtype=jnp.int32))
        raw_scores = jnp.einsum(
            "qhd,khd->hqk",
            query_h,
            keys_blk.reshape(key_count, H, HD),
            preferred_element_type=jnp.float32,
        )
        allowed = (clip_q[:, None] == clip_k[None, :])[None]
        return (jnp.where(allowed, 0.125 * raw_scores, NEG_FILL), allowed)

    def stats_step(state, sliced, first_key):
        row_max, row_sum = state
        scores, allowed = block_scores(sliced[0], first_key)
        new_max = jnp.maximum(row_max, jnp.max(scores, -1))
        weights = jnp.where(allowed, jnp.exp(scores - new_max[:, :, None]), 0.0)
        return (new_max, row_sum * jnp.exp(row_max - new_max) + jnp.sum(weights, -1))

    stats_init = (
        jnp.full((H, tok_rows), NEG_FILL, jnp.float32),
        jnp.zeros((H, tok_rows), jnp.float32),
    )
    row_max, row_sum = in_blocks(
        stats_step, stats_init, (lax.all_gather(key_low, "blk", axis=0, tiled=True),)
    )
    log_sum = row_max + jnp.log(row_sum)

    def output_step(acc_state, sliced, first_key):
        keys_blk, values_blk = sliced
        key_count = keys_blk.shape[0]
        scores, allowed = block_scores(keys_blk, first_key)
        weights = jnp.where(allowed, jnp.exp(scores - log_sum[:, :, None]), 0.0)
        return acc_state + jnp.einsum(
            "hqk,khd->qhd",
            weights.astype(jnp.bfloat16),
            values_blk.reshape(key_count, H, HD),
            preferred_element_type=jnp.float32,
        )

    acc_init = jnp.zeros((tok_rows, H, HD), jnp.float32)
    attended_f = in_blocks(
        output_step,
        acc_init,
        (
            lax.all_gather(key_low, "blk", axis=0, tiled=True),
            lax.all_gather(value_low, "blk", axis=0, tiled=True),
        ),
    )
    attended_low = attended_f.reshape(tok_rows, model_width).astype(jnp.bfloat16)
    middle = (
        residual
        + jnp.dot(attended_low, proj_weight, preferred_element_type=jnp.float32)
        + proj_bias.astype(jnp.float32)
    )
    normed_two, hat_two, inv_two = norm_fwd(middle, mlp_gain_f, mlp_shift.astype(jnp.float32))
    normed_two_low = normed_two.astype(jnp.bfloat16)
    hidden = jnp.dot(
        normed_two_low, up_weight, preferred_element_type=jnp.float32
    ) + up_bias.astype(jnp.float32)
    active_low = jax.nn.gelu(hidden).astype(jnp.bfloat16)
    result = (
        middle
        + jnp.dot(active_low, down_weight, preferred_element_type=jnp.float32)
        + down_bias.astype(jnp.float32)
    )
    layer_out = result.astype(jnp.bfloat16)[None]
    cot_low = out_cotangent[0]
    cot_f = cot_low.astype(jnp.float32)
    grad_down_w = outer_sum(active_low, cot_low)
    grad_down_b = jnp.sum(cot_f, 0)
    d_active = times_transposed(cot_low, down_weight)
    hidden_unused, gelu_back = jax.vjp(jax.nn.gelu, hidden)
    d_hidden = gelu_back(d_active)[0].astype(jnp.bfloat16)
    grad_up_w = outer_sum(normed_two_low, d_hidden)
    grad_up_b = jnp.sum(d_hidden.astype(jnp.float32), 0)
    d_normed_two = times_transposed(d_hidden, up_weight)
    d_mid_norm, grad_mlp_gain, grad_mlp_shift = norm_back(
        d_normed_two, hat_two, inv_two, mlp_gain_f
    )
    d_middle = cot_f + d_mid_norm
    d_branch = d_middle.astype(jnp.bfloat16)
    grad_proj_w = outer_sum(attended_low, d_branch)
    grad_proj_b = jnp.sum(d_branch.astype(jnp.float32), 0)
    d_attended = (
        times_transposed(d_branch, proj_weight).astype(jnp.bfloat16).reshape(tok_rows, H, HD)
    )
    delta = jnp.einsum("qhd,qhd->hq", d_attended.astype(jnp.float32), attended_f)

    def back_step(state, sliced, first_key):
        dq_acc, buffers = state
        keys_blk, values_blk = sliced
        key_count = keys_blk.shape[0]
        scores, allowed = block_scores(keys_blk, first_key)
        weights = jnp.where(allowed, jnp.exp(scores - log_sum[:, :, None]), 0.0)
        d_weights = jnp.einsum(
            "qhd,khd->hqk",
            d_attended,
            values_blk.reshape(key_count, H, HD),
            preferred_element_type=jnp.float32,
        )
        d_scores = (weights * (d_weights - delta[:, :, None])).astype(jnp.bfloat16)
        dq_acc = dq_acc + 0.125 * jnp.einsum(
            "hqk,khd->qhd",
            d_scores,
            keys_blk.reshape(key_count, H, HD),
            preferred_element_type=jnp.float32,
        )
        d_keys = 0.125 * jnp.einsum(
            "hqk,qhd->khd", d_scores, query_h, preferred_element_type=jnp.float32
        )
        d_values = jnp.einsum(
            "hqk,qhd->khd",
            weights.astype(jnp.bfloat16),
            d_attended,
            preferred_element_type=jnp.float32,
        )
        key_buffer = add_rows(buffers[0], d_keys.reshape(key_count, model_width), first_key)
        value_buffer = add_rows(buffers[1], d_values.reshape(key_count, model_width), first_key)
        buffers = (key_buffer, value_buffer)
        return (dq_acc, buffers)

    buffer_init = (
        jnp.zeros((seq_len, model_width), jnp.float32),
        jnp.zeros((seq_len, model_width), jnp.float32),
    )
    back_init = (jnp.zeros((tok_rows, H, HD), jnp.float32), buffer_init)
    d_queries, key_grads = in_blocks(
        back_step,
        back_init,
        (
            lax.all_gather(key_low, "blk", axis=0, tiled=True),
            lax.all_gather(value_low, "blk", axis=0, tiled=True),
        ),
    )
    d_keys_own, d_values_own = (
        lax.psum_scatter(key_grads[0], "blk", scatter_dimension=0, tiled=True),
        lax.psum_scatter(key_grads[1], "blk", scatter_dimension=0, tiled=True),
    )
    d_queries_pre = rotate(d_queries, cos_tab, -sin_tab).reshape(tok_rows, model_width)
    d_keys_pre = rotate(d_keys_own.reshape(tok_rows, H, HD), cos_tab, -sin_tab).reshape(
        tok_rows, model_width
    )
    d_mixed = jnp.concatenate([d_queries_pre, d_keys_pre, d_values_own], axis=1).astype(
        jnp.bfloat16
    )
    grad_qkv_w = outer_sum(normed_low, d_mixed)
    grad_qkv_b = jnp.sum(d_mixed.astype(jnp.float32), 0)
    d_normed = times_transposed(d_mixed, qkv_weight)
    d_res_norm, grad_attn_gain, grad_attn_shift = norm_back(d_normed, hat_one, inv_one, attn_gain_f)
    tokens_grad = (d_middle + d_res_norm)[None]
    summed = (
        lax.psum_scatter(grad_qkv_w, ("batch", "blk"), scatter_dimension=0, tiled=True),
        lax.psum_scatter(grad_proj_w, ("batch", "blk"), scatter_dimension=0, tiled=True),
        lax.psum_scatter(grad_up_w, ("batch", "blk"), scatter_dimension=0, tiled=True),
        lax.psum_scatter(grad_down_w, ("batch", "blk"), scatter_dimension=0, tiled=True),
        lax.psum_scatter(grad_attn_gain, ("batch", "blk"), scatter_dimension=0, tiled=True),
        lax.psum_scatter(grad_attn_shift, ("batch", "blk"), scatter_dimension=0, tiled=True),
        lax.psum_scatter(grad_qkv_b, ("batch", "blk"), scatter_dimension=0, tiled=True),
        lax.psum_scatter(grad_proj_b, ("batch", "blk"), scatter_dimension=0, tiled=True),
        lax.psum_scatter(grad_mlp_gain, ("batch", "blk"), scatter_dimension=0, tiled=True),
        lax.psum_scatter(grad_mlp_shift, ("batch", "blk"), scatter_dimension=0, tiled=True),
        lax.psum_scatter(grad_up_b, ("batch", "blk"), scatter_dimension=0, tiled=True),
        lax.psum_scatter(grad_down_b, ("batch", "blk"), scatter_dimension=0, tiled=True),
    )
    return (
        layer_out,
        tokens_grad,
        summed[4],
        summed[5],
        summed[0],
        summed[6],
        summed[1],
        summed[7],
        summed[8],
        summed[9],
        summed[2],
        summed[10],
        summed[3],
        summed[11],
    )


BF = jnp.bfloat16
F32 = jnp.float32
AXES = ("x", "core", "zh", "zl", "y")
ROW = ("zh", "zl", "y")
GELU_A = 0.7978845608028654
GELU_B = 0.044715
VMEM_MIB = 32
PIN = 400000
LOW_PIN = 200000
NO_PIN = 1 << 30


def mm(left, right):
    return jnp.dot(left, right, preferred_element_type=F32)


def swap_over(value, *names):
    mask = sum(16 >> AXES.index(name) for name in names)
    return lax.ppermute(value, AXES, [(i, i ^ mask) for i in range(32)])


def whole(shape):
    zeros = (0,) * len(shape)
    return pl.BlockSpec(shape, lambda *_: zeros)


def arr(shape, dtype):
    return jax.ShapeDtypeStruct(shape, dtype)


def call(
    body, grid, in_specs, out_specs, out_shape, scratch, pin, scalars, args, out_pin=None
):
    return pl.pallas_call(
        body,
        grid_spec=pltpu.PrefetchScalarGridSpec(
            num_scalar_prefetch=1,
            grid=grid,
            in_specs=in_specs,
            out_specs=out_specs,
            scratch_shapes=scratch,
        ),
        out_shape=[pltpu.HBM(o.shape, o.dtype) if big(o, out_pin or pin) else o for o in out_shape],
        compiler_params=pltpu.CompilerParams(vmem_limit_bytes=VMEM_MIB << 20),
        cost_estimate=pl.CostEstimate(flops=0, bytes_accessed=1024, transcendentals=0),
    )(scalars, *(pinned(v, pin) for v in args))


def big(v, pin):
    return math.prod(v.shape) * v.dtype.itemsize >= pin


def pinned(v, pin):
    return pltpu.with_memory_space_constraint(v, pltpu.HBM) if big(v, pin) else v


def one_step(body, outs, scratch, pin, scalars, args, out_pin=None):
    return call(
        body, (1,), [whole(v.shape) for v in args], [whole(o.shape) for o in outs], outs, scratch,
        pin, scalars, args, out_pin,
    )


def standardize(x):
    mean = jnp.mean(x, -1, keepdims=True)
    centered = x - mean
    inv = lax.rsqrt(jnp.mean(centered * centered, -1, keepdims=True) + 1e-06)
    return centered * inv, inv


def swap_halves(x):
    lane = lax.broadcasted_iota(jnp.int32, x.shape, 1)
    return jnp.where(lane % 64 < 32, pltpu.roll(x, 96, 1), pltpu.roll(x, 32, 1))


def gelu_both(h):
    t = jnp.tanh(h * (GELU_A + (GELU_A * GELU_B) * (h * h)))
    half = 0.5 * h
    act = half + half * t
    slope = (0.5 + 0.5 * t) + half * (1.0 - t * t) * (GELU_A + (3.0 * GELU_A * GELU_B) * (h * h))
    return act, slope


def down_back_body(place, cot, down, d_act, bias_part):
    @pl.when(pl.program_id(0) == 0)
    def _():
        bias_part[...] = jnp.sum(cot[...].astype(F32), 0, keepdims=True)

    d_act[...] = times_transposed(cot[...], down[...])


def qkv_half(place, blocks, vecs, ws, cos, sin, hat_out, normed):
    g = vecs[0:1, :]
    s = vecs[1:2, :]
    for j in range(4):
        rows = slice(128 * j, 128 * j + 128)
        hat, _ = standardize(blocks[j][...].astype(F32))
        hat_out[rows, :] = hat.astype(BF)
        normed[rows, :] = (hat * g + s).astype(BF)
    lanes = pl.ds(pl.multiple_of(place[0] * 128, 128), 128)
    bias3 = jnp.concatenate([vecs[12 + p : 13 + p, lanes] for p in range(3)], 1)
    mixed = mm(normed[...], jnp.concatenate([w[...] for w in ws], 1)) + bias3
    c = cos[...]
    sn = sin[...]
    q = mixed[:, :128]
    k = mixed[:, 128:256]
    return (
        ((q * c + swap_halves(q) * sn) * 0.125).astype(BF),
        (k * c + swap_halves(k) * sn).astype(BF),
        mixed[:, 256:].astype(BF),
    )


def near_body(place, *refs):
    blocks = refs[:4]
    vecs, wq, wk, wv, cos, sin, hat_out, q_out, k_out, v_out, normed = refs[4:]
    q, k, v = qkv_half(place, blocks, vecs, (wq, wk, wv), cos, sin, hat_out, normed)
    q_out[...] = q
    k_out[...] = k
    v_out[...] = v


def far_body(place, *refs):
    blocks = refs[:4]
    vecs, wq, wk, wv, cos, sin, q0, k0, v0, hat_out, q_out, k_out, v_out, normed = refs[4:]
    q, k, v = qkv_half(place, blocks, vecs, (wq, wk, wv), cos, sin, hat_out, normed)
    for out, near, far in ((q_out, q0, q), (k_out, k0, k), (v_out, v0, v)):
        out[:512, :] = near[...]
        out[512:, :] = far


def head_mask(shape, head):
    return lax.broadcasted_iota(jnp.int32, shape, 1) // 64 == head


def attend_body(place, q, k_all, v_all, id_col, id_row, att_f, att_low, probs, row_scale):
    keys = k_all[...]
    values = v_all[...]
    queries = q[...]
    own = id_col[...]
    allowed = jnp.concatenate([own] * 4, 1) == id_row[0:1, :]
    halves, scales = [], []
    for head in range(2):
        mine = jnp.where(head_mask(queries.shape, head), queries, jnp.zeros_like(queries))
        scores = jnp.where(allowed, times_transposed(keys, mine), NEG_FILL)
        weights = jnp.exp(scores - jnp.max(scores, 0, keepdims=True))
        low = weights.astype(BF)
        probs[head] = low
        scale = 1.0 / jnp.sum(weights, 0, keepdims=True)
        scales.append(scale)
        halves.append(outer_sum(values, low)[64 * head : 64 * head + 64] * scale)
    out = jnp.concatenate(halves, 0).T
    att_f[...] = out
    row_scale[...] = jnp.concatenate([jnp.broadcast_to(v, (64, 512)) for v in scales], 0).T
    step = pl.program_id(0)
    for m in range(4):
        att_low[place[0] ^ (4 * step + m)] = out[128 * m : 128 * m + 128].astype(BF)


def proj_body(place, att, tok, proj_w, vecs, middle, normed, att_rows):
    rows = jnp.concatenate([att[k] for k in range(8)], 1)
    att_rows[...] = rows
    mid = tok[...].astype(F32) + mm(rows, proj_w[...]) + vecs[2:3, :]
    middle[...] = mid
    hat, _ = standardize(mid)
    low = (hat * vecs[3:4, :] + vecs[4:5, :]).astype(BF)
    normed[...] = low


def proj_grad(place, att, d_b, vectors, send, keep):
    grad = outer_sum(att, d_b)
    row = lax.broadcasted_iota(jnp.int32, (32, 128), 0)
    for owner in range(32):
        x, core, k = owner // 16, (owner // 8) % 2, owner % 8
        rows = grad[32 * owner : 32 * owner + 32]
        extra = jnp.zeros((32, 128), F32)
        first = 128 * (owner // 4)
        for m in range(4):
            extra = jnp.where(row == m, vectors[m : m + 1, first : first + 128], extra)
        group = 2 * x + core
        last = vectors[4 + group : 5 + group, 128 * k : 128 * k + 128]
        extra = jnp.where(row == 4, last, extra)
        rel = place[0] ^ k
        slot = (rel & 1) * 4 + (rel >> 2) * 2 + ((rel >> 1) & 1)
        for side, out in ((core == place[2], keep), (core != place[2], send)):

            @pl.when(side)
            def _():
                out[place[1] ^ x, slot, :, :1024] = rows.astype(BF)
                out[place[1] ^ x, slot, :, 1024:] = extra.astype(BF)


def mlp_body(
    place, normed, d_act, up_w, vecs, middle, cot, proj_w, down_bias, att,
    active, d_mid, d_att, proj_send, proj_keep, acc, vectors,
):
    step = pl.program_id(0)
    hidden = mm(normed[...], up_w[...]) + vecs[pl.ds(8 + step, 1), :]
    act, slope = gelu_both(hidden)
    active[...] = act.astype(BF)
    d_hidden = (d_act[...] * slope).astype(BF)
    vectors[pl.ds(4 + step, 1), :] = jnp.sum(d_hidden.astype(F32), 0, keepdims=True)
    part = times_transposed(d_hidden, up_w[...])

    @pl.when(step == 0)
    def _():
        acc[...] = part

    @pl.when(step > 0)
    def _():
        acc[...] += part

    @pl.when(step == pl.num_programs(0) - 1)
    def _():
        up = acc[...]
        hat, inv = standardize(middle[...])
        e = up * vecs[3:4, :]
        inner = e - jnp.mean(e, -1, keepdims=True) - hat * jnp.mean(e * hat, -1, keepdims=True)
        d_m = cot[...].astype(F32) + inv * inner
        d_mid[...] = d_m
        d_b = d_m.astype(BF)
        vectors[0:1, :] = jnp.sum(up * hat, 0, keepdims=True)
        vectors[1:2, :] = jnp.sum(up, 0, keepdims=True)
        vectors[2:3, :] = jnp.sum(d_b.astype(F32), 0, keepdims=True)
        vectors[3:4, :] = down_bias[...]
        d_a = times_transposed(d_b, proj_w[...]).astype(BF)
        for k in range(8):
            d_att[k] = d_a[:, 128 * k : 128 * k + 128]
        proj_grad(place, att[...], d_b, vectors, proj_send, proj_keep)


def mlp_grad_body(place, *refs):
    blocks, cots, ups, downs = refs[:8], refs[8:16], refs[16:20], refs[20:24]
    vecs, down_keep, down_send, up_keep, up_send, n_all, c_all, u_all, d_all, grad = refs[24:]
    for j in range(8):
        n_all[128 * j : 128 * j + 128, :] = blocks[j][...]
        c_all[128 * j : 128 * j + 128, :] = cots[j][...]
    lanes = pl.ds(pl.multiple_of(place[0] * 128, 128), 128)
    up_b = []
    rows = vecs[8:12, lanes]
    biases = lax.broadcasted_iota(jnp.int32, (4, 128), 0)
    for g in range(4):
        u_all[:, 128 * g : 128 * g + 128] = ups[g][...]
        d_all[128 * g : 128 * g + 128, :] = downs[g][...]
        group = (place[1] ^ (g & 1)) * 2 + (place[2] ^ (g >> 1))
        up_b.append(jnp.sum(jnp.where(biases == group, rows, 0.0), 0, keepdims=True))
    n = n_all[...]
    c = c_all[...]
    act, slope = gelu_both(mm(n, u_all[...]) + jnp.concatenate(up_b, 1))
    grad_down = outer_sum(act.astype(BF), c)
    for g in range(4):
        rows = grad_down[128 * g : 128 * g + 128]
        if g < 2:
            down_keep[g] = rows.astype(BF)
        else:
            down_send[g - 2] = rows.astype(BF)
    d_hidden = (times_transposed(c, d_all[...]) * slope).astype(BF)
    both = outer_sum(n, d_hidden)
    for g in range(4):
        group = ((place[1] ^ (g & 1)) * 2) + (place[2] ^ (g >> 1))
        lanes = pl.ds(pl.multiple_of(group * 128, 128), 128)
        grad[:, lanes] = both[:, 128 * g : 128 * g + 128]
    for rx in range(2):
        first = (place[1] ^ rx) * 512
        keep = pl.multiple_of(first + place[2] * 256, 256)
        send = pl.multiple_of(first + (1 - place[2]) * 256, 256)
        up_keep[rx] = grad[pl.ds(keep, 256), :].astype(BF)
        up_send[rx] = grad[pl.ds(send, 256), :].astype(BF)


def attend_back_body(
    place, probs, d_att, att_f, row_scale, q, k_all, v_all, cos, sin, d_all, bias_part, dq, dk, dv
):
    step = pl.program_id(0)
    keys = k_all[...]
    values = v_all[...]
    queries = q[...]
    d_out = jnp.concatenate([d_att[place[0] ^ (4 * step + m)] for m in range(4)], 0)
    scaled = d_out.astype(F32) * row_scale[...]
    d_out = scaled.astype(BF)
    products = (d_out.astype(F32) * att_f[...]).T
    key_parts, value_parts, query_parts = [], [], []
    for head in range(2):
        weights = probs[head]
        mine = jnp.where(head_mask(d_out.shape, head), d_out, jnp.zeros_like(d_out))
        delta = jnp.sum(products[64 * head : 64 * head + 64], 0, keepdims=True)
        d_weights = times_transposed(values, mine)
        d_scores = (weights.astype(F32) * (d_weights - delta)).astype(BF)
        key_parts.append(mm(d_scores, queries))
        value_parts.append(mm(weights, d_out))
        query_parts.append(outer_sum(keys, d_scores)[64 * head : 64 * head + 64])
    first = head_mask((1024, 128), 0)
    dk_new = jnp.where(first, key_parts[0], key_parts[1])
    dv_new = jnp.where(first, value_parts[0], value_parts[1])
    dq[pl.ds(pl.multiple_of(step * 512, 512), 512), :] = jnp.concatenate(query_parts, 0).T

    @pl.when(step == 0)
    def _():
        dk[...] = dk_new
        dv[...] = dv_new

    @pl.when(step > 0)
    def _():
        dk[...] += dk_new
        dv[...] += dv_new

    @pl.when(step == pl.num_programs(0) - 1)
    def _():
        total = jnp.zeros((1, 384), F32)
        for j in range(8):
            rows = slice(128 * j, 128 * j + 128)
            c = cos[rows, :]
            sn = sin[rows, :]
            back_q = 0.125 * dq[rows, :]
            back_k = dk[rows, :]
            piece = jnp.concatenate(
                [
                    back_q * c - swap_halves(back_q) * sn,
                    back_k * c - swap_halves(back_k) * sn,
                    dv[rows, :],
                ],
                1,
            ).astype(BF)
            d_all[place[0] ^ j] = piece
            total = total + jnp.sum(piece.astype(F32), 0, keepdims=True)
        bias_part[...] = total


def rel_block(step, place):
    rel = jnp.where(step < 2, 2, 0) + step % 2
    return ((rel & 1) ^ place[1]) * 2 + ((rel >> 1) ^ place[2])


def qkv_grad_body(place, h0, h1, d_all, bias_part, vecs, wq, wk, wv, send, keep):
    step = pl.program_id(0)
    d_near = jnp.concatenate([d_all[place[0] ^ j] for j in range(4)], 0)
    d_far = jnp.concatenate([d_all[place[0] ^ j] for j in range(4, 8)], 0)
    inner = outer_sum(h0[...], d_near) + outer_sum(h1[...], d_far)
    total = bias_part[...]
    w = jnp.concatenate([wq[...], wk[...], wv[...]], 1).astype(F32)
    columns = vecs[...].T
    gain = columns[:, 0:1]
    shift = columns[:, 1:2]
    grad = gain * inner + shift * total
    row = lax.broadcasted_iota(jnp.int32, (256, 128), 0) % 32
    lane = lax.broadcasted_iota(jnp.int32, (256, 128), 1)
    extra = jnp.where(
        lane == 0,
        jnp.sum(w * inner, 1, keepdims=True),
        jnp.where(lane == 1, jnp.sum(w * total, 1, keepdims=True), 0.0),
    )
    for m in range(6):
        part = total[:, 128 * (m // 2) : 128 * (m // 2) + 128]
        part = part if m % 2 else pltpu.roll(part, 64, 1)
        extra = jnp.where((row == m) & (lane >= 64), part, extra)

    @pl.when(step < 2)
    def _():
        send[0, :, :384] = grad.astype(BF)
        send[0, :, 384:] = extra.astype(BF)

    @pl.when(step >= 2)
    def _():
        keep[0, :, :384] = grad.astype(BF)
        keep[0, :, 384:] = extra.astype(BF)


def pair_body(place, keep, came, left, send):
    half = left.shape[0]
    total = (keep[...].astype(F32) + came[...].astype(F32)).astype(BF)
    left[...] = total[:half]
    send[...] = total[half:]


def low_body(place, up_left, up_came, qkv_left, qkv_came, out):
    out[:, :32] = (up_left[...].astype(F32) + up_came[...].astype(F32)).astype(BF)
    out[:, 32:] = (qkv_left[...].astype(F32) + qkv_came[...].astype(F32)).astype(BF)


def merge_body(place, *refs):
    up, up_came, down, down_came, proj_left, proj_came = refs[:6]
    left, send, down_left, down_send, proj_keep, proj_send = refs[6:]
    proj_keep[...] = (proj_left[:2].astype(F32) + proj_came[:2].astype(F32)).astype(BF)
    proj_send[...] = (proj_left[2:].astype(F32) + proj_came[2:].astype(F32)).astype(BF)
    for side, low, low_down in ((0, left, down_left), (1, send, down_send)):
        total = (up[side].astype(F32) + up_came[side].astype(F32)).astype(BF)
        for k in range(8):
            low[k] = total[32 * k : 32 * k + 32]
        low_down[...] = (down[side].astype(F32) + down_came[side].astype(F32)).astype(BF)


def finish_body(place, came, grad_up, grad_qkv, gain, shift, bias):
    total = jnp.zeros((32, 128), F32)
    low = lax.broadcasted_iota(jnp.int32, (1, 128), 1) < 64
    parts = ([], [], [])
    for k in range(8):
        for g in range(4):
            lanes = slice(1024 * g + 128 * k, 1024 * g + 128 * k + 128)
            grad_up[:, lanes] = came[k, :32, 128 * g : 128 * g + 128].astype(F32)
            if g < 3:
                grad_qkv[:, lanes] = came[k, 32:, 128 * g : 128 * g + 128].astype(F32)
        extra = came[k, 32:, 384:].astype(F32)
        total = total + extra
        for p in range(3):
            left = pltpu.roll(extra[2 * p : 2 * p + 1], 64, 1)
            both = jnp.where(low, left, extra[2 * p + 1 : 2 * p + 2])
            parts[p].append(both)
    turned = total.T
    gain[...] = turned[0:1]
    shift[...] = turned[1:2]
    row = jnp.broadcast_to(jnp.concatenate(parts[0] + parts[1] + parts[2], 1), (8, 3072))
    me = place[1] * 16 + place[2] * 8 + place[0]
    bias[...] = pltpu.roll(row, lax.rem(3072 - me * 96, 3072), 1)[0:1, :96]


def out_body(place, active, down, middle, vecs, out, acc):
    step = pl.program_id(0)
    part = mm(active[...], down[...])

    @pl.when(step == 0)
    def _():
        acc[...] = part + middle[...] + vecs[5:6, :]

    @pl.when(step > 0)
    def _():
        acc[...] += part

    @pl.when(step == pl.num_programs(0) - 1)
    def _():
        out[...] = acc[...].astype(BF)


def last_body(place, came, w, tok, d_mid, vecs, out, acc):
    step = pl.program_id(0)
    for p in range(3):

        @pl.when(step == p)
        def _():
            d_mixed = jnp.concatenate([came[k, :, 128 * p : 128 * p + 128] for k in range(8)], 1)
            part = times_transposed(d_mixed, w[...])
            if p == 0:
                acc[...] = part
            elif p == 1:
                acc[...] += part
            else:
                up = acc[...] + part
                hat, inv = standardize(tok[...].astype(F32))
                e = up * vecs[0:1, :]
                mean = jnp.mean(e, -1, keepdims=True)
                inner = e - mean - hat * jnp.mean(e * hat, -1, keepdims=True)
                out[...] = d_mid[...] + inv * inner


def frequency_rows():
    rows = np.zeros((8, 128), np.float32)
    for lane in range(128):
        pair = lane % 32
        part, rank, count = (0, pair, 10) if pair < 10 else ((1, pair - 10, 11) if pair < 21 else (2, pair - 21, 11))
        rows[part, lane] = 10000.0 ** (-rank / count)
        rows[3, lane] = -1.0 if lane % 64 < 32 else 1.0
    return rows


def clip_starts(place, pos):
    ids = jnp.zeros_like(pos)
    start = jnp.zeros_like(pos)
    end = jnp.int32(0)
    for c in range(8):
        length = place[8 + c]
        end = end + length
        past = pos >= end.astype(F32)
        ids = jnp.where(past, ids + 1.0, ids)
        start = jnp.where(past, end.astype(F32), start)
    return ids, start


def prep_body(place, freq, cos, sin, id_col, id_row):
    for j in range(8):
        first = ((place[0] ^ j) * 128).astype(F32)
        rows = slice(128 * j, 128 * j + 128)
        pos = first + lax.broadcasted_iota(jnp.int32, (128, 128), 0).astype(F32)
        ids, start = clip_starts(place, pos)
        id_col[rows, :] = ids
        within = pos - start
        row14 = jnp.floor((within + 0.5) * (1.0 / 14.0))
        t = jnp.floor((within + 0.5) * (1.0 / 196.0))
        angle = t * freq[0:1, :] + (row14 - 14.0 * t) * freq[1:2, :] + (within - 14.0 * row14) * freq[2:3, :]
        cos[rows, :] = jnp.cos(angle)
        sin[rows, :] = jnp.sin(angle) * freq[3:4, :]
        flat = first + lax.broadcasted_iota(jnp.int32, (8, 128), 1).astype(F32)
        id_row[:, 128 * j : 128 * j + 128] = clip_starts(place, flat)[0]


def after(value, *others):
    return lax.optimization_barrier((value, *others))[0]


def spread_four(a):
    return [a, swap_over(a, "y"), swap_over(a, "zl"), swap_over(a, "zl", "y")]


def fast_shards(
    tokens_in, clip_lengths, attn_gain, attn_shift, qkv_weight, qkv_bias, proj_weight, proj_bias,
    mlp_gain, mlp_shift, up_weight, up_bias, down_weight, down_bias, out_cotangent,
):
    x, core, zh, zl, y = (lax.axis_index(name) for name in AXES)
    k = zh * 4 + zl * 2 + y
    me = x * 16 + core * 8 + k
    place = jnp.concatenate(
        [jnp.stack([k, x, core, k, k, k, k, k]).astype(jnp.int32), clip_lengths[0]]
    )
    tok = tokens_in[0]
    cot = out_cotangent[0]

    far_tok = swap_over(tok, "zh")
    near = spread_four(tok)
    rows = [attn_gain, attn_shift, proj_bias, mlp_gain, mlp_shift, down_bias, down_bias, down_bias]
    vecs = jnp.concatenate([v.astype(F32).reshape(-1, 1024) for v in (*rows, up_bias, qkv_bias)], 0)
    cos_tab, sin_tab, id_col, id_row = one_step(
        prep_body,
        [arr((1024, 128), F32), arr((1024, 128), F32), arr((1024, 128), F32), arr((8, 1024), F32)],
        [],
        PIN,
        place,
        (jnp.asarray(frequency_rows()),),
    )
    far_tok, cos_tab, vecs, *near = lax.optimization_barrier((far_tok, cos_tab, vecs, *near))
    far = spread_four(far_tok)

    def table_half(part):
        return pl.BlockSpec((512, 128), lambda i, s: (part, 0))

    half = arr((512, 128), BF)
    full = arr((1024, 128), BF)
    common = (vecs, qkv_weight, qkv_weight, qkv_weight, cos_tab, sin_tab)
    columns_of = [pl.BlockSpec((1024, 128), lambda i, s, p=p: (0, 8 * p + s[0])) for p in range(3)]

    def qkv(body, part, blocks, more, outs):
        specs = [whole(v.shape) for v in (*blocks, vecs)] + columns_of
        specs += [table_half(part), table_half(part)] + [whole(v.shape) for v in more]
        return call(
            body, (1,), specs, [whole(o.shape) for o in outs], outs,
            [pltpu.VMEM((512, 1024), BF)], PIN, place, (*blocks, *common, *more),
        )

    hat0, q0, k0, v0 = qkv(near_body, 0, near, (), [arr((512, 1024), BF), half, half, half])
    d_act, down_bias_part = call(
        down_back_body,
        (4,),
        [whole((128, 1024)), pl.BlockSpec((1024, 1024), lambda i, s: (i, 0))],
        [pl.BlockSpec((128, 1024), lambda i, s: (0, i)), whole((1, 1024))],
        [arr((128, 4096), F32), arr((1, 1024), F32)],
        [],
        PIN,
        place,
        (after(cot, q0), down_weight),
    )
    far = lax.optimization_barrier((q0, d_act, *far))[2:]
    cot_here = after(cot, q0)
    far_cot = swap_over(cot_here, "zh")
    cots = spread_four(cot_here)
    hat1, q_all, k_all, v_all = qkv(
        far_body, 1, far, (q0, k0, v0), [arr((512, 1024), BF), full, full, full]
    )
    step_rows = pl.BlockSpec((256, 128), lambda i, s: (i, 0))
    flat = whole((1024, 128))
    two_rows = pl.BlockSpec((512, 128), lambda i, s: (i, 0))
    att_f, att_low, probs, row_scale = call(
        attend_body,
        (2,),
        [
            two_rows, flat, flat, flat, pl.BlockSpec((8, 512), lambda i, s: (0, i)),
        ],
        [two_rows, whole((8, 128, 128)), pl.BlockSpec((2, 1024, 512), lambda i, s: (0, 0, i)),
         two_rows],
        [arr((1024, 128), F32), arr((8, 128, 128), BF), arr((2, 1024, 1024), BF),
         arr((1024, 128), F32)],
        [],
        PIN,
        place,
        (q_all, k_all, v_all, id_col, id_row),
    )
    att_low, far_cot, *cots = lax.optimization_barrier((att_low, far_cot, *cots))
    att_in = lax.all_to_all(att_low, ROW, 0, 0, tiled=True)
    cots += [far_cot, swap_over(far_cot, "y"), swap_over(far_cot, "zl")]
    middle, normed2, att_rows = one_step(
        proj_body,
        [arr((128, 1024), F32), arr((128, 1024), BF), arr((128, 1024), BF)],
        [],
        PIN,
        place,
        (att_in, tok, proj_weight, vecs),
        LOW_PIN,
    )
    normed2, *cots = lax.optimization_barrier((normed2, *cots))
    far_n = swap_over(normed2, "zh")
    near_n = spread_four(normed2)
    wide = pl.BlockSpec((128, 1024), lambda i, s: (0, i))
    fixed = whole((128, 1024))
    active, d_mid, d_att, proj_send, proj_keep = call(
        mlp_body,
        (4,),
        [
            fixed, wide, wide_columns(), whole((15, 1024)), fixed, fixed, whole((1024, 1024)),
            whole((1, 1024)), fixed,
        ],
        [wide, fixed, whole((8, 128, 128)), whole((2, 8, 32, 1152)), whole((2, 8, 32, 1152))],
        [
            arr((128, 4096), BF), arr((128, 1024), F32), arr((8, 128, 128), BF),
            arr((2, 8, 32, 1152), BF), arr((2, 8, 32, 1152), BF),
        ],
        [pltpu.VMEM((128, 1024), F32), pltpu.VMEM((8, 1024), F32)],
        LOW_PIN,
        place,
        (normed2, d_act, up_weight, vecs, middle, cot, proj_weight, down_bias_part, att_rows),
    )
    d_att, far_n, far_y, active, proj_send, *near_n = lax.optimization_barrier(
        (d_att, far_n, cots[5], active, proj_send, *near_n)
    )
    last_cot = swap_over(far_y, "zl")
    d_att_in = lax.all_to_all(d_att, ROW, 0, 0, tiled=True)

    far_n = spread_four(far_n)

    def pair(keep, came):
        half = arr((keep.shape[0] // 2, *keep.shape[1:]), BF)
        return one_step(pair_body, [half, half], [], NO_PIN, place, (keep, came))

    flat_proj = (16, 32, 1152)
    proj_left, proj_low = pair(
        proj_keep.reshape(flat_proj), swap_over(proj_send.reshape(flat_proj), "core")
    )

    d_all, qkv_bias_part = call(
        attend_back_body,
        (2,),
        [
            pl.BlockSpec((2, 1024, 512), lambda i, s: (0, 0, i)), whole((8, 128, 128)), two_rows,
            two_rows, two_rows, flat, flat, flat, flat,
        ],
        [whole((8, 128, 384)), whole((1, 384))],
        [arr((8, 128, 384), BF), arr((1, 384), F32)],
        [pltpu.VMEM((1024, 128), F32)] * 3,
        PIN,
        place,
        (probs, after(d_att_in, proj_low), att_f, row_scale, q_all, k_all, v_all, cos_tab, sin_tab),
    )
    block_of = lambda i, s: (rel_block(i, s), 0)
    lanes_of = lambda i, s: (0, rel_block(i, s))
    send, keep = call(
        qkv_grad_body,
        (4,),
        [
            pl.BlockSpec((512, 256), lanes_of), pl.BlockSpec((512, 256), lanes_of),
            whole((8, 128, 384)), whole((1, 384)), pl.BlockSpec((8, 256), lanes_of),
        ]
        + [pl.BlockSpec((256, 128), lambda i, s, p=p: (rel_block(i, s), 8 * p + s[0])) for p in range(3)],
        [
            pl.BlockSpec((1, 256, 512), lambda i, s: (jnp.minimum(i, 1), 0, 0)),
            pl.BlockSpec((1, 256, 512), lambda i, s: (jnp.maximum(i - 2, 0), 0, 0)),
        ],
        [arr((2, 256, 512), BF), arr((2, 256, 512), BF)],
        [],
        PIN,
        place,
        (hat0, hat1, d_all, qkv_bias_part, vecs, qkv_weight, qkv_weight, qkv_weight),
    )
    def turn(value):
        return lax.all_to_all(value, ROW, 0, 0, tiled=True)
    d_all, send, last_cot, *far_n = lax.optimization_barrier((d_all, send, last_cot, *far_n))
    moved = lax.all_to_all(d_all, ROW, 0, 0, tiled=True)
    proj_left, proj_low = pair(after(proj_left, d_all), swap_over(proj_low, "x"))

    flat_qkv = (16, 32, 512)
    qkv_left, qkv_low = pair(
        keep.reshape(flat_qkv), swap_over(send.reshape(flat_qkv), "core")
    )
    qkv_came = swap_over(qkv_low, "x")

    def group_of(s, g):
        return (s[1] ^ (g & 1)) * 16 + (s[2] ^ (g >> 1)) * 8 + s[0]

    outs = [
        arr((2, 128, 1024), BF), arr((2, 128, 1024), BF), arr((2, 256, 512), BF),
        arr((2, 256, 512), BF),
    ]
    down_keep, down_send, up_keep, up_send = call(
        mlp_grad_body,
        (1,),
        [fixed] * 16
        + [pl.BlockSpec((1024, 128), lambda i, s, g=g: (0, group_of(s, g))) for g in range(4)]
        + [pl.BlockSpec((128, 1024), lambda i, s, g=g: (group_of(s, g), 0)) for g in range(4)]
        + [whole((15, 1024))],
        [whole(o.shape) for o in outs],
        outs,
        [
            pltpu.VMEM((1024, 1024), BF), pltpu.VMEM((1024, 1024), BF),
            pltpu.VMEM((1024, 512), BF), pltpu.VMEM((512, 1024), BF), pltpu.VMEM((1024, 512), F32),
        ],
        LOW_PIN,
        place,
        (after(near_n[0], d_all, proj_low, qkv_low), *near_n[1:], *far_n, *cots, last_cot, *([up_weight] * 4), *([down_weight] * 4), vecs),
    )


    up_send, down_send, proj_came, qkv_came = lax.optimization_barrier(
        (up_send, down_send, swap_over(proj_low, "y"), qkv_came)
    )
    left, low_send, down_left, down_low, proj_left, proj_low = one_step(
        merge_body,
        [arr((8, 32, 512), BF)] * 2 + [arr((128, 1024), BF)] * 2 + [arr((2, 32, 1152), BF)] * 2,
        [],
        PIN,
        place,
        (
            after(up_keep, moved), swap_over(up_send, "core"),
            down_keep, swap_over(down_send, "core"), proj_left, proj_came,
        ),
        NO_PIN,
    )
    low_came = swap_over(low_send, "x")
    (tokens_grad,) = call(
        last_body,
        (3,),
        [
            whole((8, 128, 384)), pl.BlockSpec((1024, 1024), lambda i, s: (0, i)), fixed, fixed,
            whole((15, 1024)),
        ],
        [fixed],
        [arr((128, 1024), F32)],
        [pltpu.VMEM((128, 1024), F32)],
        PIN,
        place,
        (after(moved, left), qkv_weight, tok, d_mid, vecs),
    )

    left, low_came, _ = lax.optimization_barrier((left, low_came, tokens_grad))
    (lows,) = one_step(
        low_body, [arr((8, 64, 512), BF)], [], NO_PIN, place, (left, low_came, qkv_left, qkv_came)
    )
    came = turn(lows)
    proj_left, proj_low = pair(after(proj_left, lows), swap_over(proj_low, "zh"))
    proj_came = swap_over(proj_low, "zl")
    down_low, _ = lax.optimization_barrier((down_low, lows))
    grad_down = down_left.astype(F32) + swap_over(down_low, "x").astype(F32)
    proj_total = proj_left[0].astype(F32) + proj_came[0].astype(F32)
    (layer_out,) = call(
        out_body,
        (4,),
        [wide, pl.BlockSpec((1024, 1024), lambda i, s: (i, 0)), fixed, whole((15, 1024))],
        [fixed],
        [arr((128, 1024), BF)],
        [pltpu.VMEM((128, 1024), F32)],
        PIN,
        place,
        (after(active, lows), down_weight, middle, vecs),
    )
    layer_out = layer_out[None]
    grad_proj = proj_total[:, :1024]
    own = lax.dynamic_slice(proj_total[:4, 1024:], (0, (me % 4) * 32), (4, 32))
    grad_up_b = proj_total[4, 1024:]

    grad_up, grad_qkv, gain_sum, shift_sum, grad_qkv_b = one_step(
        finish_body,
        [arr((32, 4096), F32), arr((32, 3072), F32), arr((1, 32), F32), arr((1, 32), F32), arr((1, 96), F32)],
        [],
        NO_PIN,
        place,
        (came,),
    )

    return (
        layer_out, tokens_grad[None], gain_sum[0], shift_sum[0], grad_qkv, grad_qkv_b[0], grad_proj,
        own[2], own[0], own[1], grad_up, grad_up_b, grad_down, own[3],
    )


def wide_columns():
    return pl.BlockSpec((1024, 1024), lambda i, s: (0, i))


def fast_solution(mesh):
    wide_mesh = Mesh(mesh.devices.reshape(2, 2, 2, 2, 2), AXES)
    batch, blk = AXES[:2], AXES[2:]
    spread = P(batch, blk, None)
    return jax.shard_map(
        fast_shards,
        mesh=wide_mesh,
        in_specs=(spread, P(batch, None)) + (P(),) * 12 + (spread,),
        out_specs=(spread, spread)
        + tuple(P(AXES, None) if i in (2, 4, 8, 10) else P(AXES) for i in range(12)),
        check_vma=False,
    )


def solution(mesh):
    if tuple(mesh.devices.shape) == (4, 8):
        return fast_solution(mesh)
    placed = (
        P("batch", "blk", None),
        P("batch", None),
        P(),
        P(),
        P(),
        P(),
        P(),
        P(),
        P(),
        P(),
        P(),
        P(),
        P(),
        P(),
        P("batch", "blk", None),
    )
    return jax.shard_map(
        shards,
        mesh=mesh,
        in_specs=placed,
        out_specs=(
            P("batch", "blk", None),
            P("batch", "blk", None),
            P(("batch", "blk")),
            P(("batch", "blk")),
            P(("batch", "blk"), None),
            P(("batch", "blk")),
            P(("batch", "blk"), None),
            P(("batch", "blk")),
            P(("batch", "blk")),
            P(("batch", "blk")),
            P(("batch", "blk"), None),
            P(("batch", "blk")),
            P(("batch", "blk"), None),
            P(("batch", "blk")),
        ),
        check_vma=False,
    )
```
